128 devices in a mesh: dp: 16 (over z_lo, x, core), seq: 8 (over y, z_hi).
Axes of the slice: x: 4, y: 4, z: 4 (z_hi: 2, z_lo: 2; z = z_hi * 2 + z_lo), core: 2. Of those that a mesh axis runs over, the one named last changes fastest.
Arguments:
- enc_states: bfloat16 [16, 256, 4096], P('dp'), may hold values from -6 to 6
- lengths: int32 [16], replicated, may hold values from 1 to 128, as said below
- prompt_owner_sample: int32 [16], replicated, may hold values from 0 to 15, each once
- t5_gain: float32 [4096], replicated, may hold values from 0.5 to 1.5
- t5_in_weight: bfloat16 [2, 4096, 5120], P(None, None, 'seq'), may hold values from -0.09375 to 0.09375
- t5_out_weight: bfloat16 [5120, 4096], P('seq'), may hold values from -0.078125 to 0.078125
- t5_final_gain: float32 [4096], replicated, may hold values from 0.5 to 1.5
- context_weight: bfloat16 [4096, 3072], P('seq', 'dp'), may hold values from -0.09375 to 0.09375
- text_shift: float32 [16, 3072], P('dp'), may hold values from -3 to 3
- text_scale: float32 [16, 3072], P('dp'), may hold values from -0.5 to 0.5
- kv_weight: bfloat16 [3072, 2, 3072], P('dp', None, 'seq'), may hold values from -0.109375 to 0.109375
- text_key_gain: float32 [128], replicated, may hold values from 0.25 to 1.75
- image_query_key_value: bfloat16 [16, 1024, 3, 3072], P('dp', 'seq'), may hold values from -6 to 6
- image_qk_gain: float32 [2, 128], replicated, may hold values from 0.25 to 1.75
- proj_weight: bfloat16 [3072, 3072], P('seq', 'dp'), may hold values from -0.109375 to 0.109375
- dora_a: float32 [3072, 64], P('seq'), may hold values from -0.109375 to 0.109375
- dora_b: float32 [64, 3072], P(None, 'dp'), may hold values from -0.375 to 0.375
- magnitude: float32 [3072], P('dp'), may hold values from 0.5 to 2
- grad_out: bfloat16 [16, 1024, 3072], P('dp', 'seq'), may hold values from -6 to 6
Outputs:
- image_out: bfloat16 [16, 1024, 3072], P('dp', 'seq')
- grad_a: float32 [3072, 64], P('seq')
- grad_b: float32 [64, 3072], P(None, 'dp')
- grad_magnitude: float32 [3072], P('dp')
The draws below stay inside these ranges and needn't reach their ends.
Inputs may be any that keep to these rules, and one draw needn't show every extreme that they name: `lengths`: prompt token counts; in every draw one prompt has exactly 128 tokens. `prompt_owner_sample`: each DiT sample index appears exactly once.
All inputs are finite; a program needn't handle non-finite values.
Results may differ from the reference program's by a relative error of at most 0.024.
Values may be sent and summed in bfloat16 or wider, within the bound.
No kernel may reach another device: no remote copies, remote signals or barrier semaphores. Data moves between devices by JAX's collectives and lax.ppermute only.
A program may use at most 128 MiB of HBM per device.

```python
import math
import jax
import jax.numpy as jnp
from jax import lax

D5 = 4096
F5 = 5120
D = 3072
HEADS = 24
HD = 128
RANK = 64
LTXT = 256
BLK = 128
IMG = 1024
SAMPLES = 16
N_SEQ = 8


def draw_lengths(key, part):
    length_key, pick_key = jax.random.split(key)
    drawn_lengths = jax.random.randint(length_key, (SAMPLES,), 1, BLK + 1, dtype=jnp.int32)
    longest = jax.random.randint(pick_key, (), 0, SAMPLES, dtype=jnp.int32)
    return jnp.where(jnp.arange(SAMPLES, dtype=jnp.int32) == longest, BLK, drawn_lengths).astype(jnp.int32)


def shard_levels(key, extent, pieces, low, top_value):
    def one(axis_at, shards_of):
        steps = jax.random.uniform(jax.random.fold_in(jax.random.fold_in(key, 6), axis_at), (shards_of,), jnp.float32, low / len(pieces), top_value / len(pieces))
        return jnp.repeat(jnp.exp(steps), extent[axis_at] // shards_of).reshape((-1,) + (1,) * (len(extent) - axis_at - 1))

    factor_of = one(*pieces[0])
    for cut in pieces[1:]:
        factor_of = factor_of * one(*cut)
    return factor_of


def noise(own_key, shape, scale, reach, shards=(), kind=jnp.bfloat16):
    values = jax.random.normal(own_key, shape, jnp.float32) * scale
    if len(shards) > 0:
        values = shard_levels(own_key, shape, shards, -0.22, 0.18) * values
    return jnp.clip(values, min=-reach, max=reach).astype(kind)


def setup_inputs(seed: int = 0) -> dict:
    keys = jax.random.split(jax.random.key(seed), 20)
    enc_states = noise(keys[0], (SAMPLES, LTXT, D5), 1.0, 6.0, ((0, 16),))
    lengths = draw_lengths(jax.random.fold_in(keys[19], 71), 0)
    prompt_owner_sample = jax.random.permutation(keys[2], SAMPLES).astype(jnp.int32)
    t5_gain = jnp.clip(1.0 + 0.1 * jax.random.normal(keys[3], (D5,), jnp.float32), 0.5, 1.5)
    t5_in_weight = noise(keys[4], (2, D5, F5), D5 ** -0.5, 0.09375, ((2, 8),))
    t5_out_weight = noise(keys[5], (F5, D5), F5 ** -0.5, 0.078125, ((0, 8),))
    t5_final_gain = jnp.clip(1.0 + 0.1 * jax.random.normal(keys[6], (D5,), jnp.float32), 0.5, 1.5)
    context_weight = noise(keys[7], (D5, D), D5 ** -0.5, 0.09375, ((0, 8), (1, 16)))
    text_shift = noise(keys[8], (SAMPLES, D), 0.5, 3.0, ((0, 16),), jnp.float32)
    text_scale = jnp.clip(jax.random.uniform(keys[9], (SAMPLES, D), jnp.float32, -0.5, 0.5) * shard_levels(keys[9], (SAMPLES, D), ((0, 16),), -0.4, 0.0), -0.5, 0.5)
    kv_weight = noise(keys[10], (D, 2, D), D ** -0.5, 0.109375, ((0, 16), (2, 8)))
    text_key_gain = jnp.clip(1.0 + 0.15 * jax.random.normal(keys[11], (HD,), jnp.float32), 0.25, 1.75)
    image_query_key_value = noise(keys[12], (SAMPLES, IMG, 3, D), 1.0, 6.0, ((0, 16), (1, 8)))
    image_qk_gain = jnp.clip(1.0 + 0.15 * jax.random.normal(keys[13], (2, HD), jnp.float32), 0.25, 1.75)
    proj_weight = noise(keys[14], (D, D), D ** -0.5, 0.109375, ((0, 8), (1, 16)))
    dora_a = noise(keys[15], (D, RANK), D ** -0.5, 0.109375, ((0, 8),), jnp.float32)
    dora_b = noise(keys[16], (RANK, D), (4 * RANK) ** -0.5, 0.375, ((1, 16),), jnp.float32)
    magnitude = jnp.clip(jnp.exp(math.log(2.0) - 1.3862944 * jax.random.uniform(keys[17], (D,), jnp.float32) ** shard_levels(keys[17], (D,), ((0, 16),), -0.2, 0.2)), 0.5, 2.0)
    grad_out = noise(keys[18], (SAMPLES, IMG, D), 1.0, 6.0, ((0, 16), (1, 8)))
    return {"enc_states": enc_states, "lengths": lengths, "prompt_owner_sample": prompt_owner_sample, "t5_gain": t5_gain, "t5_in_weight": t5_in_weight, "t5_out_weight": t5_out_weight, "t5_final_gain": t5_final_gain, "context_weight": context_weight, "text_shift": text_shift, "text_scale": text_scale, "kv_weight": kv_weight, "text_key_gain": text_key_gain, "image_query_key_value": image_query_key_value, "image_qk_gain": image_qk_gain, "proj_weight": proj_weight, "dora_a": dora_a, "dora_b": dora_b, "magnitude": magnitude, "grad_out": grad_out}


EPSILON = 1e-06

def rms_scale(values, gain):
    return values * lax.rsqrt(lax.optimization_barrier(jnp.mean(values * values, -1, keepdims=True)) + EPSILON) * gain

def reference(enc_states, lengths, prompt_owner_sample, t5_gain, t5_in_weight, t5_out_weight, t5_final_gain, context_weight, text_shift, text_scale, kv_weight, text_key_gain, image_query_key_value, image_qk_gain, proj_weight, dora_a, dora_b, magnitude, grad_out):
    flat_tokens = enc_states.reshape(SAMPLES * LTXT, D5).astype(jnp.float32)
    normed = rms_scale(flat_tokens, t5_gain).astype(jnp.bfloat16)
    gate_proj = jnp.dot(normed, t5_in_weight[0], preferred_element_type=jnp.float32)
    upward = jnp.dot(normed, t5_in_weight[1], preferred_element_type=jnp.float32)
    hidden = (jax.nn.gelu(gate_proj, approximate=True) * upward).astype(jnp.bfloat16)
    hidden_slice = F5 // N_SEQ
    ffn_sum = jnp.zeros((SAMPLES * LTXT, D5), jnp.float32)
    for shard_index in range(N_SEQ):
        partial_value = jnp.dot(hidden[:, shard_index * hidden_slice:(shard_index + 1) * hidden_slice], t5_out_weight[shard_index * hidden_slice:(shard_index + 1) * hidden_slice], preferred_element_type=jnp.float32)
        ffn_sum = ffn_sum + lax.optimization_barrier(partial_value.astype(jnp.bfloat16)).astype(jnp.float32)
    encoded = ((flat_tokens + ffn_sum) * t5_final_gain).astype(jnp.bfloat16)
    feature_slice = D5 // N_SEQ
    context_sum = jnp.zeros((SAMPLES * LTXT, D), jnp.float32)
    for shard_index in range(N_SEQ):
        partial_value = jnp.dot(encoded[:, shard_index * feature_slice:(shard_index + 1) * feature_slice], context_weight[shard_index * feature_slice:(shard_index + 1) * feature_slice], preferred_element_type=jnp.float32)
        context_sum = context_sum + lax.optimization_barrier(partial_value.astype(jnp.bfloat16)).astype(jnp.float32)
    text_embed = context_sum.astype(jnp.bfloat16).reshape(SAMPLES, LTXT, D)
    routed = jnp.zeros_like(text_embed).at[prompt_owner_sample].set(text_embed)
    diffusion_lengths = jnp.zeros_like(lengths).at[prompt_owner_sample].set(lengths)
    routed_values = routed.astype(jnp.float32)
    centre = lax.optimization_barrier(jnp.mean(routed_values, -1, keepdims=True))
    spread = lax.optimization_barrier(jnp.mean((routed_values - centre) * (routed_values - centre), -1, keepdims=True))
    layer_normed = (routed_values - centre) * lax.rsqrt(spread + EPSILON)
    modulated = ((1.0 + text_scale[:, None, :]) * layer_normed + text_shift[:, None, :]).astype(jnp.bfloat16)
    key_value = jnp.dot(modulated.reshape(SAMPLES * LTXT, D), kv_weight.reshape(D, 2 * D), preferred_element_type=jnp.float32).reshape(SAMPLES, LTXT, 2, HEADS, HD)
    prompt_key_rows = rms_scale(key_value[:, :, 0], text_key_gain).astype(jnp.bfloat16)
    prompt_value_rows = key_value[:, :, 1].astype(jnp.bfloat16)
    score_scale = 1.0 / math.sqrt(HD)

    def sample_attention(inputs):
        qkv_rows, keys_text, values_text, prompt_length = inputs
        split_heads = qkv_rows.reshape(IMG, 3, HEADS, HD)
        queries = rms_scale(split_heads[:, 0].astype(jnp.float32), image_qk_gain[0]).astype(jnp.bfloat16)
        key_image = rms_scale(split_heads[:, 1].astype(jnp.float32), image_qk_gain[1]).astype(jnp.bfloat16)
        value_image = split_heads[:, 2]
        key_valid_mask = jnp.arange(LTXT, dtype=jnp.int32) < prompt_length
        text_scores = jnp.einsum('qhd,khd->hqk', queries.astype(jnp.float32), keys_text.astype(jnp.float32)) * score_scale
        text_weight = jnp.where(key_valid_mask[None, None, :], jnp.exp(text_scores), 0.0)
        image_scores = jnp.einsum('qhd,khd->hqk', queries.astype(jnp.float32), key_image.astype(jnp.float32)) * score_scale
        image_weight = jnp.exp(image_scores)
        denominator = lax.optimization_barrier(jnp.sum(text_weight, -1)) + lax.optimization_barrier(jnp.sum(image_weight, -1))
        text_probs = (text_weight / denominator[..., None]).astype(jnp.bfloat16)
        image_probs = (image_weight / denominator[..., None]).astype(jnp.bfloat16)
        mixture = jnp.einsum('hqk,khd->qhd', text_probs.astype(jnp.float32), values_text.astype(jnp.float32))
        mixture = mixture + jnp.einsum('hqk,khd->qhd', image_probs.astype(jnp.float32), value_image.astype(jnp.float32))
        return mixture.astype(jnp.bfloat16).reshape(IMG, D)
    attended_rows = lax.map(sample_attention, (image_query_key_value, prompt_key_rows, prompt_value_rows, diffusion_lengths))
    flat_attended = attended_rows.reshape(SAMPLES * IMG, D)
    direction = proj_weight.astype(jnp.float32) + jnp.dot(dora_a, dora_b, precision=lax.Precision.HIGHEST)
    column_norm = jnp.sqrt(lax.optimization_barrier(jnp.sum(direction * direction, 0)) + EPSILON)
    column_ratio = magnitude / column_norm
    scaled = (direction * column_ratio).astype(jnp.bfloat16)
    head_width = D // N_SEQ
    out_sum = jnp.zeros((SAMPLES * IMG, D), jnp.float32)
    for shard_index in range(N_SEQ):
        partial_value = jnp.dot(flat_attended[:, shard_index * head_width:(shard_index + 1) * head_width], scaled[shard_index * head_width:(shard_index + 1) * head_width], preferred_element_type=jnp.float32)
        out_sum = out_sum + lax.optimization_barrier(partial_value.astype(jnp.bfloat16)).astype(jnp.float32)
    image_out = out_sum.astype(jnp.bfloat16).reshape(SAMPLES, IMG, D)
    weight_grad = jnp.dot(flat_attended.T, grad_out.reshape(SAMPLES * IMG, D), preferred_element_type=jnp.float32)
    grad_magnitude = lax.optimization_barrier(jnp.sum(weight_grad * direction, 0)) / column_norm
    scaled_grad = weight_grad * column_ratio
    grad_a = jnp.dot(scaled_grad, dora_b.T, precision=lax.Precision.HIGHEST)
    grad_b = jnp.dot(dora_a.T, scaled_grad, precision=lax.Precision.HIGHEST)
    return (image_out, grad_a, grad_b, grad_magnitude)
```

```python
import math

import jax
import jax.numpy as jnp
from jax import lax
from jax.experimental import pallas as pl
from jax.experimental.pallas import tpu as pltpu
from jax.sharding import PartitionSpec as P

HD = 128
BLK = 128
EPSILON = 1e-06
F32 = jnp.float32
BF16 = jnp.bfloat16
Y_GROUPS = [[0, 2, 4, 6], [1, 3, 5, 7]]
Z_GROUPS = [[0, 1], [2, 3], [4, 5], [6, 7]]


def rms_scale(values, gain):
    return values * lax.rsqrt(jnp.mean(values * values, -1, keepdims=True) + EPSILON) * gain


def swap(values, axes, groups=None):
    return lax.all_to_all(values, axes, 0, 0, tiled=True, axis_index_groups=groups)


def dot_t(left, right):
    return lax.dot_general(left, right, (((1,), (1,)), ((), ())), preferred_element_type=F32)


def image_kernel(q_ref, k_ref, v_ref, gain_ref, num_ref, den_ref, keys, values):
    @pl.when(pl.program_id(1) == 0)
    def _():
        k = k_ref[...].reshape(-1, HD).astype(F32)
        keys[...] = rms_scale(k, gain_ref[1:2, :]).astype(BF16)
        values[:, :HD] = v_ref[...].reshape(-1, HD)
        values[:, HD:] = jnp.ones((values.shape[0], HD), BF16)

    q = q_ref[...].reshape(-1, HD).astype(F32)
    q = rms_scale(q, gain_ref[0:1, :] * (math.log2(math.e) / math.sqrt(HD))).astype(BF16)
    weight = jnp.exp2(dot_t(q, keys[...])).astype(BF16)
    both = jnp.dot(weight, values[...], preferred_element_type=F32)
    num_ref[...] = both[:, :HD]
    den_ref[...] = both[:, HD:]


def image_attention(received, gains):
    sources, _, width = received.shape
    heads = width // HD
    image_len = sources * BLK
    step = 2
    rows = step * BLK
    return pl.pallas_call(
        image_kernel,
        grid=(heads, sources // step),
        in_specs=[
            pl.BlockSpec((step, BLK, HD), lambda h, b: (b, 0, h)),
            pl.BlockSpec((sources, BLK, HD), lambda h, b: (0, 1, h)),
            pl.BlockSpec((sources, BLK, HD), lambda h, b: (0, 2, h)),
            pl.BlockSpec((2, HD), lambda h, b: (0, 0)),
        ],
        out_specs=[
            pl.BlockSpec((rows, HD), lambda h, b: (b, h)),
            pl.BlockSpec((rows, HD), lambda h, b: (b, h)),
        ],
        out_shape=[jax.ShapeDtypeStruct((image_len, width), F32)] * 2,
        scratch_shapes=[pltpu.VMEM((image_len, HD), BF16), pltpu.VMEM((image_len, 2 * HD), BF16)],
        compiler_params=pltpu.CompilerParams(vmem_limit_bytes=24 * 1024 * 1024),
        cost_estimate=pl.CostEstimate(
            flops=6 * image_len * image_len * width,
            bytes_accessed=14 * image_len * width,
            transcendentals=heads * image_len * image_len,
        ),
    )(received, received, received, gains)


def text_kernel(length_ref, q_ref, k_ref, v_ref, gain_ref, text_gain_ref, num_ref, den_ref, out_ref):
    k = rms_scale(k_ref[...], text_gain_ref[...]).astype(BF16)
    v = v_ref[...].astype(BF16)
    q = q_ref[...].reshape(-1, HD).astype(F32)
    q = rms_scale(q, gain_ref[0:1, :] * (math.log2(math.e) / math.sqrt(HD))).astype(BF16)
    weight = jnp.exp2(dot_t(q, k))
    valid = lax.broadcasted_iota(jnp.int32, weight.shape, 1) < length_ref[0]
    weight = jnp.where(valid, weight, 0.0).astype(BF16)
    stacked = jnp.concatenate([v, jnp.ones_like(v)], axis=1)
    both = jnp.dot(weight, stacked, preferred_element_type=F32)
    total = num_ref[...] + both[:, :HD]
    out_ref[...] = (total / (den_ref[...] + both[:, HD:])).astype(BF16)


def text_attention(length, received, key_value, gains, text_gain, num, den):
    sources, _, width = received.shape
    heads = width // HD
    image_len = sources * BLK
    step = sources // 2
    rows = step * BLK
    return pl.pallas_call(
        text_kernel,
        grid=(heads, sources // step),
        in_specs=[
            pl.BlockSpec(memory_space=pltpu.SMEM),
            pl.BlockSpec((step, BLK, HD), lambda h, b: (b, 0, h)),
            pl.BlockSpec((BLK, HD), lambda h, b: (0, h)),
            pl.BlockSpec((BLK, HD), lambda h, b: (0, heads + h)),
            pl.BlockSpec((2, HD), lambda h, b: (0, 0)),
            pl.BlockSpec((1, HD), lambda h, b: (0, 0)),
            pl.BlockSpec((rows, HD), lambda h, b: (b, h)),
            pl.BlockSpec((rows, HD), lambda h, b: (b, h)),
        ],
        out_specs=pl.BlockSpec((rows, HD), lambda h, b: (b, h)),
        out_shape=jax.ShapeDtypeStruct((image_len, width), BF16),
        compiler_params=pltpu.CompilerParams(vmem_limit_bytes=24 * 1024 * 1024),
        cost_estimate=pl.CostEstimate(
            flops=6 * image_len * BLK * width,
            bytes_accessed=12 * image_len * width,
            transcendentals=heads * image_len * BLK,
        ),
    )(length, received, key_value, key_value, gains, text_gain, num, den)


def on_device(
    enc_states,
    lengths,
    prompt_owner_sample,
    t5_gain,
    t5_in_weight,
    t5_out_weight,
    t5_final_gain,
    context_weight,
    text_shift,
    text_scale,
    kv_weight,
    text_key_gain,
    image_query_key_value,
    image_qk_gain,
    proj_weight,
    dora_a,
    dora_b,
    magnitude,
    grad_out,
):
    seq_rank = lax.axis_index("seq")
    data_rank = lax.axis_index("dp")
    n_seq = lax.axis_size("seq")
    n_dp = lax.axis_size("dp")
    n_all = n_seq * n_dp
    both = ("dp", "seq")
    rank, own_cols = dora_b.shape
    own_rows = dora_a.shape[0]
    model = own_cols * n_dp
    lanes = 128
    rows_of = model // lanes
    cotangent = grad_out[0]

    context_all = lax.all_gather(context_weight.T, "dp", axis=0, tiled=True)
    kv_all = lax.all_gather(
        kv_weight.reshape(kv_weight.shape[0], -1), "dp", axis=0, tiled=True
    )

    direction_t = proj_weight.T.astype(F32) + lax.dot_general(
        dora_b, dora_a, (((0,), (1,)), ((), ())), precision=lax.Precision.HIGHEST
    )
    image = image_query_key_value[0].reshape(BLK, 3, n_seq, own_rows)
    image = image.transpose(2, 1, 0, 3).reshape(n_seq, 3 * BLK, own_rows)
    packed = jnp.concatenate(
        [image, jnp.broadcast_to(direction_t.astype(BF16)[None], (n_seq, own_cols, own_rows))], 1
    )
    received = swap(packed, "seq")

    tokens = enc_states[0, :BLK]
    feat = tokens.shape[1] // n_seq
    normed = rms_scale(tokens.astype(F32), t5_gain).astype(BF16)
    gate_proj = jnp.dot(normed, t5_in_weight[0], preferred_element_type=F32)
    upward = jnp.dot(normed, t5_in_weight[1], preferred_element_type=F32)
    hidden = (jax.nn.gelu(gate_proj, approximate=True) * upward).astype(BF16)
    ffn = jnp.dot(hidden, t5_out_weight, preferred_element_type=F32).astype(BF16)
    ffn = ffn.reshape(BLK, n_seq, feat).transpose(1, 0, 2)
    ffn_sum = jnp.sum(swap(ffn, "seq").astype(F32), 0)
    own_tokens = lax.dynamic_slice_in_dim(tokens, seq_rank * feat, feat, 1).astype(F32)
    own_final = lax.dynamic_slice_in_dim(t5_final_gain, seq_rank * feat, feat, 0)
    encoded = ((own_tokens + ffn_sum) * own_final).astype(BF16)
    context = dot_t(encoded, context_all).astype(BF16)

    rows_t = received[:, 3 * BLK :, :]
    rows_f = rows_t.astype(F32)
    column_norm = jnp.sqrt(jnp.sum(rows_f * rows_f, (0, 2)) + EPSILON)
    ratio = magnitude / column_norm
    pair = seq_rank % 2
    rows_z = rows_f.reshape(n_seq // 2, 2, own_cols, own_rows)
    rows_z = jnp.where(pair == 0, rows_z[:, 0], rows_z[:, 1])
    scaled_t = (rows_z * ratio[None, :, None]).astype(BF16)
    scaled_t = scaled_t.transpose(1, 0, 2).reshape(own_cols, -1)
    scaled_all = lax.all_gather(scaled_t, "dp", axis=0, tiled=True)

    share = rank // n_seq
    up_rows = share * own_cols // lanes
    up = lax.dynamic_slice_in_dim(dora_b * ratio, seq_rank * share, share, 0).astype(BF16)
    up = jnp.broadcast_to(up.reshape(1, up_rows, lanes), (BLK, up_rows, lanes))
    pad_rows = (-(rows_of + up_rows)) % 8
    message = jnp.concatenate(
        [context.reshape(BLK, rows_of, lanes), up, jnp.zeros((BLK, pad_rows, lanes), BF16)], 1
    )
    arrived = swap(message, both)
    token_of = jnp.sum(
        arrived[:, :rows_of].reshape(n_dp, n_seq, rows_of, lanes).astype(F32), 1
    ).astype(BF16)
    up_all = arrived[:, rows_of : rows_of + up_rows].reshape(n_dp, rank, own_cols)
    up_all = up_all.transpose(1, 0, 2).reshape(rank, model)
    values = token_of.astype(F32)
    centre = jnp.mean(values, (1, 2), keepdims=True)
    spread = jnp.mean((values - centre) * (values - centre), (1, 2), keepdims=True)
    layer_normed = ((values - centre) * lax.rsqrt(spread + EPSILON)).astype(BF16)
    target = jnp.arange(n_all, dtype=jnp.int32) // n_seq
    one_hot = (target[:, None] == prompt_owner_sample[None, :]).astype(BF16)
    outgoing = jnp.einsum("sp,pab->sab", one_hot, layer_normed, preferred_element_type=F32)
    text = swap(outgoing.astype(BF16), both).reshape(BLK, model)
    modulated = ((1.0 + text_scale) * text.astype(F32) + text_shift).astype(BF16)
    length = jnp.sum(jnp.where(prompt_owner_sample == data_rank, lengths, 0))
    key_value = jnp.dot(modulated, kv_all, preferred_element_type=F32)

    num, den = image_attention(received, image_qk_gain)
    attended = text_attention(
        length.reshape(1), received, key_value, image_qk_gain, text_key_gain.reshape(1, HD), num, den
    )

    tokens_y = 2 * BLK
    gathered = swap(attended.reshape(n_seq // 2, tokens_y, own_rows), "seq", Y_GROUPS)
    gathered = gathered.transpose(1, 0, 2).reshape(tokens_y, -1)
    out_part = dot_t(gathered, scaled_all).astype(BF16).reshape(2, BLK, model)
    out = jnp.sum(swap(out_part, "seq", Z_GROUPS).astype(F32), 0)
    image_out = out.astype(BF16)[None]

    down = dot_t(cotangent, up_all).astype(BF16)
    down_all = swap(jnp.broadcast_to(down[None], (n_seq, BLK, rank)), "seq").reshape(-1, rank)
    grad_a_t = lax.dot_general(
        down_all, attended, (((0,), (0,)), ((), ())), preferred_element_type=F32
    ).astype(BF16)
    lowered = jnp.dot(attended, dora_a.astype(BF16), preferred_element_type=F32).astype(BF16)
    lowered = jnp.sum(swap(lowered.reshape(n_seq, BLK, rank), "seq").astype(F32), 0).astype(BF16)
    up_part = lax.dot_general(
        lowered, cotangent, (((0,), (0,)), ((), ())), preferred_element_type=F32
    ).astype(BF16)
    parts = jnp.concatenate(
        [
            jnp.broadcast_to(grad_a_t[None], (n_dp, rank, own_rows)),
            up_part.reshape(rank, n_dp, own_cols).transpose(1, 0, 2),
        ],
        2,
    )
    parts = jnp.sum(swap(parts, "dp").astype(F32), 0)
    grad_a = parts[:, :own_rows].T
    grad_b = parts[:, own_rows:].astype(BF16)
    grad_b = swap(jnp.broadcast_to(grad_b[None], (n_seq, rank, own_cols)), "seq")
    grad_b = jnp.sum(grad_b.astype(F32), 0) * ratio
    magnitude_part = jnp.sum(out * cotangent.astype(F32), 0).astype(BF16)
    magnitude_part = jnp.broadcast_to(
        magnitude_part.reshape(n_dp, 1, own_cols), (n_dp, n_seq, own_cols)
    )
    magnitude_part = swap(magnitude_part.reshape(n_all, own_cols), both)
    grad_magnitude = jnp.sum(magnitude_part.astype(F32), 0) / magnitude
    return (image_out, grad_a, grad_b, grad_magnitude)


def solution(mesh):
    return jax.shard_map(
        on_device,
        mesh=mesh,
        in_specs=(
            P("dp", None, None),
            P(),
            P(),
            P(),
            P(None, None, "seq"),
            P("seq", None),
            P(),
            P("seq", "dp"),
            P("dp", None),
            P("dp", None),
            P("dp", None, "seq"),
            P(),
            P("dp", "seq", None, None),
            P(),
            P("seq", "dp"),
            P("seq", None),
            P(None, "dp"),
            P("dp"),
            P("dp", "seq", None),
        ),
        out_specs=(P("dp", "seq", None), P("seq", None), P(None, "dp"), P("dp")),
        check_vma=False,
    )
```

```python
import math

import jax
import jax.numpy as jnp
from jax import lax
from jax.experimental import pallas as pl
from jax.experimental.pallas import tpu as pltpu
from jax.sharding import PartitionSpec as P

HD = 128
BLK = 128
EPSILON = 1e-06
F32 = jnp.float32
BF16 = jnp.bfloat16
Y_GROUPS = [[0, 2, 4, 6], [1, 3, 5, 7]]
QUERY_SCALE = math.log2(math.e) / math.sqrt(HD)


def rms_scale(values, gain):
    return values * lax.rsqrt(jnp.mean(values * values, -1, keepdims=True) + EPSILON) * gain


def swap(values, axes, groups=None):
    return lax.all_to_all(values, axes, 0, 0, tiled=True, axis_index_groups=groups)


def dot_t(left, right):
    return lax.dot_general(left, right, (((1,), (1,)), ((), ())), preferred_element_type=F32)


def pack_kernel(_, in_ref, out_ref):
    out_ref[0, 0] = in_ref[...].reshape(out_ref.shape[2:])


def pack_heads(rows, pair, n_seq):
    kinds, count, model = rows.shape
    width = model // n_seq
    return pl.pallas_call(
        pack_kernel,
        grid_spec=pltpu.PrefetchScalarGridSpec(
            num_scalar_prefetch=1,
            grid=(n_seq // 2, 2),
            in_specs=[
                pl.BlockSpec((kinds, count, width), lambda y, k, z: (0, 0, 2 * y + (z[0] + k) % 2))
            ],
            out_specs=pl.BlockSpec((1, 1, kinds * count, width), lambda y, k, z: (y, k, 0, 0)),
        ),
        out_shape=jax.ShapeDtypeStruct((n_seq // 2, 2, kinds * count, width), rows.dtype),
        compiler_params=pltpu.CompilerParams(vmem_limit_bytes=16 * 1024 * 1024),
        cost_estimate=pl.CostEstimate(flops=0, bytes_accessed=4 * rows.size, transcendentals=0),
    )(pair.reshape(1), rows)


def image_kernel(
    q_own, q_other, k_own, k_other, v_own, v_other, gain_ref, num_ref, den_ref, keys, values
):
    half = keys.shape[0] // 2

    @pl.when(pl.program_id(1) == 0)
    def _():
        for at, k_ref, v_ref in ((0, k_own, v_own), (half, k_other, v_other)):
            k = k_ref[...].reshape(-1, HD).astype(F32)
            keys[at : at + half, :] = rms_scale(k, gain_ref[1:2, :]).astype(BF16)
            values[at : at + half, :HD] = v_ref[...].reshape(-1, HD)
        values[:, HD:] = jnp.ones((2 * half, HD), BF16)

    q = jnp.concatenate([q_own[...].reshape(-1, HD), q_other[...].reshape(-1, HD)], 0)
    q = rms_scale(q.astype(F32), gain_ref[0:1, :] * QUERY_SCALE).astype(BF16)
    weight = jnp.exp2(dot_t(q, keys[...])).astype(BF16)
    both = jnp.dot(weight, values[...], preferred_element_type=F32)
    num_ref[...] = both[:, :HD]
    den_ref[...] = both[:, HD:]


def image_attention(own, other, gains):
    n_y, _, _, width = own.shape
    heads = width // HD
    rows = 2 * BLK
    image_len = n_y * rows

    def own_spec(count, kind):
        if count == 1:
            return pl.BlockSpec((1, 1, BLK, HD), lambda h, b: (b, 0, kind, h))
        return pl.BlockSpec((count, 1, BLK, HD), lambda h, b: (0, 0, kind, h))

    def other_spec(count, kind):
        if count == 1:
            return pl.BlockSpec((1, BLK, HD), lambda h, b: (b, kind, h))
        return pl.BlockSpec((count, BLK, HD), lambda h, b: (0, kind, h))

    return pl.pallas_call(
        image_kernel,
        grid=(heads, n_y),
        in_specs=[
            own_spec(1, 0),
            other_spec(1, 0),
            own_spec(n_y, 1),
            other_spec(n_y, 1),
            own_spec(n_y, 2),
            other_spec(n_y, 2),
            pl.BlockSpec((2, HD), lambda h, b: (0, 0)),
        ],
        out_specs=[
            pl.BlockSpec((rows, HD), lambda h, b: (b, h)),
            pl.BlockSpec((rows, HD), lambda h, b: (b, h)),
        ],
        out_shape=[jax.ShapeDtypeStruct((image_len, width), F32)] * 2,
        scratch_shapes=[pltpu.VMEM((image_len, HD), BF16), pltpu.VMEM((image_len, 2 * HD), BF16)],
        compiler_params=pltpu.CompilerParams(vmem_limit_bytes=24 * 1024 * 1024),
        cost_estimate=pl.CostEstimate(
            flops=6 * image_len * image_len * width,
            bytes_accessed=14 * image_len * width,
            transcendentals=heads * image_len * image_len,
        ),
    )(own, other, own, other, own, other, gains)


def text_kernel(
    length_ref, q_own, q_other, k_ref, v_ref, gain_ref, text_gain_ref, num_ref, den_ref, out_ref
):
    k = rms_scale(k_ref[...], text_gain_ref[...]).astype(BF16)
    v = v_ref[...].astype(BF16)
    stacked = jnp.concatenate([v, jnp.ones_like(v)], axis=1)
    for b in range(q_other.shape[0]):
        q = jnp.concatenate([q_own[b, 0], q_other[b]], 0).astype(F32)
        q = rms_scale(q, gain_ref[0:1, :] * QUERY_SCALE).astype(BF16)
        weight = jnp.exp2(dot_t(q, k))
        valid = lax.broadcasted_iota(jnp.int32, weight.shape, 1) < length_ref[0]
        weight = jnp.where(valid, weight, 0.0).astype(BF16)
        both = jnp.dot(weight, stacked, preferred_element_type=F32)
        rows = slice(b * q.shape[0], (b + 1) * q.shape[0])
        total = num_ref[rows, :] + both[:, :HD]
        out_ref[rows, :] = (total / (den_ref[rows, :] + both[:, HD:])).astype(BF16)


def text_attention(length, own, other, key_value, gains, text_gain, num, den):
    n_y, _, _, width = own.shape
    heads = width // HD
    image_len = n_y * 2 * BLK
    step = n_y // 2
    rows = step * 2 * BLK
    return pl.pallas_call(
        text_kernel,
        grid=(heads, n_y // step),
        in_specs=[
            pl.BlockSpec(memory_space=pltpu.SMEM),
            pl.BlockSpec((step, 1, BLK, HD), lambda h, b: (b, 0, 0, h)),
            pl.BlockSpec((step, BLK, HD), lambda h, b: (b, 0, h)),
            pl.BlockSpec((BLK, HD), lambda h, b: (0, h)),
            pl.BlockSpec((BLK, HD), lambda h, b: (0, heads + h)),
            pl.BlockSpec((2, HD), lambda h, b: (0, 0)),
            pl.BlockSpec((1, HD), lambda h, b: (0, 0)),
            pl.BlockSpec((rows, HD), lambda h, b: (b, h)),
            pl.BlockSpec((rows, HD), lambda h, b: (b, h)),
        ],
        out_specs=pl.BlockSpec((rows, HD), lambda h, b: (b, h)),
        out_shape=jax.ShapeDtypeStruct((image_len, width), BF16),
        compiler_params=pltpu.CompilerParams(vmem_limit_bytes=24 * 1024 * 1024),
        cost_estimate=pl.CostEstimate(
            flops=6 * image_len * BLK * width,
            bytes_accessed=12 * image_len * width,
            transcendentals=heads * image_len * BLK,
        ),
    )(length, own, other, key_value, key_value, gains, text_gain, num, den)


def on_device(
    enc_states,
    lengths,
    prompt_owner_sample,
    t5_gain,
    t5_in_weight,
    t5_out_weight,
    t5_final_gain,
    context_weight,
    text_shift,
    text_scale,
    kv_weight,
    text_key_gain,
    image_query_key_value,
    image_qk_gain,
    proj_weight,
    dora_a,
    dora_b,
    magnitude,
    grad_out,
):
    seq_rank = lax.axis_index("seq")
    data_rank = lax.axis_index("dp")
    n_seq = lax.axis_size("seq")
    n_dp = lax.axis_size("dp")
    n_all = n_seq * n_dp
    both = ("dp", "seq")
    rank, own_cols = dora_b.shape
    own_rows = dora_a.shape[0]
    model = own_cols * n_dp
    lanes = 128
    rows_of = model // lanes
    cotangent = grad_out[0]

    pair = seq_rank % 2
    flip_z = [(i, i ^ 1) for i in range(n_seq)]
    n_y = n_seq // 2

    weights = jnp.concatenate(
        [context_weight.T, kv_weight.reshape(kv_weight.shape[0], -1)], 1
    )
    weights = lax.all_gather(weights, "dp", axis=0, tiled=True)
    depth = context_weight.shape[0]
    context_all, kv_all = weights[:, :depth], weights[:, depth:]

    direction_t = proj_weight.T.astype(F32) + lax.dot_general(
        dora_b, dora_a, (((0,), (1,)), ((), ())), precision=lax.Precision.HIGHEST
    )
    direction_t = direction_t.astype(BF16)
    rows_y = swap(jnp.broadcast_to(direction_t[None], (n_y, own_cols, own_rows)), "seq", Y_GROUPS)

    tokens = enc_states[0, :BLK]
    feat = tokens.shape[1] // n_seq
    normed = rms_scale(tokens.astype(F32), t5_gain).astype(BF16)
    gate_proj = jnp.dot(normed, t5_in_weight[0], preferred_element_type=F32)
    upward = jnp.dot(normed, t5_in_weight[1], preferred_element_type=F32)
    hidden = (jax.nn.gelu(gate_proj, approximate=True) * upward).astype(BF16)
    ffn = jnp.dot(hidden, t5_out_weight, preferred_element_type=F32).astype(BF16)
    ffn = ffn.reshape(BLK, n_seq, feat).transpose(1, 0, 2)
    packed = pack_heads(image_query_key_value[0].transpose(1, 0, 2), pair, n_seq)
    rows_y, ffn, packed = lax.optimization_barrier((rows_y, ffn, packed))
    ffn = swap(ffn, "seq")
    ffn, packed = lax.optimization_barrier((ffn, packed))
    ffn_sum = jnp.sum(ffn.astype(F32), 0)

    own_heads = swap(packed, "seq", Y_GROUPS)

    rows_f = rows_y.astype(F32)
    column_sq = jnp.sum(rows_f * rows_f, (0, 2))
    column_sq = column_sq + lax.ppermute(column_sq, "seq", flip_z)
    ratio = magnitude / jnp.sqrt(column_sq + EPSILON)
    scaled_t = (rows_f * ratio[None, :, None]).astype(BF16)
    scaled_t = scaled_t.transpose(1, 0, 2).reshape(own_cols, -1)
    reach = scaled_t.shape[1]
    up = jnp.pad((dora_b * ratio).astype(BF16).T, ((0, 0), (0, lanes - rank)))
    scaled_all = lax.all_gather(jnp.concatenate([scaled_t, up], 1), "dp", axis=0, tiled=True)
    up_all = scaled_all[:, reach:]

    own_tokens = lax.dynamic_slice_in_dim(tokens, seq_rank * feat, feat, 1).astype(F32)
    own_final = lax.dynamic_slice_in_dim(t5_final_gain, seq_rank * feat, feat, 0)
    encoded = ((own_tokens + ffn_sum) * own_final).astype(BF16)
    context = dot_t(encoded, context_all).astype(BF16).reshape(BLK, rows_of, lanes)
    context, own_heads = lax.optimization_barrier((context, own_heads))
    other_heads = lax.ppermute(own_heads[:, 1], "seq", flip_z)
    arrived = swap(context, both)
    token_of = jnp.sum(arrived.reshape(n_dp, n_seq, rows_of, lanes).astype(F32), 1).astype(BF16)
    values = token_of.astype(F32)
    centre = jnp.mean(values, (1, 2), keepdims=True)
    spread = jnp.mean((values - centre) * (values - centre), (1, 2), keepdims=True)
    layer_normed = ((values - centre) * lax.rsqrt(spread + EPSILON)).astype(BF16)
    target = jnp.arange(n_all, dtype=jnp.int32) // n_seq
    one_hot = (target[:, None] == prompt_owner_sample[None, :]).astype(BF16)
    outgoing = jnp.einsum("sp,pab->sab", one_hot, layer_normed, preferred_element_type=F32)
    text = swap(outgoing.astype(BF16), both).reshape(BLK, model)
    modulated = ((1.0 + text_scale) * text.astype(F32) + text_shift).astype(BF16)
    length = jnp.sum(jnp.where(prompt_owner_sample == data_rank, lengths, 0))
    key_value = jnp.dot(modulated, kv_all, preferred_element_type=F32)

    num, den = image_attention(own_heads, other_heads, image_qk_gain)
    num, den, key_value = lax.optimization_barrier((num, den, key_value))
    attended = text_attention(
        length.reshape(1),
        own_heads,
        other_heads,
        key_value,
        image_qk_gain,
        text_key_gain.reshape(1, HD),
        num,
        den,
    )

    lowered = jnp.dot(attended, dora_a.astype(BF16), preferred_element_type=F32).astype(BF16)
    outgoing = jnp.concatenate([attended, lowered], 1).reshape(n_y, 2 * BLK, own_rows + rank)
    gathered = swap(outgoing, "seq", Y_GROUPS)
    lowered = jnp.sum(gathered[:, :, own_rows:].astype(F32), 0)
    gathered = gathered[:, :, :own_rows].transpose(1, 0, 2).reshape(2 * BLK, -1)
    scaled_z = scaled_all[:, :reach]
    sent = dot_t(gathered[BLK:], scaled_z)
    sent = jnp.concatenate([sent, lowered[BLK:]], 1).astype(BF16)
    landed = lax.ppermute(sent, "seq", flip_z).astype(F32)
    kept = lax.optimization_barrier(dot_t(gathered[:BLK], scaled_z))
    out = kept + landed[:, :model]
    image_out = out.astype(BF16)[None]
    lowered = (lowered[:BLK] + landed[:, model:]).astype(BF16)

    down = jnp.dot(cotangent, up_all, preferred_element_type=F32).astype(BF16)
    down = jnp.concatenate([down, lax.ppermute(down, "seq", flip_z)], 0)
    down_all = swap(jnp.broadcast_to(down[None], (n_y,) + down.shape), "seq", Y_GROUPS)
    down_all = down_all.reshape(-1, lanes)[:, :rank]
    grad_a = lax.dot_general(
        down_all, attended, (((0,), (0,)), ((), ())), preferred_element_type=F32
    )
    for bit in (1, 2, 4, 8):
        grad_a = grad_a.astype(BF16)
        moved = lax.ppermute(grad_a, "dp", [(i, i ^ bit) for i in range(n_dp)])
        grad_a = grad_a.astype(F32) + moved.astype(F32)
    grad_a = grad_a.T
    up_part = lax.dot_general(
        lowered, cotangent, (((0,), (0,)), ((), ())), preferred_element_type=F32
    ).astype(BF16)
    magnitude_part = jnp.sum(out * cotangent.astype(F32), 0).astype(BF16)
    parts = jnp.concatenate([up_part, jnp.pad(magnitude_part[None], ((0, 7), (0, 0)))], 0)
    parts = parts.reshape(rank + 8, n_dp, own_cols).transpose(1, 0, 2)
    parts = jnp.sum(swap(parts, "dp").astype(F32), 0).astype(BF16)
    parts = swap(jnp.broadcast_to(parts[None], (n_seq,) + parts.shape), "seq")
    parts = jnp.sum(parts.astype(F32), 0)
    grad_b = parts[:rank] * ratio
    grad_magnitude = parts[rank] / magnitude
    return (image_out, grad_a, grad_b, grad_magnitude)


def solution(mesh):
    return jax.shard_map(
        on_device,
        mesh=mesh,
        in_specs=(
            P("dp", None, None),
            P(),
            P(),
            P(),
            P(None, None, "seq"),
            P("seq", None),
            P(),
            P("seq", "dp"),
            P("dp", None),
            P("dp", None),
            P("dp", None, "seq"),
            P(),
            P("dp", "seq", None, None),
            P(),
            P("seq", "dp"),
            P("seq", None),
            P(None, "dp"),
            P("dp"),
            P("dp", "seq", None),
        ),
        out_specs=(P("dp", "seq", None), P("seq", None), P(None, "dp"), P("dp")),
        check_vma=False,
    )
```

```python
import math

import jax
import jax.numpy as jnp
from jax import lax
from jax.experimental import pallas as pl
from jax.experimental.pallas import tpu as pltpu
from jax.sharding import PartitionSpec as P

HD = 128
BLK = 128
EPSILON = 1e-06
F32 = jnp.float32
BF16 = jnp.bfloat16
Y_GROUPS = [[0, 2, 4, 6], [1, 3, 5, 7]]
QUERY_SCALE = math.log2(math.e) / math.sqrt(HD)


def rms_scale(values, gain):
    return values * lax.rsqrt(jnp.mean(values * values, -1, keepdims=True) + EPSILON) * gain


def swap(values, axes, groups=None):
    return lax.all_to_all(values, axes, 0, 0, tiled=True, axis_index_groups=groups)


def gather_columns(values):
    n_dp = lax.axis_size("dp")
    near = n_dp // 2
    other = lax.ppermute(values, "dp", [(i, (i + near) % n_dp) for i in range(n_dp)])
    low = lax.axis_index("dp") < near
    halves = jnp.stack([jnp.where(low, values, other), jnp.where(low, other, values)])
    groups = [list(range(near)), list(range(near, n_dp))]
    gathered = lax.all_gather(halves, "dp", axis=0, axis_index_groups=groups)
    return gathered.reshape(n_dp * values.shape[0], values.shape[1])


def to_gathered(values, n_dp):
    rows = values.shape[0]
    cut = values.reshape(rows, 2, n_dp // 2, -1)
    return cut.transpose(0, 2, 1, 3).reshape(rows, -1)


def from_gathered(values, n_dp):
    rows = values.shape[0]
    cut = values.reshape(rows, n_dp // 2, 2, -1)
    return cut.transpose(0, 2, 1, 3).reshape(rows, -1)


def dot_t(left, right):
    return lax.dot_general(left, right, (((1,), (1,)), ((), ())), preferred_element_type=F32)


def pack_kernel(_, in_ref, out_ref):
    out_ref[0, 0] = in_ref[...].reshape(out_ref.shape[2:])


def pack_heads(rows, pair, n_seq):
    kinds, count, model = rows.shape
    width = model // n_seq
    return pl.pallas_call(
        pack_kernel,
        grid_spec=pltpu.PrefetchScalarGridSpec(
            num_scalar_prefetch=1,
            grid=(n_seq // 2, 2),
            in_specs=[
                pl.BlockSpec((kinds, count, width), lambda y, k, z: (0, 0, 2 * y + (z[0] + k) % 2))
            ],
            out_specs=pl.BlockSpec((1, 1, kinds * count, width), lambda y, k, z: (y, k, 0, 0)),
        ),
        out_shape=jax.ShapeDtypeStruct((n_seq // 2, 2, kinds * count, width), rows.dtype),
        compiler_params=pltpu.CompilerParams(vmem_limit_bytes=16 * 1024 * 1024),
        cost_estimate=pl.CostEstimate(flops=0, bytes_accessed=4 * rows.size, transcendentals=0),
    )(pair.reshape(1), rows)


def image_kernel(
    q_own, q_other, k_own, k_other, v_own, v_other, gain_ref, num_ref, den_ref, keys, values
):
    half = keys.shape[0] // 2

    @pl.when(pl.program_id(1) == 0)
    def _():
        for at, k_ref, v_ref in ((0, k_own, v_own), (half, k_other, v_other)):
            k = k_ref[...].reshape(-1, HD).astype(F32)
            keys[at : at + half, :] = rms_scale(k, gain_ref[1:2, :]).astype(BF16)
            values[at : at + half, :HD] = v_ref[...].reshape(-1, HD)
        values[:, HD:] = jnp.ones((2 * half, HD), BF16)

    q = jnp.concatenate([q_own[...].reshape(-1, HD), q_other[...].reshape(-1, HD)], 0)
    q = rms_scale(q.astype(F32), gain_ref[0:1, :] * QUERY_SCALE).astype(BF16)
    weight = jnp.exp2(dot_t(q, keys[...])).astype(BF16)
    both = jnp.dot(weight, values[...], preferred_element_type=F32)
    num_ref[...] = both[:, :HD]
    den_ref[...] = both[:, HD:]


def image_attention(own, other, gains):
    n_y, _, _, width = own.shape
    heads = width // HD
    rows = 2 * BLK
    image_len = n_y * rows

    def own_spec(count, kind):
        if count == 1:
            return pl.BlockSpec((1, 1, BLK, HD), lambda h, b: (b, 0, kind, h))
        return pl.BlockSpec((count, 1, BLK, HD), lambda h, b: (0, 0, kind, h))

    def other_spec(count, kind):
        if count == 1:
            return pl.BlockSpec((1, BLK, HD), lambda h, b: (b, kind, h))
        return pl.BlockSpec((count, BLK, HD), lambda h, b: (0, kind, h))

    return pl.pallas_call(
        image_kernel,
        grid=(heads, n_y),
        in_specs=[
            own_spec(1, 0),
            other_spec(1, 0),
            own_spec(n_y, 1),
            other_spec(n_y, 1),
            own_spec(n_y, 2),
            other_spec(n_y, 2),
            pl.BlockSpec((2, HD), lambda h, b: (0, 0)),
        ],
        out_specs=[
            pl.BlockSpec((rows, HD), lambda h, b: (b, h)),
            pl.BlockSpec((rows, HD), lambda h, b: (b, h)),
        ],
        out_shape=[jax.ShapeDtypeStruct((image_len, width), F32)] * 2,
        scratch_shapes=[pltpu.VMEM((image_len, HD), BF16), pltpu.VMEM((image_len, 2 * HD), BF16)],
        compiler_params=pltpu.CompilerParams(vmem_limit_bytes=24 * 1024 * 1024),
        cost_estimate=pl.CostEstimate(
            flops=6 * image_len * image_len * width,
            bytes_accessed=14 * image_len * width,
            transcendentals=heads * image_len * image_len,
        ),
    )(own, other, own, other, own, other, gains)


def text_kernel(
    length_ref, q_own, q_other, k_ref, v_ref, gain_ref, text_gain_ref, num_ref, den_ref, out_ref
):
    k = rms_scale(k_ref[...], text_gain_ref[...]).astype(BF16)
    v = v_ref[...].astype(BF16)
    stacked = jnp.concatenate([v, jnp.ones_like(v)], axis=1)
    for b in range(q_other.shape[0]):
        q = jnp.concatenate([q_own[b, 0], q_other[b]], 0).astype(F32)
        q = rms_scale(q, gain_ref[0:1, :] * QUERY_SCALE).astype(BF16)
        weight = jnp.exp2(dot_t(q, k))
        valid = lax.broadcasted_iota(jnp.int32, weight.shape, 1) < length_ref[0]
        weight = jnp.where(valid, weight, 0.0).astype(BF16)
        both = jnp.dot(weight, stacked, preferred_element_type=F32)
        rows = slice(b * q.shape[0], (b + 1) * q.shape[0])
        total = num_ref[rows, :] + both[:, :HD]
        out_ref[rows, :] = (total / (den_ref[rows, :] + both[:, HD:])).astype(BF16)


def text_attention(length, own, other, key_value, gains, text_gain, num, den):
    n_y, _, _, width = own.shape
    heads = width // HD
    image_len = n_y * 2 * BLK
    step = n_y // 2
    rows = step * 2 * BLK
    return pl.pallas_call(
        text_kernel,
        grid=(heads, n_y // step),
        in_specs=[
            pl.BlockSpec(memory_space=pltpu.SMEM),
            pl.BlockSpec((step, 1, BLK, HD), lambda h, b: (b, 0, 0, h)),
            pl.BlockSpec((step, BLK, HD), lambda h, b: (b, 0, h)),
            pl.BlockSpec((BLK, HD), lambda h, b: (0, h)),
            pl.BlockSpec((BLK, HD), lambda h, b: (0, heads + h)),
            pl.BlockSpec((2, HD), lambda h, b: (0, 0)),
            pl.BlockSpec((1, HD), lambda h, b: (0, 0)),
            pl.BlockSpec((rows, HD), lambda h, b: (b, h)),
            pl.BlockSpec((rows, HD), lambda h, b: (b, h)),
        ],
        out_specs=pl.BlockSpec((rows, HD), lambda h, b: (b, h)),
        out_shape=jax.ShapeDtypeStruct((image_len, width), BF16),
        compiler_params=pltpu.CompilerParams(vmem_limit_bytes=24 * 1024 * 1024),
        cost_estimate=pl.CostEstimate(
            flops=6 * image_len * BLK * width,
            bytes_accessed=12 * image_len * width,
            transcendentals=heads * image_len * BLK,
        ),
    )(length, own, other, key_value, key_value, gains, text_gain, num, den)


def on_device(
    enc_states,
    lengths,
    prompt_owner_sample,
    t5_gain,
    t5_in_weight,
    t5_out_weight,
    t5_final_gain,
    context_weight,
    text_shift,
    text_scale,
    kv_weight,
    text_key_gain,
    image_query_key_value,
    image_qk_gain,
    proj_weight,
    dora_a,
    dora_b,
    magnitude,
    grad_out,
):
    seq_rank = lax.axis_index("seq")
    data_rank = lax.axis_index("dp")
    n_seq = lax.axis_size("seq")
    n_dp = lax.axis_size("dp")
    n_all = n_seq * n_dp
    both = ("dp", "seq")
    rank, own_cols = dora_b.shape
    own_rows = dora_a.shape[0]
    model = own_cols * n_dp
    lanes = 128
    rows_of = model // lanes
    cotangent = to_gathered(grad_out[0], n_dp)

    pair = seq_rank % 2
    flip_z = [(i, i ^ 1) for i in range(n_seq)]
    n_y = n_seq // 2

    weights = jnp.concatenate(
        [context_weight.T, kv_weight.reshape(kv_weight.shape[0], -1)], 1
    )
    weights = gather_columns(weights)
    depth = context_weight.shape[0]
    context_all, kv_all = weights[:, :depth], weights[:, depth:]

    direction_t = proj_weight.T.astype(F32) + lax.dot_general(
        dora_b, dora_a, (((0,), (1,)), ((), ())), precision=lax.Precision.HIGHEST
    )
    direction_t = direction_t.astype(BF16)
    rows_y = swap(jnp.broadcast_to(direction_t[None], (n_y, own_cols, own_rows)), "seq", Y_GROUPS)

    tokens = enc_states[0, :BLK]
    feat = tokens.shape[1] // n_seq
    normed = rms_scale(tokens.astype(F32), t5_gain).astype(BF16)
    gate_proj = jnp.dot(normed, t5_in_weight[0], preferred_element_type=F32)
    upward = jnp.dot(normed, t5_in_weight[1], preferred_element_type=F32)
    hidden = (jax.nn.gelu(gate_proj, approximate=True) * upward).astype(BF16)
    ffn = jnp.dot(hidden, t5_out_weight, preferred_element_type=F32).astype(BF16)
    ffn = ffn.reshape(BLK, n_seq, feat).transpose(1, 0, 2)
    packed = pack_heads(image_query_key_value[0].transpose(1, 0, 2), pair, n_seq)
    rows_y, ffn, packed = lax.optimization_barrier((rows_y, ffn, packed))
    ffn = swap(ffn, "seq")
    ffn, packed = lax.optimization_barrier((ffn, packed))
    ffn_sum = jnp.sum(ffn.astype(F32), 0)

    own_heads = swap(packed, "seq", Y_GROUPS)

    rows_f = rows_y.astype(F32)
    column_sq = jnp.sum(rows_f * rows_f, (0, 2))
    column_sq = column_sq + lax.ppermute(column_sq, "seq", flip_z)
    ratio = magnitude / jnp.sqrt(column_sq + EPSILON)
    scaled_t = (rows_f * ratio[None, :, None]).astype(BF16)
    scaled_t = scaled_t.transpose(1, 0, 2).reshape(own_cols, -1)
    reach = scaled_t.shape[1]
    up = jnp.pad((dora_b * ratio).astype(BF16).T, ((0, 0), (0, lanes - rank)))
    scaled_all = gather_columns(jnp.concatenate([scaled_t, up], 1))
    up_all = scaled_all[:, reach:]

    own_tokens = lax.dynamic_slice_in_dim(tokens, seq_rank * feat, feat, 1).astype(F32)
    own_final = lax.dynamic_slice_in_dim(t5_final_gain, seq_rank * feat, feat, 0)
    encoded = ((own_tokens + ffn_sum) * own_final).astype(BF16)
    context = dot_t(encoded, context_all).astype(BF16).reshape(BLK, rows_of, lanes)
    context, own_heads = lax.optimization_barrier((context, own_heads))
    other_heads = lax.ppermute(own_heads[:, 1], "seq", flip_z)
    arrived = swap(context, both)
    token_of = jnp.sum(arrived.reshape(n_dp, n_seq, rows_of, lanes).astype(F32), 1).astype(BF16)
    values = token_of.astype(F32)
    centre = jnp.mean(values, (1, 2), keepdims=True)
    spread = jnp.mean((values - centre) * (values - centre), (1, 2), keepdims=True)
    layer_normed = ((values - centre) * lax.rsqrt(spread + EPSILON)).astype(BF16)
    target = jnp.arange(n_all, dtype=jnp.int32) // n_seq
    one_hot = (target[:, None] == prompt_owner_sample[None, :]).astype(BF16)
    outgoing = jnp.einsum("sp,pab->sab", one_hot, layer_normed, preferred_element_type=F32)
    text = swap(outgoing.astype(BF16), both).reshape(BLK, model)
    scale, shift = to_gathered(text_scale, n_dp), to_gathered(text_shift, n_dp)
    modulated = ((1.0 + scale) * text.astype(F32) + shift).astype(BF16)
    length = jnp.sum(jnp.where(prompt_owner_sample == data_rank, lengths, 0))
    key_value = jnp.dot(modulated, kv_all, preferred_element_type=F32)

    num, den = image_attention(own_heads, other_heads, image_qk_gain)
    num, den, key_value = lax.optimization_barrier((num, den, key_value))
    attended = text_attention(
        length.reshape(1),
        own_heads,
        other_heads,
        key_value,
        image_qk_gain,
        text_key_gain.reshape(1, HD),
        num,
        den,
    )

    lowered = jnp.dot(attended, dora_a.astype(BF16), preferred_element_type=F32).astype(BF16)
    outgoing = jnp.concatenate([attended, lowered], 1).reshape(n_y, 2 * BLK, own_rows + rank)
    gathered = swap(outgoing, "seq", Y_GROUPS)
    lowered = jnp.sum(gathered[:, :, own_rows:].astype(F32), 0)
    gathered = gathered[:, :, :own_rows].transpose(1, 0, 2).reshape(2 * BLK, -1)
    scaled_z = scaled_all[:, :reach]
    sent = dot_t(gathered[BLK:], scaled_z)
    sent = jnp.concatenate([sent, lowered[BLK:]], 1).astype(BF16)
    landed = lax.ppermute(sent, "seq", flip_z).astype(F32)
    kept = lax.optimization_barrier(dot_t(gathered[:BLK], scaled_z))
    out = kept + landed[:, :model]
    image_out = from_gathered(out.astype(BF16), n_dp)[None]
    lowered = (lowered[:BLK] + landed[:, model:]).astype(BF16)

    down = jnp.dot(cotangent, up_all, preferred_element_type=F32).astype(BF16)
    down = jnp.concatenate([down, lax.ppermute(down, "seq", flip_z)], 0)
    down_all = swap(jnp.broadcast_to(down[None], (n_y,) + down.shape), "seq", Y_GROUPS)
    down_all = down_all.reshape(-1, lanes)[:, :rank]
    grad_a = lax.dot_general(
        down_all, attended, (((0,), (0,)), ((), ())), preferred_element_type=F32
    )
    for bit in (1, 2, 4, 8):
        grad_a = grad_a.astype(BF16)
        moved = lax.ppermute(grad_a, "dp", [(i, i ^ bit) for i in range(n_dp)])
        grad_a = grad_a.astype(F32) + moved.astype(F32)
    grad_a = grad_a.T
    up_part = lax.dot_general(
        lowered, cotangent, (((0,), (0,)), ((), ())), preferred_element_type=F32
    ).astype(BF16)
    magnitude_part = jnp.sum(out * cotangent.astype(F32), 0).astype(BF16)
    parts = jnp.concatenate([up_part, jnp.pad(magnitude_part[None], ((0, 7), (0, 0)))], 0)
    parts = parts.reshape(rank + 8, n_dp // 2, 2, own_cols).transpose(2, 1, 0, 3)
    parts = parts.reshape(n_dp, rank + 8, own_cols)
    parts = jnp.sum(swap(parts, "dp").astype(F32), 0).astype(BF16)
    parts = swap(jnp.broadcast_to(parts[None], (n_seq,) + parts.shape), "seq")
    parts = jnp.sum(parts.astype(F32), 0)
    grad_b = parts[:rank] * ratio
    grad_magnitude = parts[rank] / magnitude
    return (image_out, grad_a, grad_b, grad_magnitude)


def solution(mesh):
    return jax.shard_map(
        on_device,
        mesh=mesh,
        in_specs=(
            P("dp", None, None),
            P(),
            P(),
            P(),
            P(None, None, "seq"),
            P("seq", None),
            P(),
            P("seq", "dp"),
            P("dp", None),
            P("dp", None),
            P("dp", None, "seq"),
            P(),
            P("dp", "seq", None, None),
            P(),
            P("seq", "dp"),
            P("seq", None),
            P(None, "dp"),
            P("dp"),
            P("dp", "seq", None),
        ),
        out_specs=(P("dp", "seq", None), P("seq", None), P(None, "dp"), P("dp")),
        check_vma=False,
    )
```

```python
import math

import jax
import jax.numpy as jnp
from jax import lax
from jax.experimental import pallas as pl
from jax.experimental.pallas import tpu as pltpu
from jax.sharding import PartitionSpec as P

HD = 128
BLK = 128
EPSILON = 1e-06
F32 = jnp.float32
BF16 = jnp.bfloat16
Y_GROUPS = [[0, 2, 4, 6], [1, 3, 5, 7]]
QUERY_SCALE = math.log2(math.e) / math.sqrt(HD)


def rms_scale(values, gain):
    return values * lax.rsqrt(jnp.mean(values * values, -1, keepdims=True) + EPSILON) * gain


def swap(values, axes, groups=None):
    return lax.all_to_all(values, axes, 0, 0, tiled=True, axis_index_groups=groups)


def near_shard(values):
    n_dp = lax.axis_size("dp")
    return lax.ppermute(values, "dp", [(i, (i + n_dp // 2) % n_dp) for i in range(n_dp)])


def gather_columns(values, other):
    n_dp = lax.axis_size("dp")
    near = n_dp // 2
    low = lax.axis_index("dp") < near
    halves = jnp.stack([jnp.where(low, values, other), jnp.where(low, other, values)])
    groups = [list(range(near)), list(range(near, n_dp))]
    gathered = lax.all_gather(halves, "dp", axis=0, axis_index_groups=groups)
    return gathered.reshape(n_dp * values.shape[0], values.shape[1])


def to_gathered(values, n_dp):
    rows = values.shape[0]
    cut = values.reshape(rows, 2, n_dp // 2, -1)
    return cut.transpose(0, 2, 1, 3).reshape(rows, -1)


def from_gathered(values, n_dp):
    rows = values.shape[0]
    cut = values.reshape(rows, n_dp // 2, 2, -1)
    return cut.transpose(0, 2, 1, 3).reshape(rows, -1)


def dot_t(left, right):
    return lax.dot_general(left, right, (((1,), (1,)), ((), ())), preferred_element_type=F32)


def pack_kernel(_, own_in, other_in, own_ref, other_ref):
    own_ref[0] = own_in[...].reshape(own_ref.shape[1:])
    other_ref[0] = other_in[...].reshape(other_ref.shape[1:])


def pack_heads(rows, pair, n_seq):
    kinds, count, model = rows.shape
    width = model // n_seq
    n_y = n_seq // 2
    block = (kinds, count, width)
    shape = jax.ShapeDtypeStruct((n_y, kinds * count, width), rows.dtype)
    out_spec = pl.BlockSpec((1, kinds * count, width), lambda y, z: (y, 0, 0))
    return pl.pallas_call(
        pack_kernel,
        grid_spec=pltpu.PrefetchScalarGridSpec(
            num_scalar_prefetch=1,
            grid=(n_y,),
            in_specs=[
                pl.BlockSpec(block, lambda y, z: (0, 0, 2 * y + z[0])),
                pl.BlockSpec(block, lambda y, z: (0, 0, 2 * y + 1 - z[0])),
            ],
            out_specs=[out_spec, out_spec],
        ),
        out_shape=[shape, shape],
        compiler_params=pltpu.CompilerParams(vmem_limit_bytes=16 * 1024 * 1024),
        cost_estimate=pl.CostEstimate(flops=0, bytes_accessed=4 * rows.size, transcendentals=0),
    )(pair.reshape(1), rows, rows)


def image_kernel(q_ref, k_ref, v_ref, gain_ref, num_ref, den_ref, keys, values):
    @pl.when(pl.program_id(1) == 0)
    def _():
        k = k_ref[...].reshape(-1, HD).astype(F32)
        keys[...] = rms_scale(k, gain_ref[1:2, :]).astype(BF16)
        values[:, :HD] = v_ref[...].reshape(-1, HD)
        values[:, HD:] = jnp.ones((values.shape[0], HD), BF16)

    q = q_ref[...].reshape(-1, HD).astype(F32)
    q = rms_scale(q, gain_ref[0:1, :] * QUERY_SCALE).astype(BF16)
    weight = jnp.exp2(dot_t(q, keys[...])).astype(BF16)
    both = jnp.dot(weight, values[...], preferred_element_type=F32)
    num_ref[...] = both[:, :HD]
    den_ref[...] = both[:, HD:]


def image_attention(received, gains):
    sources, _, width = received.shape
    heads = width // HD
    image_len = sources * BLK
    step = 2
    rows = step * BLK
    return pl.pallas_call(
        image_kernel,
        grid=(heads, sources // step),
        in_specs=[
            pl.BlockSpec((step, BLK, HD), lambda h, b: (b, 0, h)),
            pl.BlockSpec((sources, BLK, HD), lambda h, b: (0, 1, h)),
            pl.BlockSpec((sources, BLK, HD), lambda h, b: (0, 2, h)),
            pl.BlockSpec((2, HD), lambda h, b: (0, 0)),
        ],
        out_specs=[
            pl.BlockSpec((rows, HD), lambda h, b: (b, h)),
            pl.BlockSpec((rows, HD), lambda h, b: (b, h)),
        ],
        out_shape=[jax.ShapeDtypeStruct((image_len, width), F32)] * 2,
        scratch_shapes=[pltpu.VMEM((image_len, HD), BF16), pltpu.VMEM((image_len, 2 * HD), BF16)],
        compiler_params=pltpu.CompilerParams(vmem_limit_bytes=24 * 1024 * 1024),
        cost_estimate=pl.CostEstimate(
            flops=6 * image_len * image_len * width,
            bytes_accessed=14 * image_len * width,
            transcendentals=heads * image_len * image_len,
        ),
    )(received, received, received, gains)


def text_kernel(length_ref, q_ref, k_ref, v_ref, gain_ref, text_gain_ref, num_ref, den_ref, out_ref):
    k = rms_scale(k_ref[...], text_gain_ref[...]).astype(BF16)
    v = v_ref[...].astype(BF16)
    q = q_ref[...].reshape(-1, HD).astype(F32)
    q = rms_scale(q, gain_ref[0:1, :] * QUERY_SCALE).astype(BF16)
    weight = jnp.exp2(dot_t(q, k))
    valid = lax.broadcasted_iota(jnp.int32, weight.shape, 1) < length_ref[0]
    weight = jnp.where(valid, weight, 0.0).astype(BF16)
    stacked = jnp.concatenate([v, jnp.ones_like(v)], axis=1)
    both = jnp.dot(weight, stacked, preferred_element_type=F32)
    total = num_ref[...] + both[:, :HD]
    out_ref[...] = (total / (den_ref[...] + both[:, HD:])).astype(BF16)


def text_attention(length, received, key_value, gains, text_gain, num, den):
    sources, _, width = received.shape
    heads = width // HD
    image_len = sources * BLK
    step = sources // 2
    rows = step * BLK
    return pl.pallas_call(
        text_kernel,
        grid=(heads, sources // step),
        in_specs=[
            pl.BlockSpec(memory_space=pltpu.SMEM),
            pl.BlockSpec((step, BLK, HD), lambda h, b: (b, 0, h)),
            pl.BlockSpec((BLK, HD), lambda h, b: (0, h)),
            pl.BlockSpec((BLK, HD), lambda h, b: (0, heads + h)),
            pl.BlockSpec((2, HD), lambda h, b: (0, 0)),
            pl.BlockSpec((1, HD), lambda h, b: (0, 0)),
            pl.BlockSpec((rows, HD), lambda h, b: (b, h)),
            pl.BlockSpec((rows, HD), lambda h, b: (b, h)),
        ],
        out_specs=pl.BlockSpec((rows, HD), lambda h, b: (b, h)),
        out_shape=jax.ShapeDtypeStruct((image_len, width), BF16),
        compiler_params=pltpu.CompilerParams(vmem_limit_bytes=24 * 1024 * 1024),
        cost_estimate=pl.CostEstimate(
            flops=6 * image_len * BLK * width,
            bytes_accessed=12 * image_len * width,
            transcendentals=heads * image_len * BLK,
        ),
    )(length, received, key_value, key_value, gains, text_gain, num, den)


def on_device(
    enc_states,
    lengths,
    prompt_owner_sample,
    t5_gain,
    t5_in_weight,
    t5_out_weight,
    t5_final_gain,
    context_weight,
    text_shift,
    text_scale,
    kv_weight,
    text_key_gain,
    image_query_key_value,
    image_qk_gain,
    proj_weight,
    dora_a,
    dora_b,
    magnitude,
    grad_out,
):
    seq_rank = lax.axis_index("seq")
    data_rank = lax.axis_index("dp")
    n_seq = lax.axis_size("seq")
    n_dp = lax.axis_size("dp")
    n_all = n_seq * n_dp
    both = ("dp", "seq")
    rank, own_cols = dora_b.shape
    own_rows = dora_a.shape[0]
    model = own_cols * n_dp
    lanes = 128
    rows_of = model // lanes
    cotangent = to_gathered(grad_out[0], n_dp)

    pair = seq_rank % 2
    flip_z = [(i, i ^ 1) for i in range(n_seq)]
    n_y = n_seq // 2

    weights = jnp.concatenate(
        [context_weight.T, kv_weight.reshape(kv_weight.shape[0], -1)], 1
    )
    near_weights = near_shard(weights)
    own_heads, other_heads = pack_heads(image_query_key_value[0].transpose(1, 0, 2), pair, n_seq)
    other_heads = lax.ppermute(other_heads, "seq", flip_z)
    direction_t = proj_weight.T.astype(F32) + lax.dot_general(
        dora_b, dora_a, (((0,), (1,)), ((), ())), precision=lax.Precision.HIGHEST
    )
    direction_t = direction_t.astype(BF16)
    rows_y = swap(jnp.broadcast_to(direction_t[None], (n_y, own_cols, own_rows)), "seq", Y_GROUPS)

    tokens = enc_states[0, :BLK]
    feat = tokens.shape[1] // n_seq
    normed = rms_scale(tokens.astype(F32), t5_gain).astype(BF16)
    gate_proj = jnp.dot(normed, t5_in_weight[0], preferred_element_type=F32)
    upward = jnp.dot(normed, t5_in_weight[1], preferred_element_type=F32)
    hidden = (jax.nn.gelu(gate_proj, approximate=True) * upward).astype(BF16)
    ffn = jnp.dot(hidden, t5_out_weight, preferred_element_type=F32).astype(BF16)
    ffn = ffn.reshape(BLK, n_seq, feat).transpose(1, 0, 2)
    rows_y, ffn, near_weights = lax.optimization_barrier((rows_y, ffn, near_weights))

    weights = gather_columns(weights, near_weights)
    depth = context_weight.shape[0]
    context_all, kv_all = weights[:, :depth], weights[:, depth:]

    rows_f = rows_y.astype(F32)
    column_sq = jnp.sum(rows_f * rows_f, (0, 2))
    column_sq = column_sq + lax.ppermute(column_sq, "seq", flip_z)
    ratio = magnitude / jnp.sqrt(column_sq + EPSILON)
    scaled_t = (rows_f * ratio[None, :, None]).astype(BF16)
    scaled_t = scaled_t.transpose(1, 0, 2).reshape(own_cols, -1)
    reach = scaled_t.shape[1]
    up = jnp.pad((dora_b * ratio).astype(BF16).T, ((0, 0), (0, lanes - rank)))
    scaled_t = jnp.concatenate([scaled_t, up], 1)
    near_scaled = near_shard(scaled_t)

    ffn = swap(ffn, "seq")
    ffn, near_scaled, other_heads = lax.optimization_barrier((ffn, near_scaled, other_heads))
    scaled_all = gather_columns(scaled_t, near_scaled)
    up_all = scaled_all[:, reach:]
    ffn_sum = jnp.sum(ffn.astype(F32), 0)

    received = swap(jnp.stack([own_heads, other_heads], 1), "seq", Y_GROUPS)
    received = received.reshape(n_seq, 3 * BLK, own_rows)

    own_tokens = lax.dynamic_slice_in_dim(tokens, seq_rank * feat, feat, 1).astype(F32)
    own_final = lax.dynamic_slice_in_dim(t5_final_gain, seq_rank * feat, feat, 0)
    encoded = ((own_tokens + ffn_sum) * own_final).astype(BF16)
    context = dot_t(encoded, context_all).astype(BF16).reshape(BLK, rows_of, lanes)
    context, received = lax.optimization_barrier((context, received))
    arrived = swap(context, both)
    token_of = jnp.sum(arrived.reshape(n_dp, n_seq, rows_of, lanes).astype(F32), 1).astype(BF16)
    values = token_of.astype(F32)
    centre = jnp.mean(values, (1, 2), keepdims=True)
    spread = jnp.mean((values - centre) * (values - centre), (1, 2), keepdims=True)
    layer_normed = ((values - centre) * lax.rsqrt(spread + EPSILON)).astype(BF16)
    target = jnp.arange(n_all, dtype=jnp.int32) // n_seq
    one_hot = (target[:, None] == prompt_owner_sample[None, :]).astype(BF16)
    outgoing = jnp.einsum("sp,pab->sab", one_hot, layer_normed, preferred_element_type=F32)
    text = swap(outgoing.astype(BF16), both).reshape(BLK, model)
    scale, shift = to_gathered(text_scale, n_dp), to_gathered(text_shift, n_dp)
    modulated = ((1.0 + scale) * text.astype(F32) + shift).astype(BF16)
    length = jnp.sum(jnp.where(prompt_owner_sample == data_rank, lengths, 0))
    key_value = jnp.dot(modulated, kv_all, preferred_element_type=F32)

    num, den = image_attention(received, image_qk_gain)
    attended = text_attention(
        length.reshape(1), received, key_value, image_qk_gain, text_key_gain.reshape(1, HD), num, den
    )

    lowered = jnp.dot(attended, dora_a.astype(BF16), preferred_element_type=F32).astype(BF16)
    outgoing = jnp.concatenate([attended, lowered], 1).reshape(n_y, 2 * BLK, own_rows + rank)
    gathered = swap(outgoing, "seq", Y_GROUPS)
    down = jnp.dot(cotangent, up_all, preferred_element_type=F32).astype(BF16)
    down = jnp.concatenate([down, lax.ppermute(down, "seq", flip_z)], 0)
    gathered, down = lax.optimization_barrier((gathered, down))
    down_all = swap(jnp.broadcast_to(down[None], (n_y,) + down.shape), "seq", Y_GROUPS)
    lowered = jnp.sum(gathered[:, :, own_rows:].astype(F32), 0)
    lowered_other = lax.ppermute(lowered[BLK:].astype(BF16), "seq", flip_z)
    gathered = gathered[:, :, :own_rows].transpose(1, 0, 2).reshape(2 * BLK, -1)
    landed = []
    for at in range(0, model, model // 2):
        part = dot_t(gathered[BLK:], scaled_all[at : at + model // 2, :reach]).astype(BF16)
        landed.append(lax.ppermute(part, "seq", flip_z))
    kept = lax.optimization_barrier(dot_t(gathered[:BLK], scaled_all[:, :reach]))
    out = kept + jnp.concatenate(landed, 1).astype(F32)
    image_out = from_gathered(out.astype(BF16), n_dp)[None]
    lowered = (lowered[:BLK] + lowered_other.astype(F32)).astype(BF16)

    down_all = down_all.reshape(-1, lanes)[:, :rank]
    grad_a = lax.dot_general(
        down_all, attended, (((0,), (0,)), ((), ())), preferred_element_type=F32
    )
    for bit in (1, 2, 4, 8):
        grad_a = grad_a.astype(BF16)
        moved = lax.ppermute(grad_a, "dp", [(i, i ^ bit) for i in range(n_dp)])
        grad_a = grad_a.astype(F32) + moved.astype(F32)
    grad_a = grad_a.T
    up_part = lax.dot_general(
        lowered, cotangent, (((0,), (0,)), ((), ())), preferred_element_type=F32
    ).astype(BF16)
    magnitude_part = jnp.sum(out * cotangent.astype(F32), 0).astype(BF16)
    parts = jnp.concatenate([up_part, jnp.pad(magnitude_part[None], ((0, 7), (0, 0)))], 0)
    parts = parts.reshape(rank + 8, n_dp // 2, 2, own_cols).transpose(2, 1, 0, 3)
    parts = parts.reshape(n_dp, rank + 8, own_cols)
    parts = jnp.sum(swap(parts, "dp").astype(F32), 0).astype(BF16)
    parts = swap(jnp.broadcast_to(parts[None], (n_seq,) + parts.shape), "seq")
    parts = jnp.sum(parts.astype(F32), 0)
    grad_b = parts[:rank] * ratio
    grad_magnitude = parts[rank] / magnitude
    return (image_out, grad_a, grad_b, grad_magnitude)


def solution(mesh):
    return jax.shard_map(
        on_device,
        mesh=mesh,
        in_specs=(
            P("dp", None, None),
            P(),
            P(),
            P(),
            P(None, None, "seq"),
            P("seq", None),
            P(),
            P("seq", "dp"),
            P("dp", None),
            P("dp", None),
            P("dp", None, "seq"),
            P(),
            P("dp", "seq", None, None),
            P(),
            P("seq", "dp"),
            P("seq", None),
            P(None, "dp"),
            P("dp"),
            P("dp", "seq", None),
        ),
        out_specs=(P("dp", "seq", None), P("seq", None), P(None, "dp"), P("dp")),
        check_vma=False,
    )
```

```python
import math

import jax
import jax.numpy as jnp
from jax import lax
from jax.experimental import pallas as pl
from jax.experimental.pallas import tpu as pltpu
from jax.sharding import PartitionSpec as P

HD = 128
BLK = 128
EPSILON = 1e-06
F32 = jnp.float32
BF16 = jnp.bfloat16
Y_GROUPS = [[0, 2, 4, 6], [1, 3, 5, 7]]
QUERY_SCALE = math.log2(math.e) / math.sqrt(HD)


def rms_scale(values, gain):
    return values * lax.rsqrt(jnp.mean(values * values, -1, keepdims=True) + EPSILON) * gain


def swap(values, axes, groups=None):
    return lax.all_to_all(values, axes, 0, 0, tiled=True, axis_index_groups=groups)


def near_shard(values):
    n_dp = lax.axis_size("dp")
    return lax.ppermute(values, "dp", [(i, (i + n_dp // 2) % n_dp) for i in range(n_dp)])


def gather_columns(values, other):
    n_dp = lax.axis_size("dp")
    near = n_dp // 2
    low = lax.axis_index("dp") < near
    halves = jnp.stack([jnp.where(low, values, other), jnp.where(low, other, values)])
    groups = [list(range(near)), list(range(near, n_dp))]
    gathered = lax.all_gather(halves, "dp", axis=0, axis_index_groups=groups)
    return gathered.reshape(n_dp * values.shape[0], values.shape[1])


def to_gathered(values, n_dp):
    rows = values.shape[0]
    cut = values.reshape(rows, 2, n_dp // 2, -1)
    return cut.transpose(0, 2, 1, 3).reshape(rows, -1)


def from_gathered(values, n_dp):
    rows = values.shape[0]
    cut = values.reshape(rows, n_dp // 2, 2, -1)
    return cut.transpose(0, 2, 1, 3).reshape(rows, -1)


def dot_t(left, right):
    return lax.dot_general(left, right, (((1,), (1,)), ((), ())), preferred_element_type=F32)


def pack_kernel(_, own_in, other_in, own_ref, other_ref):
    own_ref[0] = own_in[...].reshape(own_ref.shape[1:])
    other_ref[0] = other_in[...].reshape(other_ref.shape[1:])


def pack_heads(rows, pair, n_seq):
    kinds, count, model = rows.shape
    width = model // n_seq
    n_y = n_seq // 2
    block = (kinds, count, width)
    shape = jax.ShapeDtypeStruct((n_y, kinds * count, width), rows.dtype)
    out_spec = pl.BlockSpec((1, kinds * count, width), lambda y, z: (y, 0, 0))
    return pl.pallas_call(
        pack_kernel,
        grid_spec=pltpu.PrefetchScalarGridSpec(
            num_scalar_prefetch=1,
            grid=(n_y,),
            in_specs=[
                pl.BlockSpec(block, lambda y, z: (0, 0, 2 * y + z[0])),
                pl.BlockSpec(block, lambda y, z: (0, 0, 2 * y + 1 - z[0])),
            ],
            out_specs=[out_spec, out_spec],
        ),
        out_shape=[shape, shape],
        compiler_params=pltpu.CompilerParams(vmem_limit_bytes=16 * 1024 * 1024),
        cost_estimate=pl.CostEstimate(flops=0, bytes_accessed=4 * rows.size, transcendentals=0),
    )(pair.reshape(1), rows, rows)


def image_kernel(q_ref, k_ref, v_ref, gain_ref, num_ref, den_ref, keys, values):
    @pl.when(pl.program_id(1) == 0)
    def _():
        k = k_ref[...].reshape(-1, HD).astype(F32)
        keys[...] = rms_scale(k, gain_ref[1:2, :]).astype(BF16)
        values[:, :HD] = v_ref[...].reshape(-1, HD)
        values[:, HD:] = jnp.ones((values.shape[0], HD), BF16)

    q = q_ref[...].reshape(-1, HD).astype(F32)
    q = rms_scale(q, gain_ref[0:1, :] * QUERY_SCALE).astype(BF16)
    weight = jnp.exp2(dot_t(q, keys[...])).astype(BF16)
    both = jnp.dot(weight, values[...], preferred_element_type=F32)
    num_ref[...] = both[:, :HD]
    den_ref[...] = both[:, HD:]


def image_attention(received, gains):
    sources, _, width = received.shape
    heads = width // HD
    image_len = sources * BLK
    step = 2
    rows = step * BLK
    return pl.pallas_call(
        image_kernel,
        grid=(heads, sources // step),
        in_specs=[
            pl.BlockSpec((step, BLK, HD), lambda h, b: (b, 0, h)),
            pl.BlockSpec((sources, BLK, HD), lambda h, b: (0, 1, h)),
            pl.BlockSpec((sources, BLK, HD), lambda h, b: (0, 2, h)),
            pl.BlockSpec((2, HD), lambda h, b: (0, 0)),
        ],
        out_specs=[
            pl.BlockSpec((rows, HD), lambda h, b: (b, h)),
            pl.BlockSpec((rows, HD), lambda h, b: (b, h)),
        ],
        out_shape=[jax.ShapeDtypeStruct((image_len, width), F32)] * 2,
        scratch_shapes=[pltpu.VMEM((image_len, HD), BF16), pltpu.VMEM((image_len, 2 * HD), BF16)],
        compiler_params=pltpu.CompilerParams(vmem_limit_bytes=24 * 1024 * 1024),
        cost_estimate=pl.CostEstimate(
            flops=6 * image_len * image_len * width,
            bytes_accessed=14 * image_len * width,
            transcendentals=heads * image_len * image_len,
        ),
    )(received, received, received, gains)


def prompt_kernel(
    length_ref,
    q_ref,
    text_ref,
    k_weight,
    v_weight,
    down_ref,
    gain_ref,
    text_gain_ref,
    num_ref,
    den_ref,
    out_ref,
    lowered,
):
    head = pl.program_id(0)
    heads = pl.num_programs(0) - 1

    @pl.when(head == 0)
    def _():
        lowered[...] = jnp.zeros_like(lowered)

    @pl.when(head < heads)
    def _():
        text = text_ref[...]
        k = jnp.dot(text, k_weight[...], preferred_element_type=F32)
        k = rms_scale(k, text_gain_ref[...]).astype(BF16)
        v = jnp.dot(text, v_weight[...], preferred_element_type=F32).astype(BF16)
        stacked = jnp.concatenate([v, jnp.ones_like(v)], axis=1)
        groups, rows, _ = out_ref.shape
        for b in range(groups):
            q = q_ref[2 * b : 2 * b + 2].reshape(rows, HD).astype(F32)
            q = rms_scale(q, gain_ref[0:1, :] * QUERY_SCALE).astype(BF16)
            weight = jnp.exp2(dot_t(q, k))
            valid = lax.broadcasted_iota(jnp.int32, weight.shape, 1) < length_ref[0]
            weight = jnp.where(valid, weight, 0.0).astype(BF16)
            both = jnp.dot(weight, stacked, preferred_element_type=F32)
            at = slice(b * rows, (b + 1) * rows)
            total = num_ref[at, :] + both[:, :HD]
            attended = (total / (den_ref[at, :] + both[:, HD:])).astype(BF16)
            out_ref[b] = attended
            lowered[at, :] += jnp.dot(attended, down_ref[...], preferred_element_type=F32)

    @pl.when(head == heads)
    def _():
        out_ref[...] = lowered[...].reshape(out_ref.shape).astype(BF16)


def prompt_attention(length, received, text, weights, first, down, gains, text_gain, num, den):
    sources, _, width = received.shape
    heads = width // HD
    image_len = sources * BLK
    model = text.shape[1]
    groups = sources // 2

    def last(h):
        return jnp.minimum(h, heads - 1)

    return pl.pallas_call(
        prompt_kernel,
        grid=(heads + 1,),
        in_specs=[
            pl.BlockSpec(memory_space=pltpu.SMEM),
            pl.BlockSpec((sources, BLK, HD), lambda h: (0, 0, last(h))),
            pl.BlockSpec((BLK, model), lambda h: (0, 0)),
            pl.BlockSpec((model, HD), lambda h: (0, first + last(h))),
            pl.BlockSpec((model, HD), lambda h: (0, first + heads + last(h))),
            pl.BlockSpec((HD, down.shape[1]), lambda h: (last(h), 0)),
            pl.BlockSpec((2, HD), lambda h: (0, 0)),
            pl.BlockSpec((1, HD), lambda h: (0, 0)),
            pl.BlockSpec((image_len, HD), lambda h: (0, last(h))),
            pl.BlockSpec((image_len, HD), lambda h: (0, last(h))),
        ],
        out_specs=pl.BlockSpec((groups, 2 * BLK, HD), lambda h: (0, 0, h)),
        out_shape=jax.ShapeDtypeStruct((groups, 2 * BLK, width + HD), BF16),
        scratch_shapes=[pltpu.VMEM((image_len, HD), F32)],
        compiler_params=pltpu.CompilerParams(vmem_limit_bytes=24 * 1024 * 1024),
        cost_estimate=pl.CostEstimate(
            flops=6 * image_len * BLK * width + 4 * BLK * model * width,
            bytes_accessed=12 * image_len * width + 4 * model * width,
            transcendentals=heads * image_len * BLK,
        ),
    )(length, received, text, weights, weights, down, gains, text_gain, num, den)


def t5_kernel(x_ref, gain_ref, gate_w, up_w, out_w, out_ref, normed, hidden):
    step = pl.program_id(0)
    cuts = hidden.shape[0]

    @pl.when(step == 0)
    def _():
        normed[...] = rms_scale(x_ref[0].astype(F32), gain_ref[...]).astype(BF16)

    @pl.when(step < cuts)
    def _():
        gate = jnp.dot(normed[...], gate_w[0], preferred_element_type=F32)
        upward = jnp.dot(normed[...], up_w[0], preferred_element_type=F32)
        hidden[step] = (jax.nn.gelu(gate, approximate=True) * upward).astype(BF16)

    @pl.when(step >= cuts)
    def _():
        joined = jnp.concatenate([hidden[c] for c in range(cuts)], 1)
        total = jnp.dot(joined, out_w[...], preferred_element_type=F32)
        out_ref[0] = total.astype(BF16)


def t5_ffn(states, gain, in_weight, out_weight, n_seq):
    _, features, units = in_weight.shape
    cut = 128
    cuts = units // cut
    feat = features // n_seq

    def unit(i):
        return jnp.minimum(i, cuts - 1)

    def share(i):
        return jnp.maximum(i - cuts, 0)

    return pl.pallas_call(
        t5_kernel,
        grid=(cuts + n_seq,),
        in_specs=[
            pl.BlockSpec((1, BLK, features), lambda i: (0, 0, 0)),
            pl.BlockSpec((1, features), lambda i: (0, 0)),
            pl.BlockSpec((1, features, cut), lambda i: (0, 0, unit(i))),
            pl.BlockSpec((1, features, cut), lambda i: (1, 0, unit(i))),
            pl.BlockSpec((units, feat), lambda i: (0, share(i))),
        ],
        out_specs=pl.BlockSpec((1, BLK, feat), lambda i: (share(i), 0, 0)),
        out_shape=jax.ShapeDtypeStruct((n_seq, BLK, feat), BF16),
        scratch_shapes=[pltpu.VMEM((BLK, features), BF16), pltpu.VMEM((cuts, BLK, cut), BF16)],
        compiler_params=pltpu.CompilerParams(vmem_limit_bytes=24 * 1024 * 1024),
        cost_estimate=pl.CostEstimate(
            flops=6 * BLK * features * units,
            bytes_accessed=6 * features * units,
            transcendentals=BLK * units,
        ),
    )(states, gain.reshape(1, features), in_weight, in_weight, out_weight)


def on_device(
    enc_states,
    lengths,
    prompt_owner_sample,
    t5_gain,
    t5_in_weight,
    t5_out_weight,
    t5_final_gain,
    context_weight,
    text_shift,
    text_scale,
    kv_weight,
    text_key_gain,
    image_query_key_value,
    image_qk_gain,
    proj_weight,
    dora_a,
    dora_b,
    magnitude,
    grad_out,
):
    seq_rank = lax.axis_index("seq")
    data_rank = lax.axis_index("dp")
    n_seq = lax.axis_size("seq")
    n_dp = lax.axis_size("dp")
    n_all = n_seq * n_dp
    both = ("dp", "seq")
    rank, own_cols = dora_b.shape
    own_rows = dora_a.shape[0]
    model = own_cols * n_dp
    lanes = 128
    rows_of = model // lanes
    cotangent = to_gathered(grad_out[0], n_dp)

    pair = seq_rank % 2
    flip_z = [(i, i ^ 1) for i in range(n_seq)]
    n_y = n_seq // 2

    weights = jnp.concatenate(
        [context_weight.T, kv_weight.reshape(kv_weight.shape[0], -1)], 1
    )
    near_weights = near_shard(weights)
    own_heads, other_heads = pack_heads(image_query_key_value[0].transpose(1, 0, 2), pair, n_seq)
    t5_gain, other_heads = lax.optimization_barrier((t5_gain, other_heads))
    other_heads = lax.ppermute(other_heads, "seq", flip_z)
    direction_t = proj_weight.T.astype(F32) + lax.dot_general(
        dora_b, dora_a, (((0,), (1,)), ((), ())), precision=lax.Precision.HIGHEST
    )
    direction_t = direction_t.astype(BF16)
    rows_y = swap(jnp.broadcast_to(direction_t[None], (n_y, own_cols, own_rows)), "seq", Y_GROUPS)

    tokens = enc_states[0, :BLK]
    feat = tokens.shape[1] // n_seq
    ffn = t5_ffn(enc_states, t5_gain, t5_in_weight, t5_out_weight, n_seq)
    rows_y, ffn, near_weights = lax.optimization_barrier((rows_y, ffn, near_weights))

    weights = gather_columns(weights, near_weights)
    depth = context_weight.shape[0]
    context_all = weights[:, :depth]

    rows_f = rows_y.astype(F32)
    column_sq = jnp.sum(rows_f * rows_f, (0, 2))
    column_sq = column_sq + lax.ppermute(column_sq, "seq", flip_z)
    ratio = magnitude / jnp.sqrt(column_sq + EPSILON)
    scaled_t = (rows_f * ratio[None, :, None]).astype(BF16)
    scaled_t = scaled_t.transpose(1, 0, 2).reshape(own_cols, -1)
    reach = scaled_t.shape[1]
    up = jnp.pad((dora_b * ratio).astype(BF16).T, ((0, 0), (0, lanes - rank)))
    scaled_t = jnp.concatenate([scaled_t, up], 1)
    near_scaled = near_shard(scaled_t)

    ffn = swap(ffn, "seq")
    ffn, near_scaled, other_heads = lax.optimization_barrier((ffn, near_scaled, other_heads))
    scaled_all = gather_columns(scaled_t, near_scaled)
    up_all = scaled_all[:, reach:]
    ffn_sum = jnp.sum(ffn.astype(F32), 0)

    received = swap(jnp.stack([own_heads, other_heads], 1), "seq", Y_GROUPS)
    received = received.reshape(n_seq, 3 * BLK, own_rows)

    own_tokens = lax.dynamic_slice_in_dim(tokens, seq_rank * feat, feat, 1).astype(F32)
    own_final = lax.dynamic_slice_in_dim(t5_final_gain, seq_rank * feat, feat, 0)
    encoded = ((own_tokens + ffn_sum) * own_final).astype(BF16)
    context = dot_t(encoded, context_all).astype(BF16).reshape(BLK, rows_of, lanes)
    context, received = lax.optimization_barrier((context, received))
    arrived = swap(context, both)
    token_of = jnp.sum(arrived.reshape(n_dp, n_seq, rows_of, lanes).astype(F32), 1).astype(BF16)
    values = token_of.astype(F32)
    centre = jnp.mean(values, (1, 2), keepdims=True)
    spread = jnp.mean((values - centre) * (values - centre), (1, 2), keepdims=True)
    layer_normed = ((values - centre) * lax.rsqrt(spread + EPSILON)).astype(BF16)
    target = jnp.arange(n_all, dtype=jnp.int32) // n_seq
    one_hot = (target[:, None] == prompt_owner_sample[None, :]).astype(BF16)
    outgoing = jnp.einsum("sp,pab->sab", one_hot, layer_normed, preferred_element_type=F32)
    text = swap(outgoing.astype(BF16), both).reshape(BLK, model)
    scale, shift = to_gathered(text_scale, n_dp), to_gathered(text_shift, n_dp)
    modulated = ((1.0 + scale) * text.astype(F32) + shift).astype(BF16)
    length = jnp.sum(jnp.where(prompt_owner_sample == data_rank, lengths, 0))

    num, den = image_attention(received, image_qk_gain)
    down_factor = jnp.pad(dora_a.astype(BF16), ((0, 0), (0, lanes - rank)))
    attended = prompt_attention(
        length.reshape(1),
        received,
        modulated,
        weights,
        depth // HD,
        down_factor,
        image_qk_gain,
        text_key_gain.reshape(1, HD),
        num,
        den,
    )

    gathered = swap(attended, "seq", Y_GROUPS)
    down = jnp.dot(cotangent, up_all, preferred_element_type=F32).astype(BF16)
    down = jnp.concatenate([down, lax.ppermute(down, "seq", flip_z)], 0)
    gathered, down = lax.optimization_barrier((gathered, down))
    lowered = jnp.sum(gathered[:, :, own_rows:].astype(F32), 0)
    lowered_other = lax.ppermute(lowered[BLK:].astype(BF16), "seq", flip_z)
    gathered = gathered[:, :, :own_rows].transpose(1, 0, 2).reshape(2 * BLK, -1)
    kept_rows = gathered[:BLK]
    landed = []
    for at in range(0, model, model // 2):
        part = dot_t(gathered[BLK:], scaled_all[at : at + model // 2, :reach]).astype(BF16)
        kept_rows, part = lax.optimization_barrier((kept_rows, part))
        landed.append(lax.ppermute(part, "seq", flip_z))

    lowered = (lowered[:BLK] + lowered_other.astype(F32)).astype(BF16)[:, :rank]
    up_part = lax.dot_general(
        lowered, cotangent, (((0,), (0,)), ((), ())), preferred_element_type=F32
    ).astype(BF16)
    up_part = up_part.reshape(rank, n_dp // 2, 2, own_cols).transpose(2, 1, 0, 3)
    up_part = swap(up_part.reshape(n_dp, rank, own_cols), "dp")

    for bit in (2, 4):
        moved = lax.ppermute(down, "seq", [(i, i ^ bit) for i in range(n_seq)])
        first = (seq_rank & bit) == 0
        down = jnp.concatenate([jnp.where(first, down, moved), jnp.where(first, moved, down)], 0)
    rows_all = attended.reshape(-1, own_rows + lanes)[:, :own_rows]
    grad_a = lax.dot_general(
        down[:, :rank], rows_all, (((0,), (0,)), ((), ())), preferred_element_type=F32
    )
    for bit in (1, 2, 4):
        grad_a = grad_a.astype(BF16)
        moved = lax.ppermute(grad_a, "dp", [(i, i ^ bit) for i in range(n_dp)])
        grad_a = grad_a.astype(F32) + moved.astype(F32)
    grad_a = grad_a.astype(BF16)

    kept = dot_t(kept_rows, scaled_all[:, :reach])
    kept, up_part, grad_a = lax.optimization_barrier((kept, up_part, grad_a))
    out = kept + jnp.concatenate(landed, 1).astype(F32)
    image_out = from_gathered(out.astype(BF16), n_dp)[None]
    magnitude_part = jnp.sum(out * cotangent.astype(F32), 0).astype(BF16)
    magnitude_part = magnitude_part.reshape(n_dp // 2, 2, own_cols).transpose(1, 0, 2)
    magnitude_part = jnp.broadcast_to(
        magnitude_part.reshape(n_dp, 1, own_cols), (n_dp, n_seq, own_cols)
    )
    magnitude_part = swap(magnitude_part.reshape(n_all, own_cols), both)
    grad_magnitude = jnp.sum(magnitude_part.astype(F32), 0) / magnitude

    moved = lax.ppermute(grad_a, "dp", [(i, i ^ 8) for i in range(n_dp)])
    grad_a = (grad_a.astype(F32) + moved.astype(F32)).T
    grad_b = jnp.sum(up_part.astype(F32), 0)
    for bit in (2, 4, 1):
        grad_b = grad_b.astype(BF16)
        moved = lax.ppermute(grad_b, "seq", [(i, i ^ bit) for i in range(n_seq)])
        grad_b = grad_b.astype(F32) + moved.astype(F32)
    grad_b = grad_b * ratio
    return (image_out, grad_a, grad_b, grad_magnitude)


def solution(mesh):
    return jax.shard_map(
        on_device,
        mesh=mesh,
        in_specs=(
            P("dp", None, None),
            P(),
            P(),
            P(),
            P(None, None, "seq"),
            P("seq", None),
            P(),
            P("seq", "dp"),
            P("dp", None),
            P("dp", None),
            P("dp", None, "seq"),
            P(),
            P("dp", "seq", None, None),
            P(),
            P("seq", "dp"),
            P("seq", None),
            P(None, "dp"),
            P("dp"),
            P("dp", "seq", None),
        ),
        out_specs=(P("dp", "seq", None), P("seq", None), P(None, "dp"), P("dp")),
        check_vma=False,
    )
```

```python
import math

import jax
import jax.numpy as jnp
from jax import lax
from jax.experimental import pallas as pl
from jax.experimental.pallas import tpu as pltpu
from jax.sharding import PartitionSpec as P

HD = 128
BLK = 128
EPSILON = 1e-06
VMEM_LIMIT = 56 * 1024 * 1024
F32 = jnp.float32
BF16 = jnp.bfloat16
Y_GROUPS = [[0, 2, 4, 6], [1, 3, 5, 7]]
QUERY_SCALE = math.log2(math.e) / math.sqrt(HD)


def rms_scale(values, gain):
    return values * lax.rsqrt(jnp.mean(values * values, -1, keepdims=True) + EPSILON) * gain


def swap(values, axes, groups=None):
    return lax.all_to_all(values, axes, 0, 0, tiled=True, axis_index_groups=groups)


def near_shard(values):
    n_dp = lax.axis_size("dp")
    return lax.ppermute(values, "dp", [(i, (i + n_dp // 2) % n_dp) for i in range(n_dp)])


def gather_columns(values, other):
    n_dp = lax.axis_size("dp")
    near = n_dp // 2
    low = lax.axis_index("dp") < near
    halves = jnp.stack([jnp.where(low, values, other), jnp.where(low, other, values)])
    groups = [list(range(near)), list(range(near, n_dp))]
    gathered = lax.all_gather(halves, "dp", axis=0, axis_index_groups=groups)
    return gathered.reshape(n_dp * values.shape[0], values.shape[1])


def to_gathered(values, n_dp):
    rows = values.shape[0]
    cut = values.reshape(rows, 2, n_dp // 2, -1)
    return cut.transpose(0, 2, 1, 3).reshape(rows, -1)


def from_gathered(values, n_dp):
    rows = values.shape[0]
    cut = values.reshape(rows, n_dp // 2, 2, -1)
    return cut.transpose(0, 2, 1, 3).reshape(rows, -1)


def dot_t(left, right):
    return lax.dot_general(left, right, (((1,), (1,)), ((), ())), preferred_element_type=F32)


def pack_kernel(_, own_in, other_in, own_ref, first_ref, second_ref):
    own_ref[0] = own_in[...].reshape(own_ref.shape[1:])
    other = other_in[...].reshape(own_ref.shape[1:])
    half = first_ref.shape[1]
    first_ref[0] = other[:half]
    second_ref[0] = other[half:]


def pack_heads(rows, pair, n_seq):
    kinds, count, model = rows.shape
    width = model // n_seq
    n_y = n_seq // 2
    block = (kinds, count, width)
    total = kinds * count

    def spec(size):
        return pl.BlockSpec((1, size, width), lambda y, z: (y, 0, 0))

    def shape(size):
        return jax.ShapeDtypeStruct((n_y, size, width), rows.dtype)

    return pl.pallas_call(
        pack_kernel,
        grid_spec=pltpu.PrefetchScalarGridSpec(
            num_scalar_prefetch=1,
            grid=(n_y,),
            in_specs=[
                pl.BlockSpec(block, lambda y, z: (0, 0, 2 * y + z[0])),
                pl.BlockSpec(block, lambda y, z: (0, 0, 2 * y + 1 - z[0])),
            ],
            out_specs=[spec(total), spec(total // 2), spec(total // 2)],
        ),
        out_shape=[shape(total), shape(total // 2), shape(total // 2)],
        compiler_params=pltpu.CompilerParams(vmem_limit_bytes=VMEM_LIMIT),
        cost_estimate=pl.CostEstimate(flops=0, bytes_accessed=4 * rows.size, transcendentals=0),
    )(pair.reshape(1), rows, rows)


def image_kernel(
    q_own, q_other, k_own, k_other, v_own, v_other, gain_ref, num_ref, den_ref, keys, values
):
    half = keys.shape[0] // 2

    @pl.when(pl.program_id(1) == 0)
    def _():
        for at, k_ref, v_ref in ((0, k_own, v_own), (half, k_other, v_other)):
            k = k_ref[...].reshape(-1, HD).astype(F32)
            keys[at : at + half, :] = rms_scale(k, gain_ref[1:2, :]).astype(BF16)
            values[at : at + half, :HD] = v_ref[...].reshape(-1, HD)
        values[:, HD:] = jnp.ones((2 * half, HD), BF16)

    q = jnp.concatenate([q_own[0], q_other[0]], 0).astype(F32)
    q = rms_scale(q, gain_ref[0:1, :] * QUERY_SCALE).astype(BF16)
    weight = jnp.exp2(dot_t(q, keys[...])).astype(BF16)
    both = jnp.dot(weight, values[...], preferred_element_type=F32)
    num_ref[...] = both[:, :HD]
    den_ref[...] = both[:, HD:]


def image_attention(own, other, gains):
    n_y, _, width = own.shape
    heads = width // HD
    rows = 2 * BLK
    image_len = n_y * rows

    def queries():
        return pl.BlockSpec((1, BLK, HD), lambda h, b: (b, 0, h))

    def whole(kind):
        return pl.BlockSpec((n_y, BLK, HD), lambda h, b: (0, kind, h))

    return pl.pallas_call(
        image_kernel,
        grid=(heads, n_y),
        in_specs=[
            queries(),
            queries(),
            whole(1),
            whole(1),
            whole(2),
            whole(2),
            pl.BlockSpec((2, HD), lambda h, b: (0, 0)),
        ],
        out_specs=[
            pl.BlockSpec((rows, HD), lambda h, b: (b, h)),
            pl.BlockSpec((rows, HD), lambda h, b: (b, h)),
        ],
        out_shape=[jax.ShapeDtypeStruct((image_len, width), F32)] * 2,
        scratch_shapes=[pltpu.VMEM((image_len, HD), BF16), pltpu.VMEM((image_len, 2 * HD), BF16)],
        compiler_params=pltpu.CompilerParams(vmem_limit_bytes=VMEM_LIMIT),
        cost_estimate=pl.CostEstimate(
            flops=6 * image_len * image_len * width,
            bytes_accessed=14 * image_len * width,
            transcendentals=heads * image_len * image_len,
        ),
    )(own, other, own, other, own, other, gains)


def prompt_kernel(
    length_ref,
    q_own,
    q_other,
    text_ref,
    k_weight,
    v_weight,
    down_ref,
    gain_ref,
    text_gain_ref,
    num_ref,
    den_ref,
    out_ref,
    lowered,
):
    head = pl.program_id(0)
    heads = pl.num_programs(0) - 1

    @pl.when(head == 0)
    def _():
        lowered[...] = jnp.zeros_like(lowered)

    @pl.when(head < heads)
    def _():
        text = text_ref[...]
        k = jnp.dot(text, k_weight[...], preferred_element_type=F32)
        k = rms_scale(k, text_gain_ref[...]).astype(BF16)
        v = jnp.dot(text, v_weight[...], preferred_element_type=F32).astype(BF16)
        stacked = jnp.concatenate([v, jnp.ones_like(v)], axis=1)
        groups, rows, _ = out_ref.shape
        for b in range(groups):
            q = jnp.concatenate([q_own[b], q_other[b]], 0).astype(F32)
            q = rms_scale(q, gain_ref[0:1, :] * QUERY_SCALE).astype(BF16)
            weight = jnp.exp2(dot_t(q, k))
            valid = lax.broadcasted_iota(jnp.int32, weight.shape, 1) < length_ref[0]
            weight = jnp.where(valid, weight, 0.0).astype(BF16)
            both = jnp.dot(weight, stacked, preferred_element_type=F32)
            at = slice(b * rows, (b + 1) * rows)
            total = num_ref[at, :] + both[:, :HD]
            attended = (total / (den_ref[at, :] + both[:, HD:])).astype(BF16)
            out_ref[b] = attended
            lowered[at, :] += jnp.dot(attended, down_ref[...], preferred_element_type=F32)

    @pl.when(head == heads)
    def _():
        out_ref[...] = lowered[...].reshape(out_ref.shape).astype(BF16)


def prompt_attention(length, own, other, text, weights, first, down, gains, text_gain, num, den):
    groups, _, width = own.shape
    heads = width // HD
    image_len = groups * 2 * BLK
    model = text.shape[1]

    def last(h):
        return jnp.minimum(h, heads - 1)

    return pl.pallas_call(
        prompt_kernel,
        grid=(heads + 1,),
        in_specs=[
            pl.BlockSpec(memory_space=pltpu.SMEM),
            pl.BlockSpec((groups, BLK, HD), lambda h: (0, 0, last(h))),
            pl.BlockSpec((groups, BLK, HD), lambda h: (0, 0, last(h))),
            pl.BlockSpec((BLK, model), lambda h: (0, 0)),
            pl.BlockSpec((model, HD), lambda h: (0, first + last(h))),
            pl.BlockSpec((model, HD), lambda h: (0, first + heads + last(h))),
            pl.BlockSpec((HD, down.shape[1]), lambda h: (last(h), 0)),
            pl.BlockSpec((2, HD), lambda h: (0, 0)),
            pl.BlockSpec((1, HD), lambda h: (0, 0)),
            pl.BlockSpec((image_len, HD), lambda h: (0, last(h))),
            pl.BlockSpec((image_len, HD), lambda h: (0, last(h))),
        ],
        out_specs=pl.BlockSpec((groups, 2 * BLK, HD), lambda h: (0, 0, h)),
        out_shape=jax.ShapeDtypeStruct((groups, 2 * BLK, width + HD), BF16),
        scratch_shapes=[pltpu.VMEM((image_len, HD), F32)],
        compiler_params=pltpu.CompilerParams(vmem_limit_bytes=VMEM_LIMIT),
        cost_estimate=pl.CostEstimate(
            flops=6 * image_len * BLK * width + 4 * BLK * model * width,
            bytes_accessed=12 * image_len * width + 4 * model * width,
            transcendentals=heads * image_len * BLK,
        ),
    )(length, own, other, text, weights, weights, down, gains, text_gain, num, den)


def t5_in_kernel(x_ref, gain_ref, gate_w, up_w, out_ref, normed):
    @pl.when(pl.program_id(0) == 0)
    def _():
        normed[...] = rms_scale(x_ref[0].astype(F32), gain_ref[...]).astype(BF16)

    gate = jnp.dot(normed[...], gate_w[0], preferred_element_type=F32)
    upward = jnp.dot(normed[...], up_w[0], preferred_element_type=F32)
    out_ref[...] = (jax.nn.gelu(gate, approximate=True) * upward).astype(BF16)


def t5_in(states, gain, in_weight):
    _, features, units = in_weight.shape
    cut = 128
    return pl.pallas_call(
        t5_in_kernel,
        grid=(units // cut,),
        in_specs=[
            pl.BlockSpec((1, BLK, features), lambda i: (0, 0, 0)),
            pl.BlockSpec((1, features), lambda i: (0, 0)),
            pl.BlockSpec((1, features, cut), lambda i: (0, 0, i)),
            pl.BlockSpec((1, features, cut), lambda i: (1, 0, i)),
        ],
        out_specs=pl.BlockSpec((BLK, cut), lambda i: (0, i)),
        out_shape=jax.ShapeDtypeStruct((BLK, units), BF16),
        scratch_shapes=[pltpu.VMEM((BLK, features), BF16)],
        compiler_params=pltpu.CompilerParams(vmem_limit_bytes=VMEM_LIMIT),
        cost_estimate=pl.CostEstimate(
            flops=4 * BLK * features * units,
            bytes_accessed=4 * features * units,
            transcendentals=BLK * units,
        ),
    )(states, gain.reshape(1, features), in_weight, in_weight)


def t5_out_kernel(hidden_ref, out_w, out_ref):
    total = jnp.dot(hidden_ref[...], out_w[...], preferred_element_type=F32)
    out_ref[0] = total.astype(BF16)


def t5_out(hidden, out_weight, n_seq):
    units, features = out_weight.shape
    feat = features // n_seq
    return pl.pallas_call(
        t5_out_kernel,
        grid=(n_seq,),
        in_specs=[
            pl.BlockSpec((BLK, units), lambda i: (0, 0)),
            pl.BlockSpec((units, feat), lambda i: (0, i)),
        ],
        out_specs=pl.BlockSpec((1, BLK, feat), lambda i: (i, 0, 0)),
        out_shape=jax.ShapeDtypeStruct((n_seq, BLK, feat), BF16),
        compiler_params=pltpu.CompilerParams(vmem_limit_bytes=VMEM_LIMIT),
        cost_estimate=pl.CostEstimate(
            flops=2 * BLK * features * units,
            bytes_accessed=2 * features * units,
            transcendentals=0,
        ),
    )(hidden, out_weight)


def on_device(
    enc_states,
    lengths,
    prompt_owner_sample,
    t5_gain,
    t5_in_weight,
    t5_out_weight,
    t5_final_gain,
    context_weight,
    text_shift,
    text_scale,
    kv_weight,
    text_key_gain,
    image_query_key_value,
    image_qk_gain,
    proj_weight,
    dora_a,
    dora_b,
    magnitude,
    grad_out,
):
    seq_rank = lax.axis_index("seq")
    data_rank = lax.axis_index("dp")
    n_seq = lax.axis_size("seq")
    n_dp = lax.axis_size("dp")
    n_all = n_seq * n_dp
    both = ("dp", "seq")
    rank, own_cols = dora_b.shape
    own_rows = dora_a.shape[0]
    model = own_cols * n_dp
    lanes = 128
    rows_of = model // lanes
    cotangent = to_gathered(grad_out[0], n_dp)

    pair = seq_rank % 2
    flip_z = [(i, i ^ 1) for i in range(n_seq)]
    n_y = n_seq // 2

    weights = jnp.concatenate(
        [context_weight.T, kv_weight.reshape(kv_weight.shape[0], -1)], 1
    )
    near_weights = near_shard(weights)
    own_heads, first_heads, second_heads = pack_heads(
        image_query_key_value[0].transpose(1, 0, 2), pair, n_seq
    )
    t5_gain, first_heads = lax.optimization_barrier((t5_gain, first_heads))
    first_heads = lax.ppermute(first_heads, "seq", flip_z)
    direction_t = proj_weight.T.astype(F32) + lax.dot_general(
        dora_b, dora_a, (((0,), (1,)), ((), ())), precision=lax.Precision.HIGHEST
    )
    direction_t = direction_t.astype(BF16)
    rows_y = swap(jnp.broadcast_to(direction_t[None], (n_y, own_cols, own_rows)), "seq", Y_GROUPS)
    rows_y, own_heads = lax.optimization_barrier((rows_y, own_heads))
    own_heads = swap(own_heads, "seq", Y_GROUPS)

    tokens = enc_states[0, :BLK]
    feat = tokens.shape[1] // n_seq
    hidden = t5_in(enc_states, t5_gain, t5_in_weight)
    hidden, near_weights = lax.optimization_barrier((hidden, near_weights))
    weights = gather_columns(weights, near_weights)
    depth = context_weight.shape[0]
    context_all = weights[:, :depth]
    ffn = t5_out(hidden, t5_out_weight, n_seq)
    own_heads, ffn, first_heads, second_heads = lax.optimization_barrier(
        (own_heads, ffn, first_heads, second_heads)
    )
    second_heads = lax.ppermute(second_heads, "seq", flip_z)

    rows_f = rows_y.astype(F32)
    column_sq = jnp.sum(rows_f * rows_f, (0, 2))
    column_sq = column_sq + lax.ppermute(column_sq, "seq", flip_z)
    ratio = magnitude / jnp.sqrt(column_sq + EPSILON)
    scaled_t = (rows_f * ratio[None, :, None]).astype(BF16)
    scaled_t = scaled_t.transpose(1, 0, 2).reshape(own_cols, -1)
    reach = scaled_t.shape[1]
    up = jnp.pad((dora_b * ratio).astype(BF16).T, ((0, 0), (0, lanes - rank)))
    scaled_t = jnp.concatenate([scaled_t, up], 1)
    near_scaled = near_shard(scaled_t)

    ffn = swap(ffn, "seq")
    ffn, second_heads = lax.optimization_barrier((ffn, second_heads))
    ffn_sum = jnp.sum(ffn.astype(F32), 0)

    other_heads = swap(jnp.concatenate([first_heads, second_heads], 1), "seq", Y_GROUPS)

    own_tokens = lax.dynamic_slice_in_dim(tokens, seq_rank * feat, feat, 1).astype(F32)
    own_final = lax.dynamic_slice_in_dim(t5_final_gain, seq_rank * feat, feat, 0)
    encoded = ((own_tokens + ffn_sum) * own_final).astype(BF16)
    context = dot_t(encoded, context_all).astype(BF16).reshape(BLK, rows_of, lanes)
    context, other_heads, near_scaled = lax.optimization_barrier(
        (context, other_heads, near_scaled)
    )
    scaled_all = gather_columns(scaled_t, near_scaled)
    up_all = scaled_all[:, reach:]
    arrived = swap(context, both)
    token_of = jnp.sum(arrived.reshape(n_dp, n_seq, rows_of, lanes).astype(F32), 1).astype(BF16)
    values = token_of.astype(F32)
    centre = jnp.mean(values, (1, 2), keepdims=True)
    spread = jnp.mean((values - centre) * (values - centre), (1, 2), keepdims=True)
    layer_normed = ((values - centre) * lax.rsqrt(spread + EPSILON)).astype(BF16)
    target = jnp.arange(n_all, dtype=jnp.int32) // n_seq
    one_hot = (target[:, None] == prompt_owner_sample[None, :]).astype(BF16)
    outgoing = jnp.einsum("sp,pab->sab", one_hot, layer_normed, preferred_element_type=F32)
    text = swap(outgoing.astype(BF16), both).reshape(BLK, model)
    scale, shift = to_gathered(text_scale, n_dp), to_gathered(text_shift, n_dp)
    modulated = ((1.0 + scale) * text.astype(F32) + shift).astype(BF16)
    length = jnp.sum(jnp.where(prompt_owner_sample == data_rank, lengths, 0))

    num, den = image_attention(own_heads, other_heads, image_qk_gain)
    down_factor = jnp.pad(dora_a.astype(BF16), ((0, 0), (0, lanes - rank)))
    attended = prompt_attention(
        length.reshape(1),
        own_heads,
        other_heads,
        modulated,
        weights,
        depth // HD,
        down_factor,
        image_qk_gain,
        text_key_gain.reshape(1, HD),
        num,
        den,
    )

    gathered = swap(attended, "seq", Y_GROUPS)
    down = jnp.dot(cotangent, up_all, preferred_element_type=F32).astype(BF16)
    down = jnp.concatenate([down, lax.ppermute(down, "seq", flip_z)], 0)
    cotangent_other = lax.ppermute(cotangent, "seq", flip_z)
    gathered, down, cotangent_other = lax.optimization_barrier((gathered, down, cotangent_other))
    lowered = jnp.sum(gathered[:, :, own_rows:].astype(F32), 0)
    lowered_other = lax.ppermute(lowered[BLK:].astype(BF16), "seq", flip_z)
    gathered = gathered[:, :, :own_rows].transpose(1, 0, 2).reshape(2 * BLK, -1)
    sent_rows, kept_rows = gathered[BLK:], gathered[:BLK]
    half = model // 2
    part = dot_t(sent_rows, scaled_all[:half, :reach])
    sum_first = jnp.sum(part * cotangent_other[:, :half].astype(F32), 0)
    part = part.astype(BF16)

    lowered = (lowered[:BLK] + lowered_other.astype(F32)).astype(BF16)[:, :rank]
    up_part = lax.dot_general(
        lowered, cotangent, (((0,), (0,)), ((), ())), preferred_element_type=F32
    ).astype(BF16)
    up_part = up_part.reshape(rank, n_dp // 2, 2, own_cols).transpose(2, 1, 0, 3)
    up_part = up_part.reshape(n_dp, rank, own_cols)
    sent_rows, part, up_part = lax.optimization_barrier((sent_rows, part, up_part))
    landed_first = lax.ppermute(part, "seq", flip_z)
    up_part = swap(up_part, "dp")
    part = dot_t(sent_rows, scaled_all[half:, :reach])
    sum_second = jnp.sum(part * cotangent_other[:, half:].astype(F32), 0)
    kept_rows, part, landed_first = lax.optimization_barrier(
        (kept_rows, part.astype(BF16), landed_first)
    )
    landed_second = lax.ppermute(part, "seq", flip_z)
    kept = dot_t(kept_rows, scaled_all[:, :reach])

    for bit in (2, 4):
        moved = lax.ppermute(down, "seq", [(i, i ^ bit) for i in range(n_seq)])
        first = (seq_rank & bit) == 0
        down = jnp.concatenate([jnp.where(first, down, moved), jnp.where(first, moved, down)], 0)
    rows_all = attended.reshape(-1, own_rows + lanes)[:, :own_rows]
    grad_a = lax.dot_general(
        down[:, :rank], rows_all, (((0,), (0,)), ((), ())), preferred_element_type=F32
    )
    for bit in (1, 2, 4):
        grad_a = grad_a.astype(BF16)
        moved = lax.ppermute(grad_a, "dp", [(i, i ^ bit) for i in range(n_dp)])
        grad_a = grad_a.astype(F32) + moved.astype(F32)
    grad_a = grad_a.astype(BF16)

    magnitude_part = jnp.concatenate([sum_first, sum_second])
    magnitude_part = magnitude_part + jnp.sum(kept * cotangent.astype(F32), 0)
    magnitude_part = magnitude_part.astype(BF16).reshape(n_dp // 2, 2, own_cols).transpose(1, 0, 2)
    magnitude_part = jnp.broadcast_to(
        magnitude_part.reshape(n_dp, 1, own_cols), (n_dp, n_seq, own_cols)
    )
    magnitude_part, up_part, grad_a = lax.optimization_barrier((magnitude_part, up_part, grad_a))
    magnitude_part = swap(magnitude_part.reshape(n_all, own_cols), both)
    grad_magnitude = jnp.sum(magnitude_part.astype(F32), 0) / magnitude

    out = kept + jnp.concatenate([landed_first, landed_second], 1).astype(F32)
    image_out = from_gathered(out.astype(BF16), n_dp)[None]
    moved = lax.ppermute(grad_a, "dp", [(i, i ^ 8) for i in range(n_dp)])
    grad_a = (grad_a.astype(F32) + moved.astype(F32)).T
    grad_b = jnp.sum(up_part.astype(F32), 0)
    for bit in (2, 4, 1):
        grad_b = grad_b.astype(BF16)
        moved = lax.ppermute(grad_b, "seq", [(i, i ^ bit) for i in range(n_seq)])
        grad_b = grad_b.astype(F32) + moved.astype(F32)
    grad_b = grad_b * ratio
    return (image_out, grad_a, grad_b, grad_magnitude)


def solution(mesh):
    return jax.shard_map(
        on_device,
        mesh=mesh,
        in_specs=(
            P("dp", None, None),
            P(),
            P(),
            P(),
            P(None, None, "seq"),
            P("seq", None),
            P(),
            P("seq", "dp"),
            P("dp", None),
            P("dp", None),
            P("dp", None, "seq"),
            P(),
            P("dp", "seq", None, None),
            P(),
            P("seq", "dp"),
            P("seq", None),
            P(None, "dp"),
            P("dp"),
            P("dp", "seq", None),
        ),
        out_specs=(P("dp", "seq", None), P("seq", None), P(None, "dp"), P("dp")),
        check_vma=False,
    )
```

```python
import math

import jax
import jax.numpy as jnp
from jax import lax
from jax.experimental import pallas as pl
from jax.experimental.pallas import tpu as pltpu
from jax.sharding import PartitionSpec as P

HD = 128
BLK = 128
EPSILON = 1e-06
VMEM_LIMIT = 56 * 1024 * 1024
F32 = jnp.float32
BF16 = jnp.bfloat16
Y_GROUPS = [[0, 2, 4, 6], [1, 3, 5, 7]]
QUERY_SCALE = math.log2(math.e) / math.sqrt(HD)


def rms_scale(values, gain):
    return values * lax.rsqrt(jnp.mean(values * values, -1, keepdims=True) + EPSILON) * gain


def swap(values, axes, groups=None):
    return lax.all_to_all(values, axes, 0, 0, tiled=True, axis_index_groups=groups)


def near_shard(values):
    n_dp = lax.axis_size("dp")
    return lax.ppermute(values, "dp", [(i, (i + n_dp // 2) % n_dp) for i in range(n_dp)])


def gather_columns(values, other):
    n_dp = lax.axis_size("dp")
    near = n_dp // 2
    low = lax.axis_index("dp") < near
    halves = jnp.stack([jnp.where(low, values, other), jnp.where(low, other, values)])
    groups = [list(range(near)), list(range(near, n_dp))]
    gathered = lax.all_gather(halves, "dp", axis=0, axis_index_groups=groups)
    return gathered.reshape(n_dp * values.shape[0], values.shape[1])


def to_gathered(values, n_dp):
    rows = values.shape[0]
    cut = values.reshape(rows, 2, n_dp // 2, -1)
    return cut.transpose(0, 2, 1, 3).reshape(rows, -1)


def from_gathered(values, n_dp):
    rows = values.shape[0]
    cut = values.reshape(rows, n_dp // 2, 2, -1)
    return cut.transpose(0, 2, 1, 3).reshape(rows, -1)


def dot_t(left, right):
    return lax.dot_general(left, right, (((1,), (1,)), ((), ())), preferred_element_type=F32)


def pack_kernel(_, own_in, other_in, own_ref, first_ref, second_ref):
    own_ref[0] = own_in[...].reshape(own_ref.shape[1:])
    other = other_in[...].reshape(own_ref.shape[1:])
    half = first_ref.shape[1]
    first_ref[0] = other[:half]
    second_ref[0] = other[half:]


def pack_heads(rows, pair, n_seq):
    kinds, count, model = rows.shape
    width = model // n_seq
    n_y = n_seq // 2
    block = (kinds, count, width)
    total = kinds * count

    def spec(size):
        return pl.BlockSpec((1, size, width), lambda y, z: (y, 0, 0))

    def shape(size):
        return jax.ShapeDtypeStruct((n_y, size, width), rows.dtype)

    return pl.pallas_call(
        pack_kernel,
        grid_spec=pltpu.PrefetchScalarGridSpec(
            num_scalar_prefetch=1,
            grid=(n_y,),
            in_specs=[
                pl.BlockSpec(block, lambda y, z: (0, 0, 2 * y + z[0])),
                pl.BlockSpec(block, lambda y, z: (0, 0, 2 * y + 1 - z[0])),
            ],
            out_specs=[spec(total), spec(total // 2), spec(total // 2)],
        ),
        out_shape=[shape(total), shape(total // 2), shape(total // 2)],
        compiler_params=pltpu.CompilerParams(vmem_limit_bytes=VMEM_LIMIT),
        cost_estimate=pl.CostEstimate(flops=0, bytes_accessed=4 * rows.size, transcendentals=0),
    )(pair.reshape(1), rows, rows)


def image_kernel(
    q_own, q_other, k_own, k_other, v_own, v_other, gain_ref, num_ref, den_ref, keys, values
):
    half = keys.shape[0] // 2

    @pl.when(pl.program_id(1) == 0)
    def _():
        for at, k_ref, v_ref in ((0, k_own, v_own), (half, k_other, v_other)):
            k = k_ref[...].reshape(-1, HD).astype(F32)
            keys[at : at + half, :] = rms_scale(k, gain_ref[1:2, :]).astype(BF16)
            values[at : at + half, :HD] = v_ref[...].reshape(-1, HD)
        values[:, HD:] = jnp.ones((2 * half, HD), BF16)

    q = jnp.concatenate([q_own[0], q_other[0]], 0).astype(F32)
    q = rms_scale(q, gain_ref[0:1, :] * QUERY_SCALE).astype(BF16)
    weight = jnp.exp2(dot_t(q, keys[...])).astype(BF16)
    both = jnp.dot(weight, values[...], preferred_element_type=F32)
    num_ref[...] = both[:, :HD]
    den_ref[...] = both[:, HD:]


def image_attention(own, other, gains):
    n_y, _, width = own.shape
    heads = width // HD
    rows = 2 * BLK
    image_len = n_y * rows

    def queries():
        return pl.BlockSpec((1, BLK, HD), lambda h, b: (b, 0, h))

    def whole(kind):
        return pl.BlockSpec((n_y, BLK, HD), lambda h, b: (0, kind, h))

    return pl.pallas_call(
        image_kernel,
        grid=(heads, n_y),
        in_specs=[
            queries(),
            queries(),
            whole(1),
            whole(1),
            whole(2),
            whole(2),
            pl.BlockSpec((2, HD), lambda h, b: (0, 0)),
        ],
        out_specs=[
            pl.BlockSpec((rows, HD), lambda h, b: (b, h)),
            pl.BlockSpec((rows, HD), lambda h, b: (b, h)),
        ],
        out_shape=[jax.ShapeDtypeStruct((image_len, width), F32)] * 2,
        scratch_shapes=[pltpu.VMEM((image_len, HD), BF16), pltpu.VMEM((image_len, 2 * HD), BF16)],
        compiler_params=pltpu.CompilerParams(vmem_limit_bytes=VMEM_LIMIT),
        cost_estimate=pl.CostEstimate(
            flops=6 * image_len * image_len * width,
            bytes_accessed=14 * image_len * width,
            transcendentals=heads * image_len * image_len,
        ),
    )(own, other, own, other, own, other, gains)


def prompt_kernel(
    length_ref,
    q_own,
    q_other,
    text_ref,
    k_weight,
    v_weight,
    down_ref,
    gain_ref,
    text_gain_ref,
    num_ref,
    den_ref,
    out_ref,
    lowered,
):
    head = pl.program_id(0)
    heads = pl.num_programs(0) - 1

    @pl.when(head == 0)
    def _():
        lowered[...] = jnp.zeros_like(lowered)

    @pl.when(head < heads)
    def _():
        text = text_ref[...]
        k = jnp.dot(text, k_weight[...], preferred_element_type=F32)
        k = rms_scale(k, text_gain_ref[...]).astype(BF16)
        v = jnp.dot(text, v_weight[...], preferred_element_type=F32).astype(BF16)
        stacked = jnp.concatenate([v, jnp.ones_like(v)], axis=1)
        groups, rows, _ = out_ref.shape
        for b in range(groups):
            q = jnp.concatenate([q_own[b], q_other[b]], 0).astype(F32)
            q = rms_scale(q, gain_ref[0:1, :] * QUERY_SCALE).astype(BF16)
            weight = jnp.exp2(dot_t(q, k))
            valid = lax.broadcasted_iota(jnp.int32, weight.shape, 1) < length_ref[0]
            weight = jnp.where(valid, weight, 0.0).astype(BF16)
            both = jnp.dot(weight, stacked, preferred_element_type=F32)
            at = slice(b * rows, (b + 1) * rows)
            total = num_ref[at, :] + both[:, :HD]
            attended = (total / (den_ref[at, :] + both[:, HD:])).astype(BF16)
            out_ref[b] = attended
            lowered[at, :] += jnp.dot(attended, down_ref[...], preferred_element_type=F32)

    @pl.when(head == heads)
    def _():
        out_ref[...] = lowered[...].reshape(out_ref.shape).astype(BF16)


def prompt_attention(length, own, other, text, weights, first, down, gains, text_gain, num, den):
    groups, _, width = own.shape
    heads = width // HD
    image_len = groups * 2 * BLK
    model = text.shape[1]

    def last(h):
        return jnp.minimum(h, heads - 1)

    return pl.pallas_call(
        prompt_kernel,
        grid=(heads + 1,),
        in_specs=[
            pl.BlockSpec(memory_space=pltpu.SMEM),
            pl.BlockSpec((groups, BLK, HD), lambda h: (0, 0, last(h))),
            pl.BlockSpec((groups, BLK, HD), lambda h: (0, 0, last(h))),
            pl.BlockSpec((BLK, model), lambda h: (0, 0)),
            pl.BlockSpec((model, HD), lambda h: (0, first + last(h))),
            pl.BlockSpec((model, HD), lambda h: (0, first + heads + last(h))),
            pl.BlockSpec((HD, down.shape[1]), lambda h: (last(h), 0)),
            pl.BlockSpec((2, HD), lambda h: (0, 0)),
            pl.BlockSpec((1, HD), lambda h: (0, 0)),
            pl.BlockSpec((image_len, HD), lambda h: (0, last(h))),
            pl.BlockSpec((image_len, HD), lambda h: (0, last(h))),
        ],
        out_specs=pl.BlockSpec((groups, 2 * BLK, HD), lambda h: (0, 0, h)),
        out_shape=jax.ShapeDtypeStruct((groups, 2 * BLK, width + HD), BF16),
        scratch_shapes=[pltpu.VMEM((image_len, HD), F32)],
        compiler_params=pltpu.CompilerParams(vmem_limit_bytes=VMEM_LIMIT),
        cost_estimate=pl.CostEstimate(
            flops=6 * image_len * BLK * width + 4 * BLK * model * width,
            bytes_accessed=12 * image_len * width + 4 * model * width,
            transcendentals=heads * image_len * BLK,
        ),
    )(length, own, other, text, weights, weights, down, gains, text_gain, num, den)


def t5_in_kernel(x_ref, gain_ref, gate_w, up_w, out_ref, normed):
    @pl.when(pl.program_id(0) == 0)
    def _():
        normed[...] = rms_scale(x_ref[0].astype(F32), gain_ref[...]).astype(BF16)

    gate = jnp.dot(normed[...], gate_w[0], preferred_element_type=F32)
    upward = jnp.dot(normed[...], up_w[0], preferred_element_type=F32)
    out_ref[...] = (jax.nn.gelu(gate, approximate=True) * upward).astype(BF16)


def t5_in(states, gain, in_weight):
    _, features, units = in_weight.shape
    cut = 128
    return pl.pallas_call(
        t5_in_kernel,
        grid=(units // cut,),
        in_specs=[
            pl.BlockSpec((1, BLK, features), lambda i: (0, 0, 0)),
            pl.BlockSpec((1, features), lambda i: (0, 0)),
            pl.BlockSpec((1, features, cut), lambda i: (0, 0, i)),
            pl.BlockSpec((1, features, cut), lambda i: (1, 0, i)),
        ],
        out_specs=pl.BlockSpec((BLK, cut), lambda i: (0, i)),
        out_shape=jax.ShapeDtypeStruct((BLK, units), BF16),
        scratch_shapes=[pltpu.VMEM((BLK, features), BF16)],
        compiler_params=pltpu.CompilerParams(vmem_limit_bytes=VMEM_LIMIT),
        cost_estimate=pl.CostEstimate(
            flops=4 * BLK * features * units,
            bytes_accessed=4 * features * units,
            transcendentals=BLK * units,
        ),
    )(states, gain.reshape(1, features), in_weight, in_weight)


def t5_out_kernel(hidden_ref, out_w, out_ref):
    total = jnp.dot(hidden_ref[...], out_w[...], preferred_element_type=F32)
    out_ref[0] = total.astype(BF16)


def t5_out(hidden, out_weight, n_seq):
    units, features = out_weight.shape
    feat = features // n_seq
    return pl.pallas_call(
        t5_out_kernel,
        grid=(n_seq,),
        in_specs=[
            pl.BlockSpec((BLK, units), lambda i: (0, 0)),
            pl.BlockSpec((units, feat), lambda i: (0, i)),
        ],
        out_specs=pl.BlockSpec((1, BLK, feat), lambda i: (i, 0, 0)),
        out_shape=jax.ShapeDtypeStruct((n_seq, BLK, feat), BF16),
        compiler_params=pltpu.CompilerParams(vmem_limit_bytes=VMEM_LIMIT),
        cost_estimate=pl.CostEstimate(
            flops=2 * BLK * features * units,
            bytes_accessed=2 * features * units,
            transcendentals=0,
        ),
    )(hidden, out_weight)


def on_device(
    enc_states,
    lengths,
    prompt_owner_sample,
    t5_gain,
    t5_in_weight,
    t5_out_weight,
    t5_final_gain,
    context_weight,
    text_shift,
    text_scale,
    kv_weight,
    text_key_gain,
    image_query_key_value,
    image_qk_gain,
    proj_weight,
    dora_a,
    dora_b,
    magnitude,
    grad_out,
):
    seq_rank = lax.axis_index("seq")
    data_rank = lax.axis_index("dp")
    n_seq = lax.axis_size("seq")
    n_dp = lax.axis_size("dp")
    n_all = n_seq * n_dp
    both = ("dp", "seq")
    rank, own_cols = dora_b.shape
    own_rows = dora_a.shape[0]
    model = own_cols * n_dp
    lanes = 128
    rows_of = model // lanes
    cotangent = to_gathered(grad_out[0], n_dp)

    pair = seq_rank % 2
    flip_z = [(i, i ^ 1) for i in range(n_seq)]
    n_y = n_seq // 2

    weights = jnp.concatenate(
        [context_weight.T, kv_weight.reshape(kv_weight.shape[0], -1)], 1
    )
    near_weights = near_shard(weights)
    own_heads, first_heads, second_heads = pack_heads(
        image_query_key_value[0].transpose(1, 0, 2), pair, n_seq
    )
    t5_gain, first_heads = lax.optimization_barrier((t5_gain, first_heads))
    first_heads = lax.ppermute(first_heads, "seq", flip_z)
    direction_t = proj_weight.T.astype(F32) + lax.dot_general(
        dora_b, dora_a, (((0,), (1,)), ((), ())), precision=lax.Precision.HIGHEST
    )
    direction_t = direction_t.astype(BF16)
    shifted = [direction_t]
    for step in range(1, n_y):
        ahead = [(i, (i + 2 * step) % n_seq) for i in range(n_seq)]
        shifted.insert(0, lax.ppermute(direction_t, "seq", ahead))
    own_heads = swap(own_heads, "seq", Y_GROUPS)

    tokens = enc_states[0, :BLK]
    feat = tokens.shape[1] // n_seq
    hidden = t5_in(enc_states, t5_gain, t5_in_weight)
    hidden, near_weights, shifted = lax.optimization_barrier((hidden, near_weights, shifted))
    weights = gather_columns(weights, near_weights)
    depth = context_weight.shape[0]
    context_all = weights[:, :depth]
    rows_y = jnp.stack(shifted + shifted[:-1])
    rows_y = lax.dynamic_slice_in_dim(rows_y, n_y - 1 - seq_rank // 2, n_y, 0)
    column_sq = jnp.sum(jnp.square(jnp.stack(shifted).astype(F32)), (0, 2))
    column_other = lax.ppermute(column_sq, "seq", flip_z)
    ffn = t5_out(hidden, t5_out_weight, n_seq)
    own_heads, ffn, first_heads, second_heads, column_other = lax.optimization_barrier(
        (own_heads, ffn, first_heads, second_heads, column_other)
    )
    second_heads = lax.ppermute(second_heads, "seq", flip_z)

    rows_f = rows_y.astype(F32)
    ratio = magnitude / jnp.sqrt(column_sq + column_other + EPSILON)
    scaled_t = (rows_f * ratio[None, :, None]).astype(BF16)
    scaled_t = scaled_t.transpose(1, 0, 2).reshape(own_cols, -1)
    reach = scaled_t.shape[1]
    up = jnp.pad((dora_b * ratio).astype(BF16).T, ((0, 0), (0, lanes - rank)))
    scaled_t = jnp.concatenate([scaled_t, up], 1)
    near_scaled = near_shard(scaled_t)

    ffn = swap(ffn, "seq")
    ffn, second_heads = lax.optimization_barrier((ffn, second_heads))
    ffn_sum = jnp.sum(ffn.astype(F32), 0)

    other_heads = swap(jnp.concatenate([first_heads, second_heads], 1), "seq", Y_GROUPS)

    own_tokens = lax.dynamic_slice_in_dim(tokens, seq_rank * feat, feat, 1).astype(F32)
    own_final = lax.dynamic_slice_in_dim(t5_final_gain, seq_rank * feat, feat, 0)
    encoded = ((own_tokens + ffn_sum) * own_final).astype(BF16)
    context = dot_t(encoded, context_all).astype(BF16).reshape(BLK, rows_of, lanes)
    context, other_heads, near_scaled = lax.optimization_barrier(
        (context, other_heads, near_scaled)
    )
    scaled_all = gather_columns(scaled_t, near_scaled)
    up_all = scaled_all[:, reach:]
    arrived = swap(context, both)
    token_of = jnp.sum(arrived.reshape(n_dp, n_seq, rows_of, lanes).astype(F32), 1).astype(BF16)
    values = token_of.astype(F32)
    centre = jnp.mean(values, (1, 2), keepdims=True)
    spread = jnp.mean((values - centre) * (values - centre), (1, 2), keepdims=True)
    layer_normed = ((values - centre) * lax.rsqrt(spread + EPSILON)).astype(BF16)
    target = jnp.arange(n_all, dtype=jnp.int32) // n_seq
    one_hot = (target[:, None] == prompt_owner_sample[None, :]).astype(BF16)
    outgoing = jnp.einsum("sp,pab->sab", one_hot, layer_normed, preferred_element_type=F32)
    num, den = image_attention(own_heads, other_heads, image_qk_gain)
    outgoing, num, den = lax.optimization_barrier((outgoing.astype(BF16), num, den))
    text = swap(outgoing, both).reshape(BLK, model)
    scale, shift = to_gathered(text_scale, n_dp), to_gathered(text_shift, n_dp)
    modulated = ((1.0 + scale) * text.astype(F32) + shift).astype(BF16)
    length = jnp.sum(jnp.where(prompt_owner_sample == data_rank, lengths, 0))

    down_factor = jnp.pad(dora_a.astype(BF16), ((0, 0), (0, lanes - rank)))
    attended = prompt_attention(
        length.reshape(1),
        own_heads,
        other_heads,
        modulated,
        weights,
        depth // HD,
        down_factor,
        image_qk_gain,
        text_key_gain.reshape(1, HD),
        num,
        den,
    )

    gathered = swap(attended, "seq", Y_GROUPS)
    down = jnp.dot(cotangent, up_all, preferred_element_type=F32).astype(BF16)
    down = jnp.concatenate([down, lax.ppermute(down, "seq", flip_z)], 0)
    cotangent_other = lax.ppermute(cotangent, "seq", flip_z)
    gathered, down, cotangent_other = lax.optimization_barrier((gathered, down, cotangent_other))
    lowered = jnp.sum(gathered[:, :, own_rows:].astype(F32), 0)
    lowered_other = lax.ppermute(lowered[BLK:].astype(BF16), "seq", flip_z)
    gathered = gathered[:, :, :own_rows].transpose(1, 0, 2).reshape(2 * BLK, -1)
    half = model // 2

    def project(rows, at):
        product = dot_t(rows, scaled_all[at : at + half, :reach])
        sums = jnp.sum(product[:BLK] * cotangent[:, at : at + half].astype(F32), 0)
        sums = sums + jnp.sum(product[BLK:] * cotangent_other[:, at : at + half].astype(F32), 0)
        return product[:BLK], product[BLK:].astype(BF16), sums

    kept_first, sent, sum_first = project(gathered, 0)
    gathered, sent = lax.optimization_barrier((gathered, sent))
    landed_first = lax.ppermute(sent, "seq", flip_z)

    lowered = (lowered[:BLK] + lowered_other.astype(F32)).astype(BF16)[:, :rank]
    up_part = lax.dot_general(
        lowered, cotangent, (((0,), (0,)), ((), ())), preferred_element_type=F32
    ).astype(BF16)
    up_part = up_part.reshape(rank, n_dp // 2, 2, own_cols).transpose(2, 1, 0, 3)
    up_part = up_part.reshape(n_dp, rank, own_cols)
    gathered, up_part = lax.optimization_barrier((gathered, up_part))
    up_part = swap(up_part, "dp")
    kept_second, sent, sum_second = project(gathered, half)
    sent, landed_first = lax.optimization_barrier((sent, landed_first))
    landed_second = lax.ppermute(sent, "seq", flip_z)

    for bit in (2, 4):
        moved = lax.ppermute(down, "seq", [(i, i ^ bit) for i in range(n_seq)])
        first = (seq_rank & bit) == 0
        down = jnp.concatenate([jnp.where(first, down, moved), jnp.where(first, moved, down)], 0)
    rows_all = attended.reshape(-1, own_rows + lanes)[:, :own_rows]
    grad_a = lax.dot_general(
        down[:, :rank], rows_all, (((0,), (0,)), ((), ())), preferred_element_type=F32
    )
    for bit in (1, 2, 4):
        grad_a = grad_a.astype(BF16)
        moved = lax.ppermute(grad_a, "dp", [(i, i ^ bit) for i in range(n_dp)])
        grad_a = grad_a.astype(F32) + moved.astype(F32)
    grad_a = grad_a.astype(BF16)

    magnitude_part = jnp.concatenate([sum_first, sum_second])
    magnitude_part = magnitude_part.astype(BF16).reshape(n_dp // 2, 2, own_cols).transpose(1, 0, 2)
    magnitude_part = jnp.broadcast_to(
        magnitude_part.reshape(n_dp, 1, own_cols), (n_dp, n_seq, own_cols)
    )
    magnitude_part, up_part = lax.optimization_barrier((magnitude_part, up_part))
    magnitude_part = swap(magnitude_part.reshape(n_all, own_cols), both)
    grad_magnitude = jnp.sum(magnitude_part.astype(F32), 0) / magnitude

    out = [kept_first + landed_first.astype(F32), kept_second + landed_second.astype(F32)]
    image_out = from_gathered(jnp.concatenate(out, 1).astype(BF16), n_dp)[None]
    moved = lax.ppermute(grad_a, "dp", [(i, i ^ 8) for i in range(n_dp)])
    grad_a = (grad_a.astype(F32) + moved.astype(F32)).T
    grad_b = jnp.sum(up_part.astype(F32), 0)
    for bit in (2, 4, 1):
        grad_b = grad_b.astype(BF16)
        moved = lax.ppermute(grad_b, "seq", [(i, i ^ bit) for i in range(n_seq)])
        grad_b = grad_b.astype(F32) + moved.astype(F32)
    grad_b = grad_b * ratio
    return (image_out, grad_a, grad_b, grad_magnitude)


def solution(mesh):
    return jax.shard_map(
        on_device,
        mesh=mesh,
        in_specs=(
            P("dp", None, None),
            P(),
            P(),
            P(),
            P(None, None, "seq"),
            P("seq", None),
            P(),
            P("seq", "dp"),
            P("dp", None),
            P("dp", None),
            P("dp", None, "seq"),
            P(),
            P("dp", "seq", None, None),
            P(),
            P("seq", "dp"),
            P("seq", None),
            P(None, "dp"),
            P("dp"),
            P("dp", "seq", None),
        ),
        out_specs=(P("dp", "seq", None), P("seq", None), P(None, "dp"), P("dp")),
        check_vma=False,
    )
```

```python
import math

import jax
import jax.numpy as jnp
from jax import lax
from jax.experimental import pallas as pl
from jax.experimental.pallas import tpu as pltpu
from jax.sharding import PartitionSpec as P

HD = 128
BLK = 128
EPSILON = 1e-06
VMEM_LIMIT = 56 * 1024 * 1024
F32 = jnp.float32
BF16 = jnp.bfloat16
Y_GROUPS = [[0, 2, 4, 6], [1, 3, 5, 7]]
QUERY_SCALE = math.log2(math.e) / math.sqrt(HD)


def rms_scale(values, gain):
    return values * lax.rsqrt(jnp.mean(values * values, -1, keepdims=True) + EPSILON) * gain


def swap(values, axes, groups=None):
    return lax.all_to_all(values, axes, 0, 0, tiled=True, axis_index_groups=groups)


def near_shard(values):
    n_dp = lax.axis_size("dp")
    return lax.ppermute(values, "dp", [(i, (i + n_dp // 2) % n_dp) for i in range(n_dp)])


def gather_columns(values, other):
    n_dp = lax.axis_size("dp")
    near = n_dp // 2
    low = lax.axis_index("dp") < near
    halves = jnp.stack([jnp.where(low, values, other), jnp.where(low, other, values)])
    groups = [list(range(near)), list(range(near, n_dp))]
    gathered = lax.all_gather(halves, "dp", axis=0, axis_index_groups=groups)
    return gathered.reshape(n_dp * values.shape[0], values.shape[1])


def to_gathered(values, n_dp):
    rows = values.shape[0]
    cut = values.reshape(rows, 2, n_dp // 2, -1)
    return cut.transpose(0, 2, 1, 3).reshape(rows, -1)


def from_gathered(values, n_dp):
    rows = values.shape[0]
    cut = values.reshape(rows, n_dp // 2, 2, -1)
    return cut.transpose(0, 2, 1, 3).reshape(rows, -1)


def dot_t(left, right):
    return lax.dot_general(left, right, (((1,), (1,)), ((), ())), preferred_element_type=F32)


def pack_kernel(_, own_in, other_in, own_ref, first_ref, second_ref):
    own_ref[0] = own_in[...].reshape(own_ref.shape[1:])
    other = other_in[...].reshape(own_ref.shape[1:])
    half = first_ref.shape[1]
    first_ref[0] = other[:half]
    second_ref[0] = other[half:]


def pack_heads(rows, pair, n_seq):
    kinds, count, model = rows.shape
    width = model // n_seq
    n_y = n_seq // 2
    block = (kinds, count, width)
    total = kinds * count

    def spec(size):
        return pl.BlockSpec((1, size, width), lambda y, z: (y, 0, 0))

    def shape(size):
        return jax.ShapeDtypeStruct((n_y, size, width), rows.dtype)

    return pl.pallas_call(
        pack_kernel,
        grid_spec=pltpu.PrefetchScalarGridSpec(
            num_scalar_prefetch=1,
            grid=(n_y,),
            in_specs=[
                pl.BlockSpec(block, lambda y, z: (0, 0, 2 * y + z[0])),
                pl.BlockSpec(block, lambda y, z: (0, 0, 2 * y + 1 - z[0])),
            ],
            out_specs=[spec(total), spec(total // 2), spec(total // 2)],
        ),
        out_shape=[shape(total), shape(total // 2), shape(total // 2)],
        compiler_params=pltpu.CompilerParams(vmem_limit_bytes=VMEM_LIMIT),
        cost_estimate=pl.CostEstimate(flops=0, bytes_accessed=4 * rows.size, transcendentals=0),
    )(pair.reshape(1), rows, rows)


def image_kernel(
    q_own, q_other, k_own, k_other, v_own, v_other, gain_ref, num_ref, den_ref, keys, values
):
    half = keys.shape[0] // 2

    @pl.when(pl.program_id(1) == 0)
    def _():
        for at, k_ref, v_ref in ((0, k_own, v_own), (half, k_other, v_other)):
            k = k_ref[...].reshape(-1, HD).astype(F32)
            keys[at : at + half, :] = rms_scale(k, gain_ref[1:2, :]).astype(BF16)
            values[at : at + half, :HD] = v_ref[...].reshape(-1, HD)
        values[:, HD:] = jnp.ones((2 * half, HD), BF16)

    q = jnp.concatenate([q_own[0], q_other[0]], 0).astype(F32)
    q = rms_scale(q, gain_ref[0:1, :] * QUERY_SCALE).astype(BF16)
    weight = jnp.exp2(dot_t(q, keys[...])).astype(BF16)
    both = jnp.dot(weight, values[...], preferred_element_type=F32)
    num_ref[...] = both[:, :HD]
    den_ref[...] = both[:, HD:]


def image_attention(own, other, gains):
    n_y, _, width = own.shape
    heads = width // HD
    rows = 2 * BLK
    image_len = n_y * rows

    def queries():
        return pl.BlockSpec((1, BLK, HD), lambda h, b: (b, 0, h))

    def whole(kind):
        return pl.BlockSpec((n_y, BLK, HD), lambda h, b: (0, kind, h))

    return pl.pallas_call(
        image_kernel,
        grid=(heads, n_y),
        in_specs=[
            queries(),
            queries(),
            whole(1),
            whole(1),
            whole(2),
            whole(2),
            pl.BlockSpec((2, HD), lambda h, b: (0, 0)),
        ],
        out_specs=[
            pl.BlockSpec((rows, HD), lambda h, b: (b, h)),
            pl.BlockSpec((rows, HD), lambda h, b: (b, h)),
        ],
        out_shape=[jax.ShapeDtypeStruct((image_len, width), F32)] * 2,
        scratch_shapes=[pltpu.VMEM((image_len, HD), BF16), pltpu.VMEM((image_len, 2 * HD), BF16)],
        compiler_params=pltpu.CompilerParams(vmem_limit_bytes=VMEM_LIMIT),
        cost_estimate=pl.CostEstimate(
            flops=6 * image_len * image_len * width,
            bytes_accessed=14 * image_len * width,
            transcendentals=heads * image_len * image_len,
        ),
    )(own, other, own, other, own, other, gains)


def prompt_kernel(
    length_ref,
    q_own,
    q_other,
    text_ref,
    k_weight,
    v_weight,
    down_ref,
    gain_ref,
    text_gain_ref,
    num_ref,
    den_ref,
    out_ref,
    lowered,
):
    head = pl.program_id(0)
    heads = pl.num_programs(0) - 1

    @pl.when(head == 0)
    def _():
        lowered[...] = jnp.zeros_like(lowered)

    @pl.when(head < heads)
    def _():
        text = text_ref[...]
        k = jnp.dot(text, k_weight[...], preferred_element_type=F32)
        k = rms_scale(k, text_gain_ref[...]).astype(BF16)
        v = jnp.dot(text, v_weight[...], preferred_element_type=F32).astype(BF16)
        stacked = jnp.concatenate([v, jnp.ones_like(v)], axis=1)
        groups, rows, _ = out_ref.shape
        for b in range(groups):
            q = jnp.concatenate([q_own[b], q_other[b]], 0).astype(F32)
            q = rms_scale(q, gain_ref[0:1, :] * QUERY_SCALE).astype(BF16)
            weight = jnp.exp2(dot_t(q, k))
            valid = lax.broadcasted_iota(jnp.int32, weight.shape, 1) < length_ref[0]
            weight = jnp.where(valid, weight, 0.0).astype(BF16)
            both = jnp.dot(weight, stacked, preferred_element_type=F32)
            at = slice(b * rows, (b + 1) * rows)
            total = num_ref[at, :] + both[:, :HD]
            attended = (total / (den_ref[at, :] + both[:, HD:])).astype(BF16)
            out_ref[b] = attended
            lowered[at, :] += jnp.dot(attended, down_ref[...], preferred_element_type=F32)

    @pl.when(head == heads)
    def _():
        out_ref[...] = lowered[...].reshape(out_ref.shape).astype(BF16)


def prompt_attention(length, own, other, text, weights, first, down, gains, text_gain, num, den):
    groups, _, width = own.shape
    heads = width // HD
    image_len = groups * 2 * BLK
    model = text.shape[1]

    def last(h):
        return jnp.minimum(h, heads - 1)

    return pl.pallas_call(
        prompt_kernel,
        grid=(heads + 1,),
        in_specs=[
            pl.BlockSpec(memory_space=pltpu.SMEM),
            pl.BlockSpec((groups, BLK, HD), lambda h: (0, 0, last(h))),
            pl.BlockSpec((groups, BLK, HD), lambda h: (0, 0, last(h))),
            pl.BlockSpec((BLK, model), lambda h: (0, 0)),
            pl.BlockSpec((model, HD), lambda h: (0, first + last(h))),
            pl.BlockSpec((model, HD), lambda h: (0, first + heads + last(h))),
            pl.BlockSpec((HD, down.shape[1]), lambda h: (last(h), 0)),
            pl.BlockSpec((2, HD), lambda h: (0, 0)),
            pl.BlockSpec((1, HD), lambda h: (0, 0)),
            pl.BlockSpec((image_len, HD), lambda h: (0, last(h))),
            pl.BlockSpec((image_len, HD), lambda h: (0, last(h))),
        ],
        out_specs=pl.BlockSpec((groups, 2 * BLK, HD), lambda h: (0, 0, h)),
        out_shape=jax.ShapeDtypeStruct((groups, 2 * BLK, width + HD), BF16),
        scratch_shapes=[pltpu.VMEM((image_len, HD), F32)],
        compiler_params=pltpu.CompilerParams(vmem_limit_bytes=VMEM_LIMIT),
        cost_estimate=pl.CostEstimate(
            flops=6 * image_len * BLK * width + 4 * BLK * model * width,
            bytes_accessed=12 * image_len * width + 4 * model * width,
            transcendentals=heads * image_len * BLK,
        ),
    )(length, own, other, text, weights, weights, down, gains, text_gain, num, den)


def t5_in_kernel(x_ref, gain_ref, gate_w, up_w, out_ref, normed):
    @pl.when(pl.program_id(0) == 0)
    def _():
        normed[...] = rms_scale(x_ref[0].astype(F32), gain_ref[...]).astype(BF16)

    gate = jnp.dot(normed[...], gate_w[0], preferred_element_type=F32)
    upward = jnp.dot(normed[...], up_w[0], preferred_element_type=F32)
    out_ref[...] = (jax.nn.gelu(gate, approximate=True) * upward).astype(BF16)


def t5_in(states, gain, in_weight):
    _, features, units = in_weight.shape
    cut = 128
    return pl.pallas_call(
        t5_in_kernel,
        grid=(units // cut,),
        in_specs=[
            pl.BlockSpec((1, BLK, features), lambda i: (0, 0, 0)),
            pl.BlockSpec((1, features), lambda i: (0, 0)),
            pl.BlockSpec((1, features, cut), lambda i: (0, 0, i)),
            pl.BlockSpec((1, features, cut), lambda i: (1, 0, i)),
        ],
        out_specs=pl.BlockSpec((BLK, cut), lambda i: (0, i)),
        out_shape=jax.ShapeDtypeStruct((BLK, units), BF16),
        scratch_shapes=[pltpu.VMEM((BLK, features), BF16)],
        compiler_params=pltpu.CompilerParams(vmem_limit_bytes=VMEM_LIMIT),
        cost_estimate=pl.CostEstimate(
            flops=4 * BLK * features * units,
            bytes_accessed=4 * features * units,
            transcendentals=BLK * units,
        ),
    )(states, gain.reshape(1, features), in_weight, in_weight)


def t5_out_kernel(hidden_ref, out_w, out_ref):
    total = jnp.dot(hidden_ref[...], out_w[...], preferred_element_type=F32)
    out_ref[0] = total.astype(BF16)


def t5_out(hidden, out_weight, n_seq):
    units, features = out_weight.shape
    feat = features // n_seq
    return pl.pallas_call(
        t5_out_kernel,
        grid=(n_seq,),
        in_specs=[
            pl.BlockSpec((BLK, units), lambda i: (0, 0)),
            pl.BlockSpec((units, feat), lambda i: (0, i)),
        ],
        out_specs=pl.BlockSpec((1, BLK, feat), lambda i: (i, 0, 0)),
        out_shape=jax.ShapeDtypeStruct((n_seq, BLK, feat), BF16),
        compiler_params=pltpu.CompilerParams(vmem_limit_bytes=VMEM_LIMIT),
        cost_estimate=pl.CostEstimate(
            flops=2 * BLK * features * units,
            bytes_accessed=2 * features * units,
            transcendentals=0,
        ),
    )(hidden, out_weight)


def on_device(
    enc_states,
    lengths,
    prompt_owner_sample,
    t5_gain,
    t5_in_weight,
    t5_out_weight,
    t5_final_gain,
    context_weight,
    text_shift,
    text_scale,
    kv_weight,
    text_key_gain,
    image_query_key_value,
    image_qk_gain,
    proj_weight,
    dora_a,
    dora_b,
    magnitude,
    grad_out,
):
    seq_rank = lax.axis_index("seq")
    data_rank = lax.axis_index("dp")
    n_seq = lax.axis_size("seq")
    n_dp = lax.axis_size("dp")
    n_all = n_seq * n_dp
    both = ("dp", "seq")
    rank, own_cols = dora_b.shape
    own_rows = dora_a.shape[0]
    model = own_cols * n_dp
    lanes = 128
    rows_of = model // lanes
    cotangent = to_gathered(grad_out[0], n_dp)

    pair = seq_rank % 2
    flip_z = [(i, i ^ 1) for i in range(n_seq)]
    n_y = n_seq // 2

    weights = jnp.concatenate(
        [context_weight.T, kv_weight.reshape(kv_weight.shape[0], -1)], 1
    )
    near_weights = near_shard(weights)
    own_heads, first_heads, second_heads = pack_heads(
        image_query_key_value[0].transpose(1, 0, 2), pair, n_seq
    )
    t5_gain, first_heads = lax.optimization_barrier((t5_gain, first_heads))
    first_heads = lax.ppermute(first_heads, "seq", flip_z)
    direction_t = proj_weight.T.astype(F32) + lax.dot_general(
        dora_b, dora_a, (((0,), (1,)), ((), ())), precision=lax.Precision.HIGHEST
    )
    direction_t = direction_t.astype(BF16)
    shifted = [direction_t]
    for step in range(1, n_y):
        ahead = [(i, (i + 2 * step) % n_seq) for i in range(n_seq)]
        shifted.insert(0, lax.ppermute(direction_t, "seq", ahead))
    own_heads = swap(own_heads, "seq", Y_GROUPS)

    tokens = enc_states[0, :BLK]
    feat = tokens.shape[1] // n_seq
    hidden = t5_in(enc_states, t5_gain, t5_in_weight)
    hidden, near_weights, shifted = lax.optimization_barrier((hidden, near_weights, shifted))
    weights = gather_columns(weights, near_weights)
    depth = context_weight.shape[0]
    context_all = weights[:, :depth]
    column_sq = jnp.sum(jnp.square(jnp.stack(shifted).astype(F32)), (0, 2))
    column_other = lax.ppermute(column_sq, "seq", flip_z)
    hidden, own_heads, first_heads, second_heads = lax.optimization_barrier(
        (hidden, own_heads, first_heads, second_heads)
    )
    second_heads = lax.ppermute(second_heads, "seq", flip_z)
    ffn = t5_out(hidden, t5_out_weight, n_seq)
    ffn, column_other = lax.optimization_barrier((ffn, column_other))

    ratio = magnitude / jnp.sqrt(column_sq + column_other + EPSILON)
    scaled_t = []
    for row in range(n_y):
        turned = [shifted[(row - at - 1) % n_y] for at in range(n_y)]
        block = lax.select_n(seq_rank // 2, *turned)
        scaled_t.append((block.astype(F32) * ratio[:, None]).astype(BF16))
    scaled_t = jnp.concatenate(scaled_t, 1)
    reach = scaled_t.shape[1]
    up = jnp.pad((dora_b * ratio).astype(BF16).T, ((0, 0), (0, lanes - rank)))
    scaled_t = jnp.concatenate([scaled_t, up], 1)
    near_scaled = near_shard(scaled_t)

    ffn = swap(ffn, "seq")
    ffn, second_heads, near_scaled, cotangent = lax.optimization_barrier(
        (ffn, second_heads, near_scaled, cotangent)
    )
    cotangent_other = lax.ppermute(cotangent, "seq", flip_z)
    scaled_all = gather_columns(scaled_t, near_scaled)
    up_all = scaled_all[:, reach:]
    ffn_sum = jnp.sum(ffn.astype(F32), 0)

    other_heads = swap(jnp.concatenate([first_heads, second_heads], 1), "seq", Y_GROUPS)

    own_tokens = lax.dynamic_slice_in_dim(tokens, seq_rank * feat, feat, 1).astype(F32)
    own_final = lax.dynamic_slice_in_dim(t5_final_gain, seq_rank * feat, feat, 0)
    encoded = ((own_tokens + ffn_sum) * own_final).astype(BF16)
    context = dot_t(encoded, context_all).astype(BF16).reshape(BLK, rows_of, lanes)
    context, other_heads, cotangent_other = lax.optimization_barrier(
        (context, other_heads, cotangent_other)
    )
    arrived = swap(context, both)
    token_of = jnp.sum(arrived.reshape(n_dp, n_seq, rows_of, lanes).astype(F32), 1).astype(BF16)
    values = token_of.astype(F32)
    centre = jnp.mean(values, (1, 2), keepdims=True)
    spread = jnp.mean((values - centre) * (values - centre), (1, 2), keepdims=True)
    layer_normed = ((values - centre) * lax.rsqrt(spread + EPSILON)).astype(BF16)
    target = jnp.arange(n_all, dtype=jnp.int32) // n_seq
    one_hot = (target[:, None] == prompt_owner_sample[None, :]).astype(BF16)
    outgoing = jnp.einsum("sp,pab->sab", one_hot, layer_normed, preferred_element_type=F32)
    num, den = image_attention(own_heads, other_heads, image_qk_gain)
    outgoing, num, den = lax.optimization_barrier((outgoing.astype(BF16), num, den))
    text = swap(outgoing, both).reshape(BLK, model)
    scale, shift = to_gathered(text_scale, n_dp), to_gathered(text_shift, n_dp)
    modulated = ((1.0 + scale) * text.astype(F32) + shift).astype(BF16)
    length = jnp.sum(jnp.where(prompt_owner_sample == data_rank, lengths, 0))

    down_factor = jnp.pad(dora_a.astype(BF16), ((0, 0), (0, lanes - rank)))
    attended = prompt_attention(
        length.reshape(1),
        own_heads,
        other_heads,
        modulated,
        weights,
        depth // HD,
        down_factor,
        image_qk_gain,
        text_key_gain.reshape(1, HD),
        num,
        den,
    )

    gathered = swap(attended, "seq", Y_GROUPS)
    down = jnp.dot(cotangent, up_all, preferred_element_type=F32).astype(BF16)
    down = jnp.concatenate([down, lax.ppermute(down, "seq", flip_z)], 0)
    gathered, down = lax.optimization_barrier((gathered, down))
    lowered = jnp.sum(gathered[:, :, own_rows:].astype(F32), 0)
    gathered, lowered = lax.optimization_barrier((gathered, lowered))
    lowered_other = lax.ppermute(lowered[BLK:].astype(BF16), "seq", flip_z)
    gathered = gathered[:, :, :own_rows].transpose(1, 0, 2).reshape(2 * BLK, -1)
    half = model // 2

    def project(rows, at):
        product = dot_t(rows, scaled_all[at : at + half, :reach])
        sums = jnp.sum(product[:BLK] * cotangent[:, at : at + half].astype(F32), 0)
        sums = sums + jnp.sum(product[BLK:] * cotangent_other[:, at : at + half].astype(F32), 0)
        return product[:BLK], product[BLK:].astype(BF16), sums

    kept_first, sent, sum_first = project(gathered, 0)
    gathered, sent = lax.optimization_barrier((gathered, sent))
    landed_first = lax.ppermute(sent, "seq", flip_z)

    lowered = (lowered[:BLK] + lowered_other.astype(F32)).astype(BF16)[:, :rank]
    up_part = lax.dot_general(
        lowered, cotangent, (((0,), (0,)), ((), ())), preferred_element_type=F32
    ).astype(BF16)
    up_part = up_part.reshape(rank, n_dp // 2, 2, own_cols).transpose(2, 1, 0, 3)
    up_part = up_part.reshape(n_dp, rank, own_cols)
    gathered, up_part = lax.optimization_barrier((gathered, up_part))
    up_part = swap(up_part, "dp")
    kept_second, sent, sum_second = project(gathered, half)
    sent, sum_second, landed_first, up_part = lax.optimization_barrier(
        (sent, sum_second, landed_first, up_part)
    )
    landed_second = lax.ppermute(sent, "seq", flip_z)

    for bit in (2, 4):
        moved = lax.ppermute(down, "seq", [(i, i ^ bit) for i in range(n_seq)])
        first = (seq_rank & bit) == 0
        down = jnp.concatenate([jnp.where(first, down, moved), jnp.where(first, moved, down)], 0)
    rows_all = attended.reshape(-1, own_rows + lanes)[:, :own_rows]
    grad_a = lax.dot_general(
        down[:, :rank], rows_all, (((0,), (0,)), ((), ())), preferred_element_type=F32
    )
    for bit in (1, 2, 4):
        grad_a = grad_a.astype(BF16)
        moved = lax.ppermute(grad_a, "dp", [(i, i ^ bit) for i in range(n_dp)])
        grad_a = grad_a.astype(F32) + moved.astype(F32)
    grad_a = grad_a.astype(BF16)

    magnitude_part = jnp.concatenate([sum_first, sum_second])
    magnitude_part = magnitude_part.astype(BF16).reshape(n_dp // 2, 2, own_cols).transpose(1, 0, 2)
    magnitude_part = jnp.broadcast_to(
        magnitude_part.reshape(n_dp, 1, own_cols), (n_dp, n_seq, own_cols)
    )
    magnitude_part, up_part = lax.optimization_barrier((magnitude_part, up_part))
    magnitude_part = swap(magnitude_part.reshape(n_all, own_cols), both)
    grad_magnitude = jnp.sum(magnitude_part.astype(F32), 0) / magnitude

    out = [kept_first + landed_first.astype(F32), kept_second + landed_second.astype(F32)]
    image_out = from_gathered(jnp.concatenate(out, 1).astype(BF16), n_dp)[None]
    moved = lax.ppermute(grad_a, "dp", [(i, i ^ 8) for i in range(n_dp)])
    grad_a = (grad_a.astype(F32) + moved.astype(F32)).T
    grad_b = jnp.sum(up_part.astype(F32), 0)
    for bit in (2, 4, 1):
        grad_b = grad_b.astype(BF16)
        moved = lax.ppermute(grad_b, "seq", [(i, i ^ bit) for i in range(n_seq)])
        grad_b = grad_b.astype(F32) + moved.astype(F32)
    grad_b = grad_b * ratio
    return (image_out, grad_a, grad_b, grad_magnitude)


def solution(mesh):
    return jax.shard_map(
        on_device,
        mesh=mesh,
        in_specs=(
            P("dp", None, None),
            P(),
            P(),
            P(),
            P(None, None, "seq"),
            P("seq", None),
            P(),
            P("seq", "dp"),
            P("dp", None),
            P("dp", None),
            P("dp", None, "seq"),
            P(),
            P("dp", "seq", None, None),
            P(),
            P("seq", "dp"),
            P("seq", None),
            P(None, "dp"),
            P("dp"),
            P("dp", "seq", None),
        ),
        out_specs=(P("dp", "seq", None), P("seq", None), P(None, "dp"), P("dp")),
        check_vma=False,
    )
```

```python
import math

import jax
import jax.numpy as jnp
from jax import lax
from jax.experimental import pallas as pl
from jax.experimental.pallas import tpu as pltpu
from jax.sharding import PartitionSpec as P

HD = 128
BLK = 128
EPSILON = 1e-06
VMEM_LIMIT = 56 * 1024 * 1024
F32 = jnp.float32
BF16 = jnp.bfloat16
Y_GROUPS = [[0, 2, 4, 6], [1, 3, 5, 7]]
QUERY_SCALE = math.log2(math.e) / math.sqrt(HD)


def rms_scale(values, gain):
    return values * lax.rsqrt(jnp.mean(values * values, -1, keepdims=True) + EPSILON) * gain


def swap(values, axes, groups=None):
    return lax.all_to_all(values, axes, 0, 0, tiled=True, axis_index_groups=groups)


def near_shard(values):
    n_dp = lax.axis_size("dp")
    return lax.ppermute(values, "dp", [(i, (i + n_dp // 2) % n_dp) for i in range(n_dp)])


def gather_columns(values, other):
    n_dp = lax.axis_size("dp")
    near = n_dp // 2
    low = lax.axis_index("dp") < near
    halves = jnp.stack([jnp.where(low, values, other), jnp.where(low, other, values)])
    groups = [list(range(near)), list(range(near, n_dp))]
    gathered = lax.all_gather(halves, "dp", axis=0, axis_index_groups=groups)
    return gathered.reshape(n_dp * values.shape[0], values.shape[1])


def to_gathered(values, n_dp):
    rows = values.shape[0]
    cut = values.reshape(rows, 2, n_dp // 2, -1)
    return cut.transpose(0, 2, 1, 3).reshape(rows, -1)


def from_gathered(values, n_dp):
    rows = values.shape[0]
    cut = values.reshape(rows, n_dp // 2, 2, -1)
    return cut.transpose(0, 2, 1, 3).reshape(rows, -1)


def dot_t(left, right):
    return lax.dot_general(left, right, (((1,), (1,)), ((), ())), preferred_element_type=F32)


def pack_kernel(_, own_in, other_in, own_ref, first_ref, second_ref):
    own_ref[0] = own_in[...].reshape(own_ref.shape[1:])
    other = other_in[...].reshape(own_ref.shape[1:])
    half = first_ref.shape[1]
    first_ref[0] = other[:half]
    second_ref[0] = other[half:]


def pack_heads(rows, pair, n_seq):
    kinds, count, model = rows.shape
    width = model // n_seq
    n_y = n_seq // 2
    block = (kinds, count, width)
    total = kinds * count

    def spec(size):
        return pl.BlockSpec((1, size, width), lambda y, z: (y, 0, 0))

    def shape(size):
        return jax.ShapeDtypeStruct((n_y, size, width), rows.dtype)

    return pl.pallas_call(
        pack_kernel,
        grid_spec=pltpu.PrefetchScalarGridSpec(
            num_scalar_prefetch=1,
            grid=(n_y,),
            in_specs=[
                pl.BlockSpec(block, lambda y, z: (0, 0, 2 * y + z[0])),
                pl.BlockSpec(block, lambda y, z: (0, 0, 2 * y + 1 - z[0])),
            ],
            out_specs=[spec(total), spec(total // 2), spec(total // 2)],
        ),
        out_shape=[shape(total), shape(total // 2), shape(total // 2)],
        compiler_params=pltpu.CompilerParams(vmem_limit_bytes=VMEM_LIMIT),
        cost_estimate=pl.CostEstimate(flops=0, bytes_accessed=4 * rows.size, transcendentals=0),
    )(pair.reshape(1), rows, rows)


def image_kernel(
    q_own, q_other, k_own, k_other, v_own, v_other, gain_ref, num_ref, den_ref, keys, values
):
    half = keys.shape[0] // 2

    @pl.when(pl.program_id(1) == 0)
    def _():
        for at, k_ref, v_ref in ((0, k_own, v_own), (half, k_other, v_other)):
            k = k_ref[...].reshape(-1, HD).astype(F32)
            keys[at : at + half, :] = rms_scale(k, gain_ref[1:2, :]).astype(BF16)
            values[at : at + half, :HD] = v_ref[...].reshape(-1, HD)
        values[:, HD:] = jnp.ones((2 * half, HD), BF16)

    q = jnp.concatenate([q_own[0], q_other[0]], 0).astype(F32)
    q = rms_scale(q, gain_ref[0:1, :] * QUERY_SCALE).astype(BF16)
    weight = jnp.exp2(dot_t(q, keys[...])).astype(BF16)
    both = jnp.dot(weight, values[...], preferred_element_type=F32)
    num_ref[...] = both[:, :HD]
    den_ref[...] = both[:, HD:]


def image_attention(own, other, gains):
    n_y, _, width = own.shape
    heads = width // HD
    rows = 2 * BLK
    image_len = n_y * rows

    def queries():
        return pl.BlockSpec((1, BLK, HD), lambda h, b: (b, 0, h))

    def whole(kind):
        return pl.BlockSpec((n_y, BLK, HD), lambda h, b: (0, kind, h))

    return pl.pallas_call(
        image_kernel,
        grid=(heads, n_y),
        in_specs=[
            queries(),
            queries(),
            whole(1),
            whole(1),
            whole(2),
            whole(2),
            pl.BlockSpec((2, HD), lambda h, b: (0, 0)),
        ],
        out_specs=[
            pl.BlockSpec((rows, HD), lambda h, b: (b, h)),
            pl.BlockSpec((rows, HD), lambda h, b: (b, h)),
        ],
        out_shape=[jax.ShapeDtypeStruct((image_len, width), F32)] * 2,
        scratch_shapes=[pltpu.VMEM((image_len, HD), BF16), pltpu.VMEM((image_len, 2 * HD), BF16)],
        compiler_params=pltpu.CompilerParams(vmem_limit_bytes=VMEM_LIMIT),
        cost_estimate=pl.CostEstimate(
            flops=6 * image_len * image_len * width,
            bytes_accessed=14 * image_len * width,
            transcendentals=heads * image_len * image_len,
        ),
    )(own, other, own, other, own, other, gains)


def prompt_kernel(
    length_ref,
    q_own,
    q_other,
    text_ref,
    k_weight,
    v_weight,
    down_ref,
    gain_ref,
    text_gain_ref,
    num_ref,
    den_ref,
    out_ref,
    lowered,
):
    head = pl.program_id(0)
    heads = pl.num_programs(0) - 1

    @pl.when(head == 0)
    def _():
        lowered[...] = jnp.zeros_like(lowered)

    @pl.when(head < heads)
    def _():
        text = text_ref[...]
        k = jnp.dot(text, k_weight[...], preferred_element_type=F32)
        k = rms_scale(k, text_gain_ref[...]).astype(BF16)
        v = jnp.dot(text, v_weight[...], preferred_element_type=F32).astype(BF16)
        stacked = jnp.concatenate([v, jnp.ones_like(v)], axis=1)
        groups, rows, _ = out_ref.shape
        for b in range(groups):
            q = jnp.concatenate([q_own[b], q_other[b]], 0).astype(F32)
            q = rms_scale(q, gain_ref[0:1, :] * QUERY_SCALE).astype(BF16)
            weight = jnp.exp2(dot_t(q, k))
            valid = lax.broadcasted_iota(jnp.int32, weight.shape, 1) < length_ref[0]
            weight = jnp.where(valid, weight, 0.0).astype(BF16)
            both = jnp.dot(weight, stacked, preferred_element_type=F32)
            at = slice(b * rows, (b + 1) * rows)
            total = num_ref[at, :] + both[:, :HD]
            attended = (total / (den_ref[at, :] + both[:, HD:])).astype(BF16)
            out_ref[b] = attended
            lowered[at, :] += jnp.dot(attended, down_ref[...], preferred_element_type=F32)

    @pl.when(head == heads)
    def _():
        out_ref[...] = lowered[...].reshape(out_ref.shape).astype(BF16)


def prompt_attention(length, own, other, text, weights, first, down, gains, text_gain, num, den):
    groups, _, width = own.shape
    heads = width // HD
    image_len = groups * 2 * BLK
    model = text.shape[1]

    def last(h):
        return jnp.minimum(h, heads - 1)

    return pl.pallas_call(
        prompt_kernel,
        grid=(heads + 1,),
        in_specs=[
            pl.BlockSpec(memory_space=pltpu.SMEM),
            pl.BlockSpec((groups, BLK, HD), lambda h: (0, 0, last(h))),
            pl.BlockSpec((groups, BLK, HD), lambda h: (0, 0, last(h))),
            pl.BlockSpec((BLK, model), lambda h: (0, 0)),
            pl.BlockSpec((model, HD), lambda h: (0, first + last(h))),
            pl.BlockSpec((model, HD), lambda h: (0, first + heads + last(h))),
            pl.BlockSpec((HD, down.shape[1]), lambda h: (last(h), 0)),
            pl.BlockSpec((2, HD), lambda h: (0, 0)),
            pl.BlockSpec((1, HD), lambda h: (0, 0)),
            pl.BlockSpec((image_len, HD), lambda h: (0, last(h))),
            pl.BlockSpec((image_len, HD), lambda h: (0, last(h))),
        ],
        out_specs=pl.BlockSpec((groups, 2 * BLK, HD), lambda h: (0, 0, h)),
        out_shape=jax.ShapeDtypeStruct((groups, 2 * BLK, width + HD), BF16),
        scratch_shapes=[pltpu.VMEM((image_len, HD), F32)],
        compiler_params=pltpu.CompilerParams(vmem_limit_bytes=VMEM_LIMIT),
        cost_estimate=pl.CostEstimate(
            flops=6 * image_len * BLK * width + 4 * BLK * model * width,
            bytes_accessed=12 * image_len * width + 4 * model * width,
            transcendentals=heads * image_len * BLK,
        ),
    )(length, own, other, text, weights, weights, down, gains, text_gain, num, den)


def t5_in_kernel(x_ref, gain_ref, gate_w, up_w, out_ref, normed):
    @pl.when(pl.program_id(0) == 0)
    def _():
        normed[...] = rms_scale(x_ref[0].astype(F32), gain_ref[...]).astype(BF16)

    gate = jnp.dot(normed[...], gate_w[0], preferred_element_type=F32)
    upward = jnp.dot(normed[...], up_w[0], preferred_element_type=F32)
    out_ref[...] = (jax.nn.gelu(gate, approximate=True) * upward).astype(BF16)


def t5_in(states, gain, in_weight):
    _, features, units = in_weight.shape
    cut = 128
    return pl.pallas_call(
        t5_in_kernel,
        grid=(units // cut,),
        in_specs=[
            pl.BlockSpec((1, BLK, features), lambda i: (0, 0, 0)),
            pl.BlockSpec((1, features), lambda i: (0, 0)),
            pl.BlockSpec((1, features, cut), lambda i: (0, 0, i)),
            pl.BlockSpec((1, features, cut), lambda i: (1, 0, i)),
        ],
        out_specs=pl.BlockSpec((BLK, cut), lambda i: (0, i)),
        out_shape=jax.ShapeDtypeStruct((BLK, units), BF16),
        scratch_shapes=[pltpu.VMEM((BLK, features), BF16)],
        compiler_params=pltpu.CompilerParams(vmem_limit_bytes=VMEM_LIMIT),
        cost_estimate=pl.CostEstimate(
            flops=4 * BLK * features * units,
            bytes_accessed=4 * features * units,
            transcendentals=BLK * units,
        ),
    )(states, gain.reshape(1, features), in_weight, in_weight)


def t5_out_kernel(hidden_ref, out_w, out_ref):
    total = jnp.dot(hidden_ref[...], out_w[...], preferred_element_type=F32)
    out_ref[0] = total.astype(BF16)


def t5_out(hidden, out_weight, n_seq):
    units, features = out_weight.shape
    feat = features // n_seq
    return pl.pallas_call(
        t5_out_kernel,
        grid=(n_seq,),
        in_specs=[
            pl.BlockSpec((BLK, units), lambda i: (0, 0)),
            pl.BlockSpec((units, feat), lambda i: (0, i)),
        ],
        out_specs=pl.BlockSpec((1, BLK, feat), lambda i: (i, 0, 0)),
        out_shape=jax.ShapeDtypeStruct((n_seq, BLK, feat), BF16),
        compiler_params=pltpu.CompilerParams(vmem_limit_bytes=VMEM_LIMIT),
        cost_estimate=pl.CostEstimate(
            flops=2 * BLK * features * units,
            bytes_accessed=2 * features * units,
            transcendentals=0,
        ),
    )(hidden, out_weight)


def on_device(
    enc_states,
    lengths,
    prompt_owner_sample,
    t5_gain,
    t5_in_weight,
    t5_out_weight,
    t5_final_gain,
    context_weight,
    text_shift,
    text_scale,
    kv_weight,
    text_key_gain,
    image_query_key_value,
    image_qk_gain,
    proj_weight,
    dora_a,
    dora_b,
    magnitude,
    grad_out,
):
    seq_rank = lax.axis_index("seq")
    data_rank = lax.axis_index("dp")
    n_seq = lax.axis_size("seq")
    n_dp = lax.axis_size("dp")
    n_all = n_seq * n_dp
    both = ("dp", "seq")
    rank, own_cols = dora_b.shape
    own_rows = dora_a.shape[0]
    model = own_cols * n_dp
    lanes = 128
    rows_of = model // lanes
    cotangent = to_gathered(grad_out[0], n_dp)

    pair = seq_rank % 2
    flip_z = [(i, i ^ 1) for i in range(n_seq)]
    n_y = n_seq // 2

    weights = jnp.concatenate(
        [context_weight.T, kv_weight.reshape(kv_weight.shape[0], -1)], 1
    )
    near_weights = near_shard(weights)
    own_heads, first_heads, second_heads = pack_heads(
        image_query_key_value[0].transpose(1, 0, 2), pair, n_seq
    )
    t5_gain, first_heads = lax.optimization_barrier((t5_gain, first_heads))
    first_heads = lax.ppermute(first_heads, "seq", flip_z)
    direction_t = proj_weight.T.astype(F32) + lax.dot_general(
        dora_b, dora_a, (((0,), (1,)), ((), ())), precision=lax.Precision.HIGHEST
    )
    direction_t = direction_t.astype(BF16)
    shifted = [direction_t]
    for step in range(1, n_y):
        ahead = [(i, (i + 2 * step) % n_seq) for i in range(n_seq)]
        shifted.insert(0, lax.ppermute(direction_t, "seq", ahead))
    own_heads = swap(own_heads, "seq", Y_GROUPS)

    tokens = enc_states[0, :BLK]
    feat = tokens.shape[1] // n_seq
    hidden = t5_in(enc_states, t5_gain, t5_in_weight)
    hidden, near_weights, shifted, first_heads, second_heads = lax.optimization_barrier(
        (hidden, near_weights, shifted, first_heads, second_heads)
    )
    second_heads = lax.ppermute(second_heads, "seq", flip_z)
    weights = gather_columns(weights, near_weights)
    depth = context_weight.shape[0]
    context_all = weights[:, :depth]
    column_sq = jnp.sum(jnp.square(jnp.stack(shifted).astype(F32)), (0, 2))
    column_other = lax.ppermute(column_sq, "seq", flip_z)
    ffn = t5_out(hidden, t5_out_weight, n_seq)
    own_heads, ffn, second_heads, column_other = lax.optimization_barrier(
        (own_heads, ffn, second_heads, column_other)
    )

    ratio = magnitude / jnp.sqrt(column_sq + column_other + EPSILON)
    scaled_t = []
    for row in range(n_y):
        turned = [shifted[(row - at - 1) % n_y] for at in range(n_y)]
        block = lax.select_n(seq_rank // 2, *turned)
        scaled_t.append((block.astype(F32) * ratio[:, None]).astype(BF16))
    scaled_t = jnp.concatenate(scaled_t, 1)
    reach = scaled_t.shape[1]
    up = jnp.pad((dora_b * ratio).astype(BF16).T, ((0, 0), (0, lanes - rank)))
    scaled_t = jnp.concatenate([scaled_t, up], 1)
    near_scaled = near_shard(scaled_t)

    ffn = swap(ffn, "seq")
    ffn, second_heads = lax.optimization_barrier((ffn, second_heads))
    ffn_sum = jnp.sum(ffn.astype(F32), 0)

    other_heads = swap(jnp.concatenate([first_heads, second_heads], 1), "seq", Y_GROUPS)

    own_tokens = lax.dynamic_slice_in_dim(tokens, seq_rank * feat, feat, 1).astype(F32)
    own_final = lax.dynamic_slice_in_dim(t5_final_gain, seq_rank * feat, feat, 0)
    encoded = ((own_tokens + ffn_sum) * own_final).astype(BF16)
    context = dot_t(encoded, context_all).astype(BF16).reshape(BLK, rows_of, lanes)
    context, other_heads, near_scaled = lax.optimization_barrier(
        (context, other_heads, near_scaled)
    )
    scaled_all = gather_columns(scaled_t, near_scaled)
    up_all = scaled_all[:, reach:]
    arrived = swap(context, both)
    token_of = jnp.sum(arrived.reshape(n_dp, n_seq, rows_of, lanes).astype(F32), 1).astype(BF16)
    values = token_of.astype(F32)
    centre = jnp.mean(values, (1, 2), keepdims=True)
    spread = jnp.mean((values - centre) * (values - centre), (1, 2), keepdims=True)
    layer_normed = ((values - centre) * lax.rsqrt(spread + EPSILON)).astype(BF16)
    target = jnp.arange(n_all, dtype=jnp.int32) // n_seq
    one_hot = (target[:, None] == prompt_owner_sample[None, :]).astype(BF16)
    outgoing = jnp.einsum("sp,pab->sab", one_hot, layer_normed, preferred_element_type=F32)
    num, den = image_attention(own_heads, other_heads, image_qk_gain)
    outgoing, num, den = lax.optimization_barrier((outgoing.astype(BF16), num, den))
    text = swap(outgoing, both).reshape(BLK, model)
    scale, shift = to_gathered(text_scale, n_dp), to_gathered(text_shift, n_dp)
    modulated = ((1.0 + scale) * text.astype(F32) + shift).astype(BF16)
    length = jnp.sum(jnp.where(prompt_owner_sample == data_rank, lengths, 0))

    down_factor = jnp.pad(dora_a.astype(BF16), ((0, 0), (0, lanes - rank)))
    attended = prompt_attention(
        length.reshape(1),
        own_heads,
        other_heads,
        modulated,
        weights,
        depth // HD,
        down_factor,
        image_qk_gain,
        text_key_gain.reshape(1, HD),
        num,
        den,
    )

    gathered = swap(attended, "seq", Y_GROUPS)
    down = jnp.dot(cotangent, up_all, preferred_element_type=F32).astype(BF16)
    down = jnp.concatenate([down, lax.ppermute(down, "seq", flip_z)], 0)
    cotangent_other, _ = lax.optimization_barrier((cotangent, attended))
    cotangent_other = lax.ppermute(cotangent_other, "seq", flip_z)
    gathered, down, cotangent_other = lax.optimization_barrier((gathered, down, cotangent_other))
    lowered = jnp.sum(gathered[:, :, own_rows:].astype(F32), 0)
    gathered, lowered = lax.optimization_barrier((gathered, lowered))
    lowered_other = lax.ppermute(lowered[BLK:].astype(BF16), "seq", flip_z)
    gathered = gathered[:, :, :own_rows].transpose(1, 0, 2).reshape(2 * BLK, -1)
    half = model // 2

    def project(rows, at):
        product = dot_t(rows, scaled_all[at : at + half, :reach])
        sums = jnp.sum(product[:BLK] * cotangent[:, at : at + half].astype(F32), 0)
        sums = sums + jnp.sum(product[BLK:] * cotangent_other[:, at : at + half].astype(F32), 0)
        return product[:BLK], product[BLK:].astype(BF16), sums

    kept_first, sent, sum_first = project(gathered, 0)
    gathered, sent = lax.optimization_barrier((gathered, sent))
    landed_first = lax.ppermute(sent, "seq", flip_z)

    lowered = (lowered[:BLK] + lowered_other.astype(F32)).astype(BF16)[:, :rank]
    up_part = lax.dot_general(
        lowered, cotangent, (((0,), (0,)), ((), ())), preferred_element_type=F32
    ).astype(BF16)
    up_part = up_part.reshape(rank, n_dp // 2, 2, own_cols).transpose(2, 1, 0, 3)
    up_part = up_part.reshape(n_dp, rank, own_cols)
    gathered, up_part = lax.optimization_barrier((gathered, up_part))
    up_part = swap(up_part, "dp")
    kept_second, sent, sum_second = project(gathered, half)
    sent, landed_first = lax.optimization_barrier((sent, landed_first))
    landed_second = lax.ppermute(sent, "seq", flip_z)

    for bit in (2, 4):
        moved = lax.ppermute(down, "seq", [(i, i ^ bit) for i in range(n_seq)])
        first = (seq_rank & bit) == 0
        down = jnp.concatenate([jnp.where(first, down, moved), jnp.where(first, moved, down)], 0)
    rows_all = attended.reshape(-1, own_rows + lanes)[:, :own_rows]
    grad_a = lax.dot_general(
        down[:, :rank], rows_all, (((0,), (0,)), ((), ())), preferred_element_type=F32
    )
    for bit in (1, 2, 4):
        grad_a = grad_a.astype(BF16)
        moved = lax.ppermute(grad_a, "dp", [(i, i ^ bit) for i in range(n_dp)])
        grad_a = grad_a.astype(F32) + moved.astype(F32)
    grad_a = grad_a.astype(BF16)

    magnitude_part = jnp.concatenate([sum_first, sum_second])
    magnitude_part = magnitude_part.astype(BF16).reshape(n_dp // 2, 2, own_cols).transpose(1, 0, 2)
    magnitude_part = jnp.broadcast_to(
        magnitude_part.reshape(n_dp, 1, own_cols), (n_dp, n_seq, own_cols)
    )
    magnitude_part, up_part = lax.optimization_barrier((magnitude_part, up_part))
    magnitude_part = swap(magnitude_part.reshape(n_all, own_cols), both)
    grad_magnitude = jnp.sum(magnitude_part.astype(F32), 0) / magnitude

    out = [kept_first + landed_first.astype(F32), kept_second + landed_second.astype(F32)]
    image_out = from_gathered(jnp.concatenate(out, 1).astype(BF16), n_dp)[None]
    moved = lax.ppermute(grad_a, "dp", [(i, i ^ 8) for i in range(n_dp)])
    grad_a = (grad_a.astype(F32) + moved.astype(F32)).T
    grad_b = jnp.sum(up_part.astype(F32), 0)
    for bit in (2, 4, 1):
        grad_b = grad_b.astype(BF16)
        moved = lax.ppermute(grad_b, "seq", [(i, i ^ bit) for i in range(n_seq)])
        grad_b = grad_b.astype(F32) + moved.astype(F32)
    grad_b = grad_b * ratio
    return (image_out, grad_a, grad_b, grad_magnitude)


def solution(mesh):
    return jax.shard_map(
        on_device,
        mesh=mesh,
        in_specs=(
            P("dp", None, None),
            P(),
            P(),
            P(),
            P(None, None, "seq"),
            P("seq", None),
            P(),
            P("seq", "dp"),
            P("dp", None),
            P("dp", None),
            P("dp", None, "seq"),
            P(),
            P("dp", "seq", None, None),
            P(),
            P("seq", "dp"),
            P("seq", None),
            P(None, "dp"),
            P("dp"),
            P("dp", "seq", None),
        ),
        out_specs=(P("dp", "seq", None), P("seq", None), P(None, "dp"), P("dp")),
        check_vma=False,
    )
```

```python
import math

import jax
import jax.numpy as jnp
from jax import lax
from jax.experimental import pallas as pl
from jax.experimental.pallas import tpu as pltpu
from jax.sharding import PartitionSpec as P

HD = 128
BLK = 128
EPSILON = 1e-06
VMEM_LIMIT = 56 * 1024 * 1024
F32 = jnp.float32
BF16 = jnp.bfloat16
Y_GROUPS = [[0, 2, 4, 6], [1, 3, 5, 7]]
QUERY_SCALE = math.log2(math.e) / math.sqrt(HD)


def rms_scale(values, gain):
    return values * lax.rsqrt(jnp.mean(values * values, -1, keepdims=True) + EPSILON) * gain


def swap(values, axes, groups=None):
    return lax.all_to_all(values, axes, 0, 0, tiled=True, axis_index_groups=groups)


def near_shard(values):
    n_dp = lax.axis_size("dp")
    return lax.ppermute(values, "dp", [(i, (i + n_dp // 2) % n_dp) for i in range(n_dp)])


def gather_columns(values, other):
    n_dp = lax.axis_size("dp")
    near = n_dp // 2
    low = lax.axis_index("dp") < near
    halves = jnp.stack([jnp.where(low, values, other), jnp.where(low, other, values)])
    groups = [list(range(near)), list(range(near, n_dp))]
    gathered = lax.all_gather(halves, "dp", axis=0, axis_index_groups=groups)
    return gathered.reshape(n_dp * values.shape[0], values.shape[1])


def to_gathered(values, n_dp):
    rows = values.shape[0]
    cut = values.reshape(rows, 2, n_dp // 2, -1)
    return cut.transpose(0, 2, 1, 3).reshape(rows, -1)


def from_gathered(values, n_dp):
    rows = values.shape[0]
    cut = values.reshape(rows, n_dp // 2, 2, -1)
    return cut.transpose(0, 2, 1, 3).reshape(rows, -1)


def dot_t(left, right):
    return lax.dot_general(left, right, (((1,), (1,)), ((), ())), preferred_element_type=F32)


def pack_kernel(_, own_in, other_in, own_ref, first_ref, second_ref):
    own_ref[0] = own_in[...].reshape(own_ref.shape[1:])
    other = other_in[...].reshape(own_ref.shape[1:])
    half = first_ref.shape[1]
    first_ref[0] = other[:half]
    second_ref[0] = other[half:]


def pack_heads(rows, pair, n_seq):
    kinds, count, model = rows.shape
    width = model // n_seq
    n_y = n_seq // 2
    block = (kinds, count, width)
    total = kinds * count

    def spec(size):
        return pl.BlockSpec((1, size, width), lambda y, z: (y, 0, 0))

    def shape(size):
        return jax.ShapeDtypeStruct((n_y, size, width), rows.dtype)

    return pl.pallas_call(
        pack_kernel,
        grid_spec=pltpu.PrefetchScalarGridSpec(
            num_scalar_prefetch=1,
            grid=(n_y,),
            in_specs=[
                pl.BlockSpec(block, lambda y, z: (0, 0, 2 * y + z[0])),
                pl.BlockSpec(block, lambda y, z: (0, 0, 2 * y + 1 - z[0])),
            ],
            out_specs=[spec(total), spec(total // 2), spec(total // 2)],
        ),
        out_shape=[shape(total), shape(total // 2), shape(total // 2)],
        compiler_params=pltpu.CompilerParams(vmem_limit_bytes=VMEM_LIMIT),
        cost_estimate=pl.CostEstimate(flops=0, bytes_accessed=4 * rows.size, transcendentals=0),
    )(pair.reshape(1), rows, rows)


def image_kernel(
    q_own, q_other, k_own, k_other, v_own, v_other, gain_ref, num_ref, den_ref, keys, values
):
    half = keys.shape[0] // 2

    @pl.when(pl.program_id(1) == 0)
    def _():
        for at, k_ref, v_ref in ((0, k_own, v_own), (half, k_other, v_other)):
            k = k_ref[...].reshape(-1, HD).astype(F32)
            keys[at : at + half, :] = rms_scale(k, gain_ref[1:2, :]).astype(BF16)
            values[at : at + half, :HD] = v_ref[...].reshape(-1, HD)
        values[:, HD:] = jnp.ones((2 * half, HD), BF16)

    q = jnp.concatenate([q_own[0], q_other[0]], 0).astype(F32)
    q = rms_scale(q, gain_ref[0:1, :] * QUERY_SCALE).astype(BF16)
    weight = jnp.exp2(dot_t(q, keys[...])).astype(BF16)
    both = jnp.dot(weight, values[...], preferred_element_type=F32)
    num_ref[...] = both[:, :HD]
    den_ref[...] = both[:, HD:]


def image_attention(own, other, gains):
    n_y, _, width = own.shape
    heads = width // HD
    rows = 2 * BLK
    image_len = n_y * rows

    def queries():
        return pl.BlockSpec((1, BLK, HD), lambda h, b: (b, 0, h))

    def whole(kind):
        return pl.BlockSpec((n_y, BLK, HD), lambda h, b: (0, kind, h))

    return pl.pallas_call(
        image_kernel,
        grid=(heads, n_y),
        in_specs=[
            queries(),
            queries(),
            whole(1),
            whole(1),
            whole(2),
            whole(2),
            pl.BlockSpec((2, HD), lambda h, b: (0, 0)),
        ],
        out_specs=[
            pl.BlockSpec((rows, HD), lambda h, b: (b, h)),
            pl.BlockSpec((rows, HD), lambda h, b: (b, h)),
        ],
        out_shape=[jax.ShapeDtypeStruct((image_len, width), F32)] * 2,
        scratch_shapes=[pltpu.VMEM((image_len, HD), BF16), pltpu.VMEM((image_len, 2 * HD), BF16)],
        compiler_params=pltpu.CompilerParams(vmem_limit_bytes=VMEM_LIMIT),
        cost_estimate=pl.CostEstimate(
            flops=6 * image_len * image_len * width,
            bytes_accessed=14 * image_len * width,
            transcendentals=heads * image_len * image_len,
        ),
    )(own, other, own, other, own, other, gains)


def prompt_kernel(
    length_ref,
    q_own,
    q_other,
    text_ref,
    k_weight,
    v_weight,
    down_ref,
    gain_ref,
    text_gain_ref,
    num_ref,
    den_ref,
    out_ref,
    lowered,
):
    head = pl.program_id(0)
    heads = pl.num_programs(0) - 1

    @pl.when(head == 0)
    def _():
        lowered[...] = jnp.zeros_like(lowered)

    @pl.when(head < heads)
    def _():
        text = text_ref[...]
        k = jnp.dot(text, k_weight[...], preferred_element_type=F32)
        k = rms_scale(k, text_gain_ref[...]).astype(BF16)
        v = jnp.dot(text, v_weight[...], preferred_element_type=F32).astype(BF16)
        stacked = jnp.concatenate([v, jnp.ones_like(v)], axis=1)
        groups, rows, _ = out_ref.shape
        for b in range(groups):
            q = jnp.concatenate([q_own[b], q_other[b]], 0).astype(F32)
            q = rms_scale(q, gain_ref[0:1, :] * QUERY_SCALE).astype(BF16)
            weight = jnp.exp2(dot_t(q, k))
            valid = lax.broadcasted_iota(jnp.int32, weight.shape, 1) < length_ref[0]
            weight = jnp.where(valid, weight, 0.0).astype(BF16)
            both = jnp.dot(weight, stacked, preferred_element_type=F32)
            at = slice(b * rows, (b + 1) * rows)
            total = num_ref[at, :] + both[:, :HD]
            attended = (total / (den_ref[at, :] + both[:, HD:])).astype(BF16)
            out_ref[b] = attended
            lowered[at, :] += jnp.dot(attended, down_ref[...], preferred_element_type=F32)

    @pl.when(head == heads)
    def _():
        out_ref[...] = lowered[...].reshape(out_ref.shape).astype(BF16)


def prompt_attention(length, own, other, text, weights, first, down, gains, text_gain, num, den):
    groups, _, width = own.shape
    heads = width // HD
    image_len = groups * 2 * BLK
    model = text.shape[1]

    def last(h):
        return jnp.minimum(h, heads - 1)

    return pl.pallas_call(
        prompt_kernel,
        grid=(heads + 1,),
        in_specs=[
            pl.BlockSpec(memory_space=pltpu.SMEM),
            pl.BlockSpec((groups, BLK, HD), lambda h: (0, 0, last(h))),
            pl.BlockSpec((groups, BLK, HD), lambda h: (0, 0, last(h))),
            pl.BlockSpec((BLK, model), lambda h: (0, 0)),
            pl.BlockSpec((model, HD), lambda h: (0, first + last(h))),
            pl.BlockSpec((model, HD), lambda h: (0, first + heads + last(h))),
            pl.BlockSpec((HD, down.shape[1]), lambda h: (last(h), 0)),
            pl.BlockSpec((2, HD), lambda h: (0, 0)),
            pl.BlockSpec((1, HD), lambda h: (0, 0)),
            pl.BlockSpec((image_len, HD), lambda h: (0, last(h))),
            pl.BlockSpec((image_len, HD), lambda h: (0, last(h))),
        ],
        out_specs=pl.BlockSpec((groups, 2 * BLK, HD), lambda h: (0, 0, h)),
        out_shape=jax.ShapeDtypeStruct((groups, 2 * BLK, width + HD), BF16),
        scratch_shapes=[pltpu.VMEM((image_len, HD), F32)],
        compiler_params=pltpu.CompilerParams(vmem_limit_bytes=VMEM_LIMIT),
        cost_estimate=pl.CostEstimate(
            flops=6 * image_len * BLK * width + 4 * BLK * model * width,
            bytes_accessed=12 * image_len * width + 4 * model * width,
            transcendentals=heads * image_len * BLK,
        ),
    )(length, own, other, text, weights, weights, down, gains, text_gain, num, den)


def t5_in_kernel(x_ref, gain_ref, gate_w, up_w, out_ref, normed):
    @pl.when(pl.program_id(0) == 0)
    def _():
        normed[...] = rms_scale(x_ref[0].astype(F32), gain_ref[...]).astype(BF16)

    gate = jnp.dot(normed[...], gate_w[0], preferred_element_type=F32)
    upward = jnp.dot(normed[...], up_w[0], preferred_element_type=F32)
    out_ref[...] = (jax.nn.gelu(gate, approximate=True) * upward).astype(BF16)


def t5_in(states, gain, in_weight):
    _, features, units = in_weight.shape
    cut = 128
    return pl.pallas_call(
        t5_in_kernel,
        grid=(units // cut,),
        in_specs=[
            pl.BlockSpec((1, BLK, features), lambda i: (0, 0, 0)),
            pl.BlockSpec((1, features), lambda i: (0, 0)),
            pl.BlockSpec((1, features, cut), lambda i: (0, 0, i)),
            pl.BlockSpec((1, features, cut), lambda i: (1, 0, i)),
        ],
        out_specs=pl.BlockSpec((BLK, cut), lambda i: (0, i)),
        out_shape=jax.ShapeDtypeStruct((BLK, units), BF16),
        scratch_shapes=[pltpu.VMEM((BLK, features), BF16)],
        compiler_params=pltpu.CompilerParams(vmem_limit_bytes=VMEM_LIMIT),
        cost_estimate=pl.CostEstimate(
            flops=4 * BLK * features * units,
            bytes_accessed=4 * features * units,
            transcendentals=BLK * units,
        ),
    )(states, gain.reshape(1, features), in_weight, in_weight)


def t5_out_kernel(hidden_ref, out_w, out_ref):
    total = jnp.dot(hidden_ref[...], out_w[...], preferred_element_type=F32)
    out_ref[0] = total.astype(BF16)


def t5_out(hidden, out_weight, n_seq):
    units, features = out_weight.shape
    feat = features // n_seq
    return pl.pallas_call(
        t5_out_kernel,
        grid=(n_seq,),
        in_specs=[
            pl.BlockSpec((BLK, units), lambda i: (0, 0)),
            pl.BlockSpec((units, feat), lambda i: (0, i)),
        ],
        out_specs=pl.BlockSpec((1, BLK, feat), lambda i: (i, 0, 0)),
        out_shape=jax.ShapeDtypeStruct((n_seq, BLK, feat), BF16),
        compiler_params=pltpu.CompilerParams(vmem_limit_bytes=VMEM_LIMIT),
        cost_estimate=pl.CostEstimate(
            flops=2 * BLK * features * units,
            bytes_accessed=2 * features * units,
            transcendentals=0,
        ),
    )(hidden, out_weight)


def on_device(
    enc_states,
    lengths,
    prompt_owner_sample,
    t5_gain,
    t5_in_weight,
    t5_out_weight,
    t5_final_gain,
    context_weight,
    text_shift,
    text_scale,
    kv_weight,
    text_key_gain,
    image_query_key_value,
    image_qk_gain,
    proj_weight,
    dora_a,
    dora_b,
    magnitude,
    grad_out,
):
    seq_rank = lax.axis_index("seq")
    data_rank = lax.axis_index("dp")
    n_seq = lax.axis_size("seq")
    n_dp = lax.axis_size("dp")
    n_all = n_seq * n_dp
    both = ("dp", "seq")
    rank, own_cols = dora_b.shape
    own_rows = dora_a.shape[0]
    model = own_cols * n_dp
    lanes = 128
    rows_of = model // lanes
    cotangent = to_gathered(grad_out[0], n_dp)

    pair = seq_rank % 2
    flip_z = [(i, i ^ 1) for i in range(n_seq)]
    n_y = n_seq // 2

    weights = jnp.concatenate(
        [context_weight.T, kv_weight.reshape(kv_weight.shape[0], -1)], 1
    )
    near_weights = near_shard(weights)
    own_heads, first_heads, second_heads = pack_heads(
        image_query_key_value[0].transpose(1, 0, 2), pair, n_seq
    )
    t5_gain, first_heads = lax.optimization_barrier((t5_gain, first_heads))
    first_heads = lax.ppermute(first_heads, "seq", flip_z)
    direction_t = proj_weight.T.astype(F32) + lax.dot_general(
        dora_b, dora_a, (((0,), (1,)), ((), ())), precision=lax.Precision.HIGHEST
    )
    direction_t = direction_t.astype(BF16)
    shifted = [direction_t]
    for step in range(1, n_y):
        ahead = [(i, (i + 2 * step) % n_seq) for i in range(n_seq)]
        shifted.insert(0, lax.ppermute(direction_t, "seq", ahead))
    own_heads = swap(own_heads, "seq", Y_GROUPS)

    tokens = enc_states[0, :BLK]
    feat = tokens.shape[1] // n_seq
    hidden = t5_in(enc_states, t5_gain, t5_in_weight)
    hidden, near_weights, shifted, first_heads, second_heads = lax.optimization_barrier(
        (hidden, near_weights, shifted, first_heads, second_heads)
    )
    second_heads = lax.ppermute(second_heads, "seq", flip_z)
    weights = gather_columns(weights, near_weights)
    depth = context_weight.shape[0]
    context_all = weights[:, :depth]
    column_sq = jnp.sum(jnp.square(jnp.stack(shifted).astype(F32)), (0, 2))
    column_other = lax.ppermute(column_sq, "seq", flip_z)
    ffn = t5_out(hidden, t5_out_weight, n_seq)
    own_heads, ffn, second_heads, column_other = lax.optimization_barrier(
        (own_heads, ffn, second_heads, column_other)
    )

    ratio = magnitude / jnp.sqrt(column_sq + column_other + EPSILON)
    scaled_t = []
    for row in range(n_y):
        turned = [shifted[(row - at - 1) % n_y] for at in range(n_y)]
        block = lax.select_n(seq_rank // 2, *turned)
        scaled_t.append((block.astype(F32) * ratio[:, None]).astype(BF16))
    scaled_t = jnp.concatenate(scaled_t, 1)
    reach = scaled_t.shape[1]
    up = jnp.pad((dora_b * ratio).astype(BF16).T, ((0, 0), (0, lanes - rank)))
    scaled_t = jnp.concatenate([scaled_t, up], 1)
    near_scaled = near_shard(scaled_t)

    ffn = swap(ffn, "seq")
    ffn, second_heads = lax.optimization_barrier((ffn, second_heads))
    ffn_sum = jnp.sum(ffn.astype(F32), 0)

    other_heads = swap(jnp.concatenate([first_heads, second_heads], 1), "seq", Y_GROUPS)

    own_tokens = lax.dynamic_slice_in_dim(tokens, seq_rank * feat, feat, 1).astype(F32)
    own_final = lax.dynamic_slice_in_dim(t5_final_gain, seq_rank * feat, feat, 0)
    encoded = ((own_tokens + ffn_sum) * own_final).astype(BF16)
    context = dot_t(encoded, context_all).astype(BF16).reshape(BLK, rows_of, lanes)
    context, other_heads, near_scaled = lax.optimization_barrier(
        (context, other_heads, near_scaled)
    )
    scaled_all = gather_columns(scaled_t, near_scaled)
    up_all = scaled_all[:, reach:]
    arrived = swap(context, both)
    token_of = jnp.sum(arrived.reshape(n_dp, n_seq, rows_of, lanes).astype(F32), 1).astype(BF16)
    values = token_of.astype(F32)
    centre = jnp.mean(values, (1, 2), keepdims=True)
    spread = jnp.mean((values - centre) * (values - centre), (1, 2), keepdims=True)
    layer_normed = ((values - centre) * lax.rsqrt(spread + EPSILON)).astype(BF16)
    target = jnp.arange(n_all, dtype=jnp.int32) // n_seq
    one_hot = (target[:, None] == prompt_owner_sample[None, :]).astype(BF16)
    outgoing = jnp.einsum("sp,pab->sab", one_hot, layer_normed, preferred_element_type=F32)
    num, den = image_attention(own_heads, other_heads, image_qk_gain)
    outgoing, num, den = lax.optimization_barrier((outgoing.astype(BF16), num, den))
    text = swap(outgoing, both).reshape(BLK, model)
    scale, shift = to_gathered(text_scale, n_dp), to_gathered(text_shift, n_dp)
    modulated = ((1.0 + scale) * text.astype(F32) + shift).astype(BF16)
    length = jnp.sum(jnp.where(prompt_owner_sample == data_rank, lengths, 0))

    down_factor = jnp.pad(dora_a.astype(BF16), ((0, 0), (0, lanes - rank)))
    attended = prompt_attention(
        length.reshape(1),
        own_heads,
        other_heads,
        modulated,
        weights,
        depth // HD,
        down_factor,
        image_qk_gain,
        text_key_gain.reshape(1, HD),
        num,
        den,
    )

    gathered = swap(attended, "seq", Y_GROUPS)
    down = jnp.dot(cotangent, up_all, preferred_element_type=F32).astype(BF16)
    down = jnp.concatenate([down, lax.ppermute(down, "seq", flip_z)], 0)
    cotangent_other = lax.ppermute(cotangent, "seq", flip_z)
    gathered, down, cotangent_other = lax.optimization_barrier((gathered, down, cotangent_other))
    lowered = jnp.sum(gathered[:, :, own_rows:].astype(F32), 0)
    lowered_other = lax.ppermute(lowered[BLK:].astype(BF16), "seq", flip_z)
    gathered = gathered[:, :, :own_rows].transpose(1, 0, 2).reshape(2 * BLK, -1)
    half = model // 2

    def project(rows, at):
        product = dot_t(rows, scaled_all[at : at + half, :reach])
        sums = jnp.sum(product[:BLK] * cotangent[:, at : at + half].astype(F32), 0)
        sums = sums + jnp.sum(product[BLK:] * cotangent_other[:, at : at + half].astype(F32), 0)
        return product[:BLK], product[BLK:].astype(BF16), sums

    kept_first, sent, sum_first = project(gathered, 0)
    gathered, sent, down = lax.optimization_barrier((gathered, sent, down))
    landed_first = lax.ppermute(sent, "seq", flip_z)

    lowered = (lowered[:BLK] + lowered_other.astype(F32)).astype(BF16)[:, :rank]
    up_part = lax.dot_general(
        lowered, cotangent, (((0,), (0,)), ((), ())), preferred_element_type=F32
    ).astype(BF16)
    up_part = up_part.reshape(rank, n_dp // 2, 2, own_cols).transpose(2, 1, 0, 3)
    up_part = up_part.reshape(n_dp, rank, own_cols)
    gathered, up_part = lax.optimization_barrier((gathered, up_part))
    up_part = swap(up_part, "dp")
    kept_second, sent, sum_second = project(gathered, half)
    sent, landed_first = lax.optimization_barrier((sent, landed_first))
    landed_second = lax.ppermute(sent, "seq", flip_z)

    for bit in (2, 4):
        moved = lax.ppermute(down, "seq", [(i, i ^ bit) for i in range(n_seq)])
        first = (seq_rank & bit) == 0
        down = jnp.concatenate([jnp.where(first, down, moved), jnp.where(first, moved, down)], 0)
    rows_all = attended.reshape(-1, own_rows + lanes)[:, :own_rows]
    grad_a = lax.dot_general(
        down[:, :rank], rows_all, (((0,), (0,)), ((), ())), preferred_element_type=F32
    )
    for bit in (1, 2, 4):
        grad_a = grad_a.astype(BF16)
        moved = lax.ppermute(grad_a, "dp", [(i, i ^ bit) for i in range(n_dp)])
        grad_a = grad_a.astype(F32) + moved.astype(F32)
    grad_a = grad_a.astype(BF16)

    magnitude_part = jnp.concatenate([sum_first, sum_second])
    magnitude_part = magnitude_part.astype(BF16).reshape(n_dp // 2, 2, own_cols).transpose(1, 0, 2)
    magnitude_part = jnp.broadcast_to(
        magnitude_part.reshape(n_dp, 1, own_cols), (n_dp, n_seq, own_cols)
    )
    magnitude_part, up_part = lax.optimization_barrier((magnitude_part, up_part))
    magnitude_part = swap(magnitude_part.reshape(n_all, own_cols), both)
    grad_magnitude = jnp.sum(magnitude_part.astype(F32), 0) / magnitude

    out = [kept_first + landed_first.astype(F32), kept_second + landed_second.astype(F32)]
    image_out = from_gathered(jnp.concatenate(out, 1).astype(BF16), n_dp)[None]
    moved = lax.ppermute(grad_a, "dp", [(i, i ^ 8) for i in range(n_dp)])
    grad_a = (grad_a.astype(F32) + moved.astype(F32)).T
    grad_b = jnp.sum(up_part.astype(F32), 0)
    for bit in (2, 4, 1):
        grad_b = grad_b.astype(BF16)
        moved = lax.ppermute(grad_b, "seq", [(i, i ^ bit) for i in range(n_seq)])
        grad_b = grad_b.astype(F32) + moved.astype(F32)
    grad_b = grad_b * ratio
    return (image_out, grad_a, grad_b, grad_magnitude)


def solution(mesh):
    return jax.shard_map(
        on_device,
        mesh=mesh,
        in_specs=(
            P("dp", None, None),
            P(),
            P(),
            P(),
            P(None, None, "seq"),
            P("seq", None),
            P(),
            P("seq", "dp"),
            P("dp", None),
            P("dp", None),
            P("dp", None, "seq"),
            P(),
            P("dp", "seq", None, None),
            P(),
            P("seq", "dp"),
            P("seq", None),
            P(None, "dp"),
            P("dp"),
            P("dp", "seq", None),
        ),
        out_specs=(P("dp", "seq", None), P("seq", None), P(None, "dp"), P("dp")),
        check_vma=False,
    )
```

```python
import math

import jax
import jax.numpy as jnp
from jax import lax
from jax.experimental import pallas as pl
from jax.experimental.pallas import tpu as pltpu
from jax.sharding import PartitionSpec as P

HD = 128
BLK = 128
EPSILON = 1e-06
VMEM_LIMIT = 56 * 1024 * 1024
F32 = jnp.float32
BF16 = jnp.bfloat16
Y_GROUPS = [[0, 2, 4, 6], [1, 3, 5, 7]]
QUERY_SCALE = math.log2(math.e) / math.sqrt(HD)


def rms_scale(values, gain):
    return values * lax.rsqrt(jnp.mean(values * values, -1, keepdims=True) + EPSILON) * gain


def swap(values, axes, groups=None):
    return lax.all_to_all(values, axes, 0, 0, tiled=True, axis_index_groups=groups)


def near_shard(values):
    n_dp = lax.axis_size("dp")
    return lax.ppermute(values, "dp", [(i, (i + n_dp // 2) % n_dp) for i in range(n_dp)])


def gather_columns(values, other):
    n_dp = lax.axis_size("dp")
    near = n_dp // 2
    low = lax.axis_index("dp") < near
    halves = jnp.stack([jnp.where(low, values, other), jnp.where(low, other, values)])
    groups = [list(range(near)), list(range(near, n_dp))]
    gathered = lax.all_gather(halves, "dp", axis=0, axis_index_groups=groups)
    return gathered.reshape(n_dp * values.shape[0], values.shape[1])


def to_gathered(values, n_dp):
    rows = values.shape[0]
    cut = values.reshape(rows, 2, n_dp // 2, -1)
    return cut.transpose(0, 2, 1, 3).reshape(rows, -1)


def from_gathered(values, n_dp):
    rows = values.shape[0]
    cut = values.reshape(rows, n_dp // 2, 2, -1)
    return cut.transpose(0, 2, 1, 3).reshape(rows, -1)


def dot_t(left, right):
    return lax.dot_general(left, right, (((1,), (1,)), ((), ())), preferred_element_type=F32)


def pack_kernel(_, own_in, other_in, own_ref, first_ref, second_ref):
    own_ref[0] = own_in[...].reshape(own_ref.shape[1:])
    other = other_in[...].reshape(own_ref.shape[1:])
    half = first_ref.shape[1]
    first_ref[0] = other[:half]
    second_ref[0] = other[half:]


def pack_heads(rows, pair, n_seq):
    kinds, count, model = rows.shape
    width = model // n_seq
    n_y = n_seq // 2
    block = (kinds, count, width)
    total = kinds * count

    def spec(size):
        return pl.BlockSpec((1, size, width), lambda y, z: (y, 0, 0))

    def shape(size):
        return jax.ShapeDtypeStruct((n_y, size, width), rows.dtype)

    return pl.pallas_call(
        pack_kernel,
        grid_spec=pltpu.PrefetchScalarGridSpec(
            num_scalar_prefetch=1,
            grid=(n_y,),
            in_specs=[
                pl.BlockSpec(block, lambda y, z: (0, 0, 2 * y + z[0])),
                pl.BlockSpec(block, lambda y, z: (0, 0, 2 * y + 1 - z[0])),
            ],
            out_specs=[spec(total), spec(total // 2), spec(total // 2)],
        ),
        out_shape=[shape(total), shape(total // 2), shape(total // 2)],
        compiler_params=pltpu.CompilerParams(vmem_limit_bytes=VMEM_LIMIT),
        cost_estimate=pl.CostEstimate(flops=0, bytes_accessed=4 * rows.size, transcendentals=0),
    )(pair.reshape(1), rows, rows)


def image_kernel(
    q_own, q_other, k_own, k_other, v_own, v_other, gain_ref, num_ref, den_ref, keys, values
):
    half = keys.shape[0] // 2

    @pl.when(pl.program_id(1) == 0)
    def _():
        for at, k_ref, v_ref in ((0, k_own, v_own), (half, k_other, v_other)):
            k = k_ref[...].reshape(-1, HD).astype(F32)
            keys[at : at + half, :] = rms_scale(k, gain_ref[1:2, :]).astype(BF16)
            values[at : at + half, :HD] = v_ref[...].reshape(-1, HD)
        values[:, HD:] = jnp.ones((2 * half, HD), BF16)

    q = jnp.concatenate([q_own[0], q_other[0]], 0).astype(F32)
    q = rms_scale(q, gain_ref[0:1, :] * QUERY_SCALE).astype(BF16)
    weight = jnp.exp2(dot_t(q, keys[...])).astype(BF16)
    both = jnp.dot(weight, values[...], preferred_element_type=F32)
    num_ref[...] = both[:, :HD]
    den_ref[...] = both[:, HD:]


def image_attention(own, other, gains):
    n_y, _, width = own.shape
    heads = width // HD
    rows = 2 * BLK
    image_len = n_y * rows

    def queries():
        return pl.BlockSpec((1, BLK, HD), lambda h, b: (b, 0, h))

    def whole(kind):
        return pl.BlockSpec((n_y, BLK, HD), lambda h, b: (0, kind, h))

    return pl.pallas_call(
        image_kernel,
        grid=(heads, n_y),
        in_specs=[
            queries(),
            queries(),
            whole(1),
            whole(1),
            whole(2),
            whole(2),
            pl.BlockSpec((2, HD), lambda h, b: (0, 0)),
        ],
        out_specs=[
            pl.BlockSpec((rows, HD), lambda h, b: (b, h)),
            pl.BlockSpec((rows, HD), lambda h, b: (b, h)),
        ],
        out_shape=[jax.ShapeDtypeStruct((image_len, width), F32)] * 2,
        scratch_shapes=[pltpu.VMEM((image_len, HD), BF16), pltpu.VMEM((image_len, 2 * HD), BF16)],
        compiler_params=pltpu.CompilerParams(vmem_limit_bytes=VMEM_LIMIT),
        cost_estimate=pl.CostEstimate(
            flops=6 * image_len * image_len * width,
            bytes_accessed=14 * image_len * width,
            transcendentals=heads * image_len * image_len,
        ),
    )(own, other, own, other, own, other, gains)


def prompt_kernel(
    length_ref,
    q_own,
    q_other,
    text_ref,
    k_weight,
    v_weight,
    down_ref,
    gain_ref,
    text_gain_ref,
    num_ref,
    den_ref,
    out_ref,
    lowered,
):
    head = pl.program_id(0)
    heads = pl.num_programs(0) - 1

    @pl.when(head == 0)
    def _():
        lowered[...] = jnp.zeros_like(lowered)

    @pl.when(head < heads)
    def _():
        text = text_ref[...]
        k = jnp.dot(text, k_weight[...], preferred_element_type=F32)
        k = rms_scale(k, text_gain_ref[...]).astype(BF16)
        v = jnp.dot(text, v_weight[...], preferred_element_type=F32).astype(BF16)
        stacked = jnp.concatenate([v, jnp.ones_like(v)], axis=1)
        groups, rows, _ = out_ref.shape
        for b in range(groups):
            q = jnp.concatenate([q_own[b], q_other[b]], 0).astype(F32)
            q = rms_scale(q, gain_ref[0:1, :] * QUERY_SCALE).astype(BF16)
            weight = jnp.exp2(dot_t(q, k))
            valid = lax.broadcasted_iota(jnp.int32, weight.shape, 1) < length_ref[0]
            weight = jnp.where(valid, weight, 0.0).astype(BF16)
            both = jnp.dot(weight, stacked, preferred_element_type=F32)
            at = slice(b * rows, (b + 1) * rows)
            total = num_ref[at, :] + both[:, :HD]
            attended = (total / (den_ref[at, :] + both[:, HD:])).astype(BF16)
            out_ref[b] = attended
            lowered[at, :] += jnp.dot(attended, down_ref[...], preferred_element_type=F32)

    @pl.when(head == heads)
    def _():
        out_ref[...] = lowered[...].reshape(out_ref.shape).astype(BF16)


def prompt_attention(length, own, other, text, weights, first, down, gains, text_gain, num, den):
    groups, _, width = own.shape
    heads = width // HD
    image_len = groups * 2 * BLK
    model = text.shape[1]

    def last(h):
        return jnp.minimum(h, heads - 1)

    return pl.pallas_call(
        prompt_kernel,
        grid=(heads + 1,),
        in_specs=[
            pl.BlockSpec(memory_space=pltpu.SMEM),
            pl.BlockSpec((groups, BLK, HD), lambda h: (0, 0, last(h))),
            pl.BlockSpec((groups, BLK, HD), lambda h: (0, 0, last(h))),
            pl.BlockSpec((BLK, model), lambda h: (0, 0)),
            pl.BlockSpec((model, HD), lambda h: (0, first + last(h))),
            pl.BlockSpec((model, HD), lambda h: (0, first + heads + last(h))),
            pl.BlockSpec((HD, down.shape[1]), lambda h: (last(h), 0)),
            pl.BlockSpec((2, HD), lambda h: (0, 0)),
            pl.BlockSpec((1, HD), lambda h: (0, 0)),
            pl.BlockSpec((image_len, HD), lambda h: (0, last(h))),
            pl.BlockSpec((image_len, HD), lambda h: (0, last(h))),
        ],
        out_specs=pl.BlockSpec((groups, 2 * BLK, HD), lambda h: (0, 0, h)),
        out_shape=jax.ShapeDtypeStruct((groups, 2 * BLK, width + HD), BF16),
        scratch_shapes=[pltpu.VMEM((image_len, HD), F32)],
        compiler_params=pltpu.CompilerParams(vmem_limit_bytes=VMEM_LIMIT),
        cost_estimate=pl.CostEstimate(
            flops=6 * image_len * BLK * width + 4 * BLK * model * width,
            bytes_accessed=12 * image_len * width + 4 * model * width,
            transcendentals=heads * image_len * BLK,
        ),
    )(length, own, other, text, weights, weights, down, gains, text_gain, num, den)


def t5_in_kernel(x_ref, gain_ref, gate_w, up_w, out_ref, normed):
    @pl.when(pl.program_id(0) == 0)
    def _():
        normed[...] = rms_scale(x_ref[0].astype(F32), gain_ref[...]).astype(BF16)

    gate = jnp.dot(normed[...], gate_w[0], preferred_element_type=F32)
    upward = jnp.dot(normed[...], up_w[0], preferred_element_type=F32)
    out_ref[...] = (jax.nn.gelu(gate, approximate=True) * upward).astype(BF16)


def t5_in(states, gain, in_weight):
    _, features, units = in_weight.shape
    cut = 128
    return pl.pallas_call(
        t5_in_kernel,
        grid=(units // cut,),
        in_specs=[
            pl.BlockSpec((1, BLK, features), lambda i: (0, 0, 0)),
            pl.BlockSpec((1, features), lambda i: (0, 0)),
            pl.BlockSpec((1, features, cut), lambda i: (0, 0, i)),
            pl.BlockSpec((1, features, cut), lambda i: (1, 0, i)),
        ],
        out_specs=pl.BlockSpec((BLK, cut), lambda i: (0, i)),
        out_shape=jax.ShapeDtypeStruct((BLK, units), BF16),
        scratch_shapes=[pltpu.VMEM((BLK, features), BF16)],
        compiler_params=pltpu.CompilerParams(vmem_limit_bytes=VMEM_LIMIT),
        cost_estimate=pl.CostEstimate(
            flops=4 * BLK * features * units,
            bytes_accessed=4 * features * units,
            transcendentals=BLK * units,
        ),
    )(states, gain.reshape(1, features), in_weight, in_weight)


def t5_out_kernel(hidden_ref, out_w, out_ref):
    total = jnp.dot(hidden_ref[...], out_w[...], preferred_element_type=F32)
    out_ref[0] = total.astype(BF16)


def t5_out(hidden, out_weight, n_seq):
    units, features = out_weight.shape
    feat = features // n_seq
    return pl.pallas_call(
        t5_out_kernel,
        grid=(n_seq,),
        in_specs=[
            pl.BlockSpec((BLK, units), lambda i: (0, 0)),
            pl.BlockSpec((units, feat), lambda i: (0, i)),
        ],
        out_specs=pl.BlockSpec((1, BLK, feat), lambda i: (i, 0, 0)),
        out_shape=jax.ShapeDtypeStruct((n_seq, BLK, feat), BF16),
        compiler_params=pltpu.CompilerParams(vmem_limit_bytes=VMEM_LIMIT),
        cost_estimate=pl.CostEstimate(
            flops=2 * BLK * features * units,
            bytes_accessed=2 * features * units,
            transcendentals=0,
        ),
    )(hidden, out_weight)


def on_device(
    enc_states,
    lengths,
    prompt_owner_sample,
    t5_gain,
    t5_in_weight,
    t5_out_weight,
    t5_final_gain,
    context_weight,
    text_shift,
    text_scale,
    kv_weight,
    text_key_gain,
    image_query_key_value,
    image_qk_gain,
    proj_weight,
    dora_a,
    dora_b,
    magnitude,
    grad_out,
):
    seq_rank = lax.axis_index("seq")
    data_rank = lax.axis_index("dp")
    n_seq = lax.axis_size("seq")
    n_dp = lax.axis_size("dp")
    n_all = n_seq * n_dp
    both = ("dp", "seq")
    rank, own_cols = dora_b.shape
    own_rows = dora_a.shape[0]
    model = own_cols * n_dp
    lanes = 128
    rows_of = model // lanes
    cotangent = to_gathered(grad_out[0], n_dp)

    pair = seq_rank % 2
    flip_z = [(i, i ^ 1) for i in range(n_seq)]
    n_y = n_seq // 2

    weights = jnp.concatenate(
        [context_weight.T, kv_weight.reshape(kv_weight.shape[0], -1)], 1
    )
    near_weights = near_shard(weights)
    own_heads, first_heads, second_heads = pack_heads(
        image_query_key_value[0].transpose(1, 0, 2), pair, n_seq
    )
    t5_gain, first_heads = lax.optimization_barrier((t5_gain, first_heads))
    first_heads = lax.ppermute(first_heads, "seq", flip_z)
    direction_t = proj_weight.T.astype(F32) + lax.dot_general(
        dora_b, dora_a, (((0,), (1,)), ((), ())), precision=lax.Precision.HIGHEST
    )
    direction_t = direction_t.astype(BF16)
    shifted = [direction_t]
    for step in range(1, n_y):
        ahead = [(i, (i + 2 * step) % n_seq) for i in range(n_seq)]
        shifted.insert(0, lax.ppermute(direction_t, "seq", ahead))
    own_heads = swap(own_heads, "seq", Y_GROUPS)

    tokens = enc_states[0, :BLK]
    feat = tokens.shape[1] // n_seq
    hidden = t5_in(enc_states, t5_gain, t5_in_weight)
    hidden, near_weights, shifted, first_heads, second_heads = lax.optimization_barrier(
        (hidden, near_weights, shifted, first_heads, second_heads)
    )
    second_heads = lax.ppermute(second_heads, "seq", flip_z)
    weights = gather_columns(weights, near_weights)
    depth = context_weight.shape[0]
    context_all = weights[:, :depth]
    column_sq = jnp.sum(jnp.square(jnp.stack(shifted).astype(F32)), (0, 2))
    column_other = lax.ppermute(column_sq, "seq", flip_z)
    ffn = t5_out(hidden, t5_out_weight, n_seq)
    own_heads, ffn, second_heads, column_other = lax.optimization_barrier(
        (own_heads, ffn, second_heads, column_other)
    )

    ratio = magnitude / jnp.sqrt(column_sq + column_other + EPSILON)
    scaled_t = []
    for row in range(n_y):
        turned = [shifted[(row - at - 1) % n_y] for at in range(n_y)]
        block = lax.select_n(seq_rank // 2, *turned)
        scaled_t.append((block.astype(F32) * ratio[:, None]).astype(BF16))
    scaled_t = jnp.concatenate(scaled_t, 1)
    reach = scaled_t.shape[1]
    up = jnp.pad((dora_b * ratio).astype(BF16).T, ((0, 0), (0, lanes - rank)))
    scaled_t = jnp.concatenate([scaled_t, up], 1)
    near_scaled = near_shard(scaled_t)

    ffn = swap(ffn, "seq")
    ffn, second_heads = lax.optimization_barrier((ffn, second_heads))
    ffn_sum = jnp.sum(ffn.astype(F32), 0)

    other_heads = swap(jnp.concatenate([first_heads, second_heads], 1), "seq", Y_GROUPS)

    own_tokens = lax.dynamic_slice_in_dim(tokens, seq_rank * feat, feat, 1).astype(F32)
    own_final = lax.dynamic_slice_in_dim(t5_final_gain, seq_rank * feat, feat, 0)
    encoded = ((own_tokens + ffn_sum) * own_final).astype(BF16)
    context = dot_t(encoded, context_all).astype(BF16).reshape(BLK, rows_of, lanes)
    context, other_heads, near_scaled = lax.optimization_barrier(
        (context, other_heads, near_scaled)
    )
    scaled_all = gather_columns(scaled_t, near_scaled)
    up_all = scaled_all[:, reach:]
    arrived = swap(context, both)
    token_of = jnp.sum(arrived.reshape(n_dp, n_seq, rows_of, lanes).astype(F32), 1).astype(BF16)
    values = token_of.astype(F32)
    centre = jnp.mean(values, (1, 2), keepdims=True)
    spread = jnp.mean((values - centre) * (values - centre), (1, 2), keepdims=True)
    layer_normed = ((values - centre) * lax.rsqrt(spread + EPSILON)).astype(BF16)
    target = jnp.arange(n_all, dtype=jnp.int32) // n_seq
    one_hot = (target[:, None] == prompt_owner_sample[None, :]).astype(BF16)
    outgoing = jnp.einsum("sp,pab->sab", one_hot, layer_normed, preferred_element_type=F32)
    num, den = image_attention(own_heads, other_heads, image_qk_gain)
    outgoing, num, den = lax.optimization_barrier((outgoing.astype(BF16), num, den))
    text = swap(outgoing, both).reshape(BLK, model)
    scale, shift = to_gathered(text_scale, n_dp), to_gathered(text_shift, n_dp)
    modulated = ((1.0 + scale) * text.astype(F32) + shift).astype(BF16)
    length = jnp.sum(jnp.where(prompt_owner_sample == data_rank, lengths, 0))

    down_factor = jnp.pad(dora_a.astype(BF16), ((0, 0), (0, lanes - rank)))
    attended = prompt_attention(
        length.reshape(1),
        own_heads,
        other_heads,
        modulated,
        weights,
        depth // HD,
        down_factor,
        image_qk_gain,
        text_key_gain.reshape(1, HD),
        num,
        den,
    )

    gathered = swap(attended, "seq", Y_GROUPS)
    down = jnp.dot(cotangent, up_all, preferred_element_type=F32).astype(BF16)
    down = jnp.concatenate([down, lax.ppermute(down, "seq", flip_z)], 0)
    cotangent_other = lax.ppermute(cotangent, "seq", flip_z)
    gathered, down, cotangent_other = lax.optimization_barrier((gathered, down, cotangent_other))
    lowered = jnp.sum(gathered[:, :, own_rows:].astype(F32), 0)
    lowered_other = lax.ppermute(lowered[BLK:].astype(BF16), "seq", flip_z)
    gathered = gathered[:, :, :own_rows].transpose(1, 0, 2).reshape(2 * BLK, -1)
    half = model // 2

    def project(rows, at):
        product = dot_t(rows, scaled_all[at : at + half, :reach])
        sums = jnp.sum(product[:BLK] * cotangent[:, at : at + half].astype(F32), 0)
        sums = sums + jnp.sum(product[BLK:] * cotangent_other[:, at : at + half].astype(F32), 0)
        return product[:BLK], product[BLK:].astype(BF16), sums

    kept_first, sent, sum_first = project(gathered, 0)
    gathered, sent = lax.optimization_barrier((gathered, sent))
    landed_first = lax.ppermute(sent, "seq", flip_z)

    lowered = (lowered[:BLK] + lowered_other.astype(F32)).astype(BF16)[:, :rank]
    up_part = lax.dot_general(
        lowered, cotangent, (((0,), (0,)), ((), ())), preferred_element_type=F32
    ).astype(BF16)
    up_part = up_part.reshape(rank, n_dp // 2, 2, own_cols).transpose(2, 1, 0, 3)
    up_part = up_part.reshape(n_dp, rank, own_cols)
    gathered, up_part = lax.optimization_barrier((gathered, up_part))
    up_part = swap(up_part, "dp")
    kept_second, sent, sum_second = project(gathered, half)
    sent, landed_first = lax.optimization_barrier((sent, landed_first))
    landed_second = lax.ppermute(sent, "seq", flip_z)

    for bit in (2, 4):
        moved = lax.ppermute(down, "seq", [(i, i ^ bit) for i in range(n_seq)])
        first = (seq_rank & bit) == 0
        down = jnp.concatenate([jnp.where(first, down, moved), jnp.where(first, moved, down)], 0)
    rows_all = attended.reshape(-1, own_rows + lanes)[:, :own_rows]
    grad_a = lax.dot_general(
        down[:, :rank], rows_all, (((0,), (0,)), ((), ())), preferred_element_type=F32
    )
    for bit in (1, 2, 4):
        grad_a = grad_a.astype(BF16)
        moved = lax.ppermute(grad_a, "dp", [(i, i ^ bit) for i in range(n_dp)])
        grad_a = grad_a.astype(F32) + moved.astype(F32)
    grad_a = grad_a.astype(BF16)

    magnitude_part = jnp.concatenate([sum_first, sum_second])
    magnitude_part = magnitude_part.astype(BF16).reshape(n_dp // 2, 2, own_cols).transpose(1, 0, 2)
    magnitude_part = jnp.broadcast_to(
        magnitude_part.reshape(n_dp, 1, own_cols), (n_dp, n_seq, own_cols)
    )
    magnitude_part, up_part = lax.optimization_barrier((magnitude_part, up_part))
    magnitude_part = swap(magnitude_part.reshape(n_all, own_cols), both)
    grad_magnitude = jnp.sum(magnitude_part.astype(F32), 0) / magnitude

    out = [kept_first + landed_first.astype(F32), kept_second + landed_second.astype(F32)]
    image_out = from_gathered(jnp.concatenate(out, 1).astype(BF16), n_dp)[None]
    moved = lax.ppermute(grad_a, "dp", [(i, i ^ 8) for i in range(n_dp)])
    grad_a = (grad_a.astype(F32) + moved.astype(F32)).T
    grad_b = jnp.sum(up_part.astype(F32), 0)
    for bit in (2, 4, 1):
        grad_b = grad_b.astype(BF16)
        moved = lax.ppermute(grad_b, "seq", [(i, i ^ bit) for i in range(n_seq)])
        grad_b = grad_b.astype(F32) + moved.astype(F32)
    grad_b = grad_b * ratio
    return (image_out, grad_a, grad_b, grad_magnitude)


def solution(mesh):
    return jax.shard_map(
        on_device,
        mesh=mesh,
        in_specs=(
            P("dp", None, None),
            P(),
            P(),
            P(),
            P(None, None, "seq"),
            P("seq", None),
            P(),
            P("seq", "dp"),
            P("dp", None),
            P("dp", None),
            P("dp", None, "seq"),
            P(),
            P("dp", "seq", None, None),
            P(),
            P("seq", "dp"),
            P("seq", None),
            P(None, "dp"),
            P("dp"),
            P("dp", "seq", None),
        ),
        out_specs=(P("dp", "seq", None), P("seq", None), P(None, "dp"), P("dp")),
        check_vma=False,
    )
```
